32 devices in a mesh: fsdp: 8 (over y, x, core), seq: 4 (over z).
Axes of the slice: x: 2, y: 2, z: 4, core: 2. Of those that a mesh axis runs over, the one named last changes fastest.
Arguments:
- streams: bfloat16 [3, 2048, 4096], P(None, 'seq', 'fsdp'), may hold values from -6 to 6
- record_blocks: int32 [3], replicated, may hold values from 1 to 8, as said below
- tail_rows: int32 [3], replicated, may hold values from 1 to 128
- unit_dest: int32 [128], replicated, may hold values from 0 to 127, as said below
- mixer_filter: float32 [128, 4096], P(None, ('fsdp', 'seq')), may hold values from -0.5 to 0.5
- feat_filter: float32 [7, 3, 4096], P(None, None, ('fsdp', 'seq')), may hold values from -2 to 2
- norm_gain: float32 [4096], P(('fsdp', 'seq')), may hold values from 0.25 to 1.75
- out_grad: bfloat16 [2048, 4096], P('seq', 'fsdp'), may hold values from -6 to 6
Outputs:
- out: bfloat16 [2048, 4096], P('seq', 'fsdp')
- stream_grad: bfloat16 [3, 2048, 4096], P(None, 'seq', 'fsdp')
- mixer_grad: float32 [128, 4096], P(None, ('fsdp', 'seq'))
- feat_grad: float32 [7, 3, 4096], P(None, None, ('fsdp', 'seq'))
- gain_grad: float32 [4096], P(('fsdp', 'seq'))
The draws below stay inside these ranges and needn't reach their ends.
Inputs may be any that keep to these rules, and one draw needn't show every extreme that they name: unit_dest is a permutation; the 32 units of each shard of 512 rows go to exactly half of the shards, 16 units to each of them, so each shard receives 16 units from each of half of the shards. record_blocks sums to 16; the second record is the longest, exactly 8 blocks.
All inputs are finite; a program needn't handle non-finite values.
Results may differ from the reference program's by a relative error of at most 0.0085.
Values may be sent and summed in bfloat16 or wider, within the bound.
No kernel may reach another device: no remote copies, remote signals or barrier semaphores. Data moves between devices by JAX's collectives and lax.ppermute only.
A program may use at most 128 MiB of HBM per device.

```python
import jax
import jax.numpy as jnp
import numpy as np
from jax import lax

C = 4096
KM = 128
KF = 7
UNIT = 16
RECORDS = 3
T_DEV = 512
TOKENS = 2048
NU = 32
UNITS = 128
CAP = 16
NBLK = 16
MOSTB = 8


def draw_unit_dest(key, part):
    shards = TOKENS // T_DEV
    subkeys = jax.random.split(key, 5)
    source_order = jax.random.permutation(subkeys[0], shards)
    target_order = jax.random.permutation(subkeys[1], shards)
    offsets = jax.random.permutation(subkeys[2], shards)[:shards // 2]
    within = jax.vmap(lambda one_key: jax.random.permutation(one_key, NU))(jax.random.split(subkeys[3], shards))
    offset_index = within // CAP
    rank_in = within % CAP
    target = target_order[(source_order[:, None] + offsets[offset_index]) % shards]
    arrival = jax.vmap(lambda one_key: jax.random.permutation(one_key, NU))(jax.random.split(subkeys[4], shards))
    local_slot = arrival[target, offset_index * CAP + rank_in]
    return (target * NU + local_slot).reshape(-1).astype(jnp.int32)


def draw_record_blocks(key, part):
    own_key = jax.random.fold_in(key, 7321)
    shard_blocks = T_DEV // KM
    first_len = jax.random.randint(own_key, (1,), shard_blocks + 1, NBLK // 2).astype(jnp.int32)
    long_len = jnp.full((1,), MOSTB, jnp.int32)
    last_len = (NBLK - MOSTB - first_len).astype(jnp.int32)
    return jnp.concatenate([first_len, long_len, last_len]).astype(jnp.int32)


def shard_levels(stream_key, dims, cuts, smallest, top_value):
    def one(axis_at, blocks):
        draws = jax.random.uniform(jax.random.fold_in(jax.random.fold_in(stream_key, 6), axis_at), (blocks,), jnp.float32, smallest / len(cuts), top_value / len(cuts))
        return jnp.repeat(jnp.exp(draws), dims[axis_at] // blocks).reshape((-1,) + (1,) * (len(dims) - axis_at - 1))

    level = one(*cuts[0])
    for cut in cuts[1:]:
        level = level * one(*cut)
    return level


def scatter_about(rng, dims, width, limit, cuts=(), held_as=jnp.bfloat16):
    array = jax.random.normal(rng, dims, jnp.float32) * width
    if len(cuts) > 0:
        array = shard_levels(rng, dims, cuts, -0.22, 0.18) * array
    return jnp.clip(array, min=-limit, max=limit).astype(held_as)


def setup_inputs(seed: int = 0) -> dict:
    splits = jax.random.split(jax.random.key(seed), 9)
    return {
        "streams": scatter_about(splits[0], (3, TOKENS, C), 1.0, 6.0, ((1, 4), (2, 8))),
        "record_blocks": draw_record_blocks(jax.random.fold_in(splits[8], 71), 0),
        "tail_rows": jax.random.randint(splits[2], (RECORDS,), 1, KM + 1).astype(jnp.int32),
        "unit_dest": draw_unit_dest(jax.random.fold_in(splits[8], 71), 0),
        "mixer_filter": scatter_about(splits[4], (KM, C), 0.09, 0.5, ((1, 32),), jnp.float32),
        "feat_filter": scatter_about(splits[5], (KF, 3, C), 0.38, 2.0, ((2, 32),), jnp.float32),
        "norm_gain": jnp.clip(1.0 + 0.15 * jax.random.normal(splits[6], (C,), jnp.float32), 0.25, 1.75),
        "out_grad": scatter_about(splits[7], (TOKENS, C), 1.0, 6.0, ((0, 4), (1, 8))),
    }


EPSILON = 1e-06

def lag_table(length):
    row_index = np.arange(length)[:, None]
    col_index = np.arange(2 * length)[None, :]
    lagged = length + row_index - col_index
    return np.where((lagged >= 0) & (lagged < length), lagged, length).astype(np.int32)

def toeplitz(filter_bf):
    padded = jnp.concatenate([filter_bf.T, jnp.zeros((filter_bf.shape[1], 1), filter_bf.dtype)], axis=1)
    return jnp.take(padded, jnp.asarray(lag_table(filter_bf.shape[0])), axis=1)

def record_masks(record_blocks, tail_rows, first_block, block_count):
    starts = jnp.cumsum(record_blocks).astype(jnp.int32) - record_blocks
    record_ends = starts + record_blocks - 1
    block_ids = first_block + jnp.arange(block_count, dtype=jnp.int32)
    starts_here = jnp.any(starts[None, :] == block_ids[:, None], axis=1)
    starts_next = jnp.any(starts[None, :] == block_ids[:, None] + 1, axis=1)
    closing = record_ends[None, :] == block_ids[:, None]
    filled_rows = jnp.where(jnp.any(closing, axis=1), lax.optimization_barrier(jnp.sum(jnp.where(closing, tail_rows[None, :], 0), axis=1)), KM)
    live_rows = (jnp.arange(KM, dtype=jnp.int32)[None, :] < filled_rows[:, None]).astype(jnp.float32)
    carry_on = 1.0 - starts_here.astype(jnp.float32)
    carry_next = 1.0 - starts_next.astype(jnp.float32)
    return (carry_on, carry_next, live_rows)

def featurize(extended, feat_taps, live_rows):
    accumulated = jnp.zeros(extended.shape[:2] + (KM, extended.shape[3]), jnp.float32)
    for tap_index in range(KF):
        window = extended[:, :, 8 - tap_index:8 - tap_index + KM].astype(jnp.float32)
        accumulated = accumulated + feat_taps[tap_index][:, None, None, :] * window
    return (accumulated * live_rows[None, :, :, None]).astype(jnp.bfloat16)

def spread(d_extended, feat_taps):
    accumulated = jnp.zeros(d_extended.shape[:2] + (KM, d_extended.shape[3]), jnp.float32)
    for tap_index in range(KF):
        window = d_extended[:, :, tap_index:tap_index + KM].astype(jnp.float32)
        accumulated = accumulated + feat_taps[tap_index][:, None, None, :] * window
    return accumulated.astype(jnp.bfloat16)

def tap_sums(d_feature, extended):
    d_float = d_feature.astype(jnp.float32)
    collected = []
    for tap_index in range(KF):
        window = extended[:, :, 8 - tap_index:8 - tap_index + KM].astype(jnp.float32)
        collected.append(lax.optimization_barrier(jnp.sum(d_float * window, axis=(1, 2))))
    return jnp.stack(collected)

def lag_sums(d_response, both_parts):
    products = jnp.einsum('bic,bkc->cik', d_response.astype(jnp.float32), both_parts.astype(jnp.float32))
    group_width = products.shape[0]
    flattened = jnp.pad(products.reshape(group_width, 2 * KM * KM), ((0, 0), (0, KM)))
    skewed = flattened.reshape(group_width, KM, 2 * KM + 1)
    summed = lax.optimization_barrier(jnp.sum(skewed[:, :, 1:KM + 1], axis=1))
    return summed[:, ::-1].T

def forward_group(packed_group, feat_taps, mixer_taps, carry_on, live_rows):
    block_count = carry_on.shape[0]
    group_width = packed_group.shape[2]
    blocks = packed_group.reshape(3, block_count, KM, group_width)
    zero_tail = jnp.zeros((3, 1, 8, group_width), blocks.dtype)
    tail_part = jnp.concatenate([zero_tail, blocks[:, :-1, KM - 8:]], axis=1)
    tail_part = jnp.where(carry_on[None, :, None, None] > 0, tail_part, jnp.zeros_like(tail_part))
    extended = jnp.concatenate([tail_part, blocks], axis=2)
    feature = featurize(extended, feat_taps, live_rows)
    mixed_in = (feature[1].astype(jnp.float32) * feature[2].astype(jnp.float32)).astype(jnp.bfloat16)
    previous = jnp.concatenate([jnp.zeros((1, KM, group_width), mixed_in.dtype), mixed_in[:-1]], axis=0)
    previous = jnp.where(carry_on[:, None, None] > 0, previous, jnp.zeros_like(previous))
    matrix = toeplitz(mixer_taps.astype(jnp.bfloat16)).astype(jnp.float32)
    response = jnp.einsum('cik,bkc->bic', matrix[:, :, KM:], mixed_in.astype(jnp.float32))
    response = response + jnp.einsum('cik,bkc->bic', matrix[:, :, :KM], previous.astype(jnp.float32))
    gated_out = (feature[0].astype(jnp.float32) * response).astype(jnp.bfloat16)
    return (extended, feature, mixed_in, previous, matrix, response, gated_out)

def backward_group(packed_group, feat_taps, mixer_taps, d_gated, carry_on, carry_next, live_rows):
    extended, feature, mixed_in, previous, matrix, response, unused_out = forward_group(packed_group, feat_taps, mixer_taps, carry_on, live_rows)
    group_width = packed_group.shape[2]
    d_gated_float = d_gated.astype(jnp.float32)
    d_query = d_gated_float * response
    d_response = (d_gated_float * feature[0].astype(jnp.float32)).astype(jnp.bfloat16)
    following = jnp.concatenate([d_response[1:], jnp.zeros((1, KM, group_width), d_response.dtype)], axis=0)
    following = jnp.where(carry_next[:, None, None] > 0, following, jnp.zeros_like(following))
    d_mixed = jnp.einsum('cik,bic->bkc', matrix[:, :, KM:], d_response.astype(jnp.float32))
    d_mixed = d_mixed + jnp.einsum('cik,bic->bkc', matrix[:, :, :KM], following.astype(jnp.float32))
    d_feature = jnp.stack([d_query, d_mixed * feature[2].astype(jnp.float32), d_mixed * feature[1].astype(jnp.float32)]).astype(jnp.bfloat16)
    mixer_part = lag_sums(d_response, jnp.concatenate([previous, mixed_in], axis=1))
    feat_part = tap_sums(d_feature, extended)
    head_rows = jnp.concatenate([d_feature[:, 1:, :8], jnp.zeros((3, 1, 8, group_width), d_feature.dtype)], axis=1)
    head_rows = jnp.where(carry_next[None, :, None, None] > 0, head_rows, jnp.zeros_like(head_rows))
    d_extended = jnp.concatenate([d_feature, head_rows], axis=2)
    return (spread(d_extended, feat_taps), mixer_part, feat_part)

def reference(streams, record_blocks, tail_rows, unit_dest, mixer_filter, feat_filter, norm_gain, out_grad):
    unit_rows = streams.reshape(3, UNITS, UNIT, C)
    inverse = jnp.zeros((UNITS,), jnp.int32).at[unit_dest].set(jnp.arange(UNITS, dtype=jnp.int32))
    packed = jnp.take(unit_rows, inverse, axis=1).reshape(3, TOKENS, C)
    carry_on, carry_next, live_rows = record_masks(record_blocks, tail_rows, 0, NBLK)
    group_width = min(128, C)
    group_count = C // group_width
    packed_groups = packed.reshape(3, TOKENS, group_count, group_width).transpose(2, 0, 1, 3)
    feat_groups = feat_filter.reshape(KF, 3, group_count, group_width).transpose(2, 0, 1, 3)
    mixer_groups = mixer_filter.reshape(KM, group_count, group_width).transpose(1, 0, 2)

    def first_pass(operands):
        return forward_group(operands[0], operands[1], operands[2], carry_on, live_rows)[6]
    gated_groups = lax.map(first_pass, (packed_groups, feat_groups, mixer_groups))
    gated_out = gated_groups.transpose(1, 2, 0, 3).reshape(NBLK, KM, C)
    squares = lax.optimization_barrier(jnp.sum(jnp.square(gated_out.astype(jnp.float32)), axis=-1))
    row_scale = live_rows * lax.rsqrt(squares / C + EPSILON)
    normed = gated_out.astype(jnp.float32) * row_scale[..., None]
    out = (normed * norm_gain).astype(jnp.bfloat16).reshape(TOKENS, C)
    grad_rows = out_grad.reshape(NBLK, KM, C).astype(jnp.float32)
    gain_grad = lax.optimization_barrier(jnp.sum(grad_rows * normed, axis=(0, 1)))
    weighted = grad_rows * norm_gain
    inner_sum = lax.optimization_barrier(jnp.sum(weighted * normed, axis=-1)) / C
    d_gated = (row_scale[..., None] * (weighted - normed * inner_sum[..., None])).astype(jnp.bfloat16)
    d_groups = d_gated.reshape(NBLK, KM, group_count, group_width).transpose(2, 0, 1, 3)

    def second_pass(operands):
        return backward_group(operands[0], operands[1], operands[2], operands[3], carry_on, carry_next, live_rows)
    d_packed, mixer_parts, feat_parts = lax.map(second_pass, (packed_groups, feat_groups, mixer_groups, d_groups))
    d_packed = d_packed.transpose(1, 2, 3, 0, 4).reshape(3, UNITS, UNIT, C)
    stream_grad = jnp.take(d_packed, unit_dest, axis=1).reshape(3, TOKENS, C)
    mixer_grad = mixer_parts.transpose(1, 0, 2).reshape(KM, C)
    feat_grad = feat_parts.transpose(1, 2, 0, 3).reshape(KF, 3, C)
    return (out, stream_grad, mixer_grad, feat_grad, gain_grad)
```

```python
import jax
import jax.numpy as jnp
import numpy as np
from jax import lax
from jax.experimental import pallas as pl
from jax.experimental.pallas import tpu as pltpu
from jax.sharding import PartitionSpec as P

KM = 128
KF = 7
UNIT = 16
HALO = 8
LANES = 128
PER_BLOCK = KM // UNIT


EPSILON = 1e-06

bf16 = jnp.bfloat16
f32 = jnp.float32


def split_bf16(matrix):
    high = matrix.astype(bf16)
    low = (matrix - high.astype(np.float64)).astype(bf16)
    return high, low


def transform_matrices():
    angle = 2.0 * np.pi * (np.arange(KM) + 0.5)[:, None] / (2 * KM)
    ahead = np.arange(KM)[None, :] * angle
    analysis = np.concatenate([np.cos(ahead), -np.sin(ahead)], axis=0)
    high, low = split_bf16(analysis)
    analysis_pair = np.concatenate([high, low], axis=1)

    def synthesis(first):
        turn = (first + np.arange(KM))[:, None] * angle.T
        matrix = np.concatenate([np.cos(turn), -np.sin(turn)], axis=1) / KM
        high, low = split_bf16(matrix)
        return np.concatenate([high, low, high], axis=1)

    return analysis_pair, synthesis(KM), synthesis(0)


def record_layout(record_blocks, tail_rows, block_count):
    starts = jnp.cumsum(record_blocks) - record_blocks
    record_ends = starts + record_blocks - 1
    block_ids = jnp.arange(block_count, dtype=jnp.int32)
    starts_here = jnp.any(starts[None, :] == block_ids[:, None], axis=1)
    starts_next = jnp.any(starts[None, :] == block_ids[:, None] + 1, axis=1)
    starts_next = starts_next | (block_ids == block_count - 1)
    closing = record_ends[None, :] == block_ids[:, None]
    filled_rows = jnp.where(
        jnp.any(closing, axis=1), jnp.sum(jnp.where(closing, tail_rows[None, :], 0), axis=1), KM
    )
    carry_on = 1 - starts_here.astype(jnp.int32)
    carry_next = 1 - starts_next.astype(jnp.int32)
    return jnp.stack([carry_on, carry_next, filled_rows.astype(jnp.int32)])


def analyse(analysis_ref, block):
    twice = jnp.concatenate([block, block], axis=0)
    return jnp.dot(analysis_ref[...], twice, preferred_element_type=f32)


def synthesise(synthesis_ref, real, imag):
    spectrum = jnp.concatenate([real, imag], axis=0)
    high = spectrum.astype(bf16)
    low = (spectrum - high.astype(f32)).astype(bf16)
    stacked = jnp.concatenate([high, high, low], axis=0)
    return jnp.dot(synthesis_ref[...], stacked, preferred_element_type=f32)


def alternate(shape):
    rows = lax.broadcasted_iota(jnp.int32, shape, 0)
    return (1 - 2 * (rows & 1)).astype(f32)


def fetch_block(source_ref, extended_ref, unit_ref, layout_ref, block):
    for unit in range(PER_BLOCK):
        first = pl.multiple_of(unit_ref[block * PER_BLOCK + unit] * UNIT, UNIT)
        extended_ref[HALO + unit * UNIT : HALO + (unit + 1) * UNIT, :] = source_ref[
            pl.ds(first, UNIT), :
        ].astype(f32)
    before = jnp.maximum(block * PER_BLOCK - 1, 0)
    first = pl.multiple_of(unit_ref[before] * UNIT, UNIT)
    rim = source_ref[pl.ds(first, UNIT), :].astype(f32)[UNIT - HALO :]
    extended_ref[0:HALO, :] = jnp.where(layout_ref[0, block] > 0, rim, 0.0)


def store_units(target_ref, unit_ref, block, rows):
    for unit in range(PER_BLOCK):
        first = pl.multiple_of(unit_ref[block * PER_BLOCK + unit] * UNIT, UNIT)
        target_ref[pl.ds(first, UNIT), :] = rows[unit * UNIT : (unit + 1) * UNIT]


def featurize(extended_ref, taps_ref, stream, filled):
    total = None
    for lag in range(KF):
        tap = taps_ref[3 * lag + stream : 3 * lag + stream + 1, :]
        term = tap * extended_ref[HALO - lag : HALO - lag + KM, :]
        total = term if total is None else total + term
    rows = lax.broadcasted_iota(jnp.int32, total.shape, 0)
    return jnp.where(rows < filled, total, 0.0).astype(bf16)


def spread(ahead_ref, taps_ref, stream):
    total = None
    for lag in range(KF):
        tap = taps_ref[3 * lag + stream : 3 * lag + stream + 1, :]
        term = tap * ahead_ref[lag : lag + KM, :]
        total = term if total is None else total + term
    return total.astype(bf16)


def fold(rows):
    return jnp.sum(rows.reshape(-1, 8, rows.shape[1]), axis=0)


def add_tap_sums(sums_ref, d_float, extended_ref):
    for lag in range(KF):
        window = extended_ref[HALO - lag : HALO - lag + KM, :]
        sums_ref[8 * lag : 8 * (lag + 1), :] += fold(d_float * window)


def set_ahead(ahead_ref, d_feature, going_on):
    head = ahead_ref[0:HALO, :]
    ahead_ref[KM : KM + HALO, :] = jnp.where(going_on > 0, head, 0.0)
    ahead_ref[0:KM, :] = d_feature.astype(f32)


def block_rows(block):
    return pl.ds(pl.multiple_of(block * KM, KM), KM)


def forward_kernel(shards, rows, *refs):
    unit_ref, layout_ref, position_ref = refs[:3]
    pieces = refs[3 : 3 + shards]
    taps_ref, mixer_ref, gain_ref, analysis_ref, synthesis_ref = refs[3 + shards : 8 + shards]
    staged_ref, feature_ref, response_ref, spectra_ref, filter_ref, gated_ref, squares_ref = refs[
        8 + shards : 15 + shards
    ]
    leaving = refs[15 + shards : 15 + 2 * shards]
    query_ext, key_ext, value_ext, last_ref, gain_rows_ref, sems = refs[15 + 2 * shards :]
    width = staged_ref.shape[2]
    pairs = staged_ref.shape[1] // (2 * KM)
    arrivals = [
        pltpu.make_async_copy(
            pieces[slot], staged_ref.at[:, pl.ds(slot * rows, rows)], sems.at[slot]
        )
        for slot in range(shards)
    ]
    for copy in arrivals:
        copy.start()
    filter_ref[...] = analyse(analysis_ref, mixer_ref[...].astype(bf16))
    last_ref[...] = jnp.zeros_like(last_ref)
    terms = [term.astype(f32) for term in three_terms(gain_ref[...])]
    rest = jnp.zeros((UNIT - 3, width), f32)
    gain_rows_ref[...] = jnp.concatenate(terms + [rest], axis=0).astype(bf16)
    for copy in arrivals:
        copy.wait()

    def pair_step(pair, carry):
        mixed, queries = [], []
        for half in range(2):
            block = 2 * pair + half
            filled = layout_ref[2, block]
            features = []
            for stream, extended_ref in enumerate((query_ext, key_ext, value_ext)):
                fetch_block(staged_ref.at[stream], extended_ref, unit_ref, layout_ref, block)
                feature = featurize(extended_ref, taps_ref, stream, filled)
                feature_ref[stream, block_rows(block), :] = feature
                features.append(feature.astype(f32))
            queries.append(features[0])
            mixed.append((features[1] * features[2]).astype(bf16))
        own = analyse(analysis_ref, jnp.concatenate(mixed, axis=1))
        first_on = (layout_ref[0, 2 * pair] > 0).astype(f32)
        second_on = (layout_ref[0, 2 * pair + 1] > 0).astype(f32)
        earlier = jnp.concatenate([last_ref[...] * first_on, own[:, :width] * second_on], axis=1)
        last_ref[...] = own[:, width:]
        sign = alternate((KM, 2 * width))
        real = earlier[:KM] + sign * own[KM:]
        imag = earlier[KM:] - sign * own[:KM]
        spectra_ref[pair, 0:KM, :] = real
        spectra_ref[pair, KM:, :] = imag
        filter_real = jnp.concatenate([filter_ref[0:KM, :]] * 2, axis=1)
        filter_imag = jnp.concatenate([filter_ref[KM:, :]] * 2, axis=1)
        response = synthesise(
            synthesis_ref,
            real * filter_real - imag * filter_imag,
            real * filter_imag + imag * filter_real,
        )
        for half in range(2):
            block = 2 * pair + half
            own_response = response[:, half * width : (half + 1) * width]
            response_ref[block_rows(block), :] = own_response
            gated = (queries[half] * own_response).astype(bf16)
            gated_ref[block_rows(block), :] = gated
            gated = gated.astype(f32)
            squares_ref[pl.ds(block, 1), :] = jnp.sum((gated * gated).T, axis=0, keepdims=True)
        return carry

    lax.fori_loop(0, pairs, pair_step, 0)
    departures = send_rows(gated_ref, leaving, position_ref[0], rows, sems)
    for slot, target in enumerate(leaving):
        departures.append(
            pltpu.make_async_copy(
                gain_rows_ref, target.at[pl.ds(rows, UNIT)], sems.at[shards + slot]
            )
        )
    for copy in departures:
        copy.start()
    for copy in departures:
        copy.wait()


def send_rows(source_ref, leaving, position, rows, sems):
    departures = []
    for slot, target in enumerate(leaving):
        first = pl.multiple_of((position ^ slot) * rows, rows)
        departures.append(
            pltpu.make_async_copy(
                source_ref.at[pl.ds(first, rows)], target.at[pl.ds(0, rows)], sems.at[slot]
            )
        )
    return departures


def send_slots(source_ref, leaving, rows, sems):
    departures = [
        pltpu.make_async_copy(source_ref.at[pl.ds(slot * rows, rows)], target, sems.at[slot])
        for slot, target in enumerate(leaving)
    ]
    for copy in departures:
        copy.start()
    for copy in departures:
        copy.wait()


def three_terms(values):
    terms = []
    for _ in range(3):
        terms.append(values.astype(bf16))
        values = values - terms[-1].astype(f32)
    return terms


def sum_lanes(values):
    terms = jnp.concatenate(three_terms(values), axis=1)
    ones = jnp.ones((8, terms.shape[1]), bf16)
    return lax.dot_general(
        ones, terms, (((1,), (1,)), ((), ())), preferred_element_type=f32
    )[0:1]


def product_kernel(shards, rows, *refs):
    position_ref = refs[0]
    pieces = refs[1 : 1 + shards]
    gated_ref, squares_ref, gain_ref, staged_ref, sums_ref, sems = refs[1 + shards :]
    blocks = gated_ref.shape[0] // KM
    arrivals = []
    for slot in range(shards):
        first = pl.multiple_of((position_ref[0] ^ slot) * rows, rows)
        arrivals.append(
            pltpu.make_async_copy(pieces[slot], staged_ref.at[pl.ds(first, rows)], sems.at[slot])
        )
    for copy in arrivals:
        copy.start()
    sums_ref[0:blocks, :] = squares_ref[...]
    for slot in range(shards):
        first_block = (position_ref[0] ^ slot) * (rows // KM)
        for step in range(rows // KM):
            gated = gated_ref[block_rows(first_block + step), :].astype(f32)
            weighted = pieces[slot][step * KM : (step + 1) * KM, :].astype(f32) * gain_ref[...]
            sums_ref[pl.ds(blocks + first_block + step, 1), :] = sum_lanes(weighted * gated)
    for copy in arrivals:
        copy.wait()


def scale_of(sums_ref, block, filled, total_channels):
    lanes = lax.broadcasted_iota(jnp.int32, (1, KM), 1)
    squares = sums_ref[pl.ds(block, 1), :]
    return jnp.where(lanes < filled, lax.rsqrt(squares / total_channels + EPSILON), 0.0)


def down_rows(rows, width):
    count = len(rows)
    terms = [term.astype(f32) for row in rows for term in three_terms(row)]
    rest = jnp.zeros((16 - 3 * count, KM), f32)
    stacked = jnp.concatenate(terms + [rest], axis=0).astype(bf16)
    shape = (16, count * width)
    source = lax.broadcasted_iota(jnp.int32, shape, 0)
    lanes = lax.broadcasted_iota(jnp.int32, shape, 1)
    first = 3 * (lanes // width)
    chosen = ((source >= first) & (source < first + 3)).astype(f32).astype(bf16)
    columns = lax.dot_general(
        stacked, chosen, (((0,), (0,)), ((), ())), preferred_element_type=f32
    )
    return [columns[:, i * width : (i + 1) * width] for i in range(count)]


def norm_kernel(total_channels, shards, rows, *refs):
    (
        unit_ref, layout_ref, cotangent_ref, response_ref, taps_ref, gain_ref, feature_ref,
        gated_ref, sums_ref, d_query_ref, d_response_ref,
    ) = refs[:11]
    leaving = refs[11 : 11 + shards]
    grad_ref, ahead_ref, sems = refs[11 + shards :]
    blocks = gated_ref.shape[0] // KM
    width = gated_ref.shape[1]
    ahead_ref[...] = jnp.zeros_like(ahead_ref)

    def block_step(step, carry):
        block = blocks - 1 - step
        scale_row = scale_of(sums_ref, block, layout_ref[2, block], total_channels)
        products = sums_ref[pl.ds(blocks + block, 1), :]
        inner_row = scale_row * products / total_channels
        scale, pull = down_rows([scale_row, scale_row * scale_row * inner_row], width)
        gated = gated_ref[block_rows(block), :].astype(f32)
        weighted = cotangent_ref[block_rows(block), :].astype(f32) * gain_ref[...]
        d_gated = (scale * weighted - pull * gated).astype(bf16).astype(f32)
        feature = feature_ref[0, block_rows(block), :].astype(f32)
        d_response_ref[block_rows(block), :] = (d_gated * feature).astype(bf16)
        d_query = (d_gated * response_ref[block_rows(block), :]).astype(bf16)
        d_query_ref[block_rows(block), :] = d_query
        set_ahead(ahead_ref, d_query, layout_ref[1, block])
        store_units(grad_ref, unit_ref, block, spread(ahead_ref, taps_ref, 0))
        return carry

    lax.fori_loop(0, blocks, block_step, 0)
    send_slots(grad_ref, leaving, rows, sems)


def mix_back_kernel(shards, rows, *refs):
    (
        unit_ref, layout_ref, taps_ref, analysis_ref, synthesis_ref, feature_ref,
        spectra_ref, filter_ref, d_response_ref, query_piece_ref, mixer_grad_ref, d_others_ref,
    ) = refs[:12]
    leaving = refs[12 : 12 + shards]
    grad_ref, key_ahead, value_ahead, next_ref, cross_ref, sems = refs[12 + shards :]
    width = feature_ref.shape[2]
    pairs = feature_ref.shape[1] // (2 * KM)
    for scratch in (key_ahead, value_ahead, next_ref, cross_ref):
        scratch[...] = jnp.zeros_like(scratch)
    query_copy = pltpu.make_async_copy(query_piece_ref, leaving[1].at[0], sems.at[shards])
    query_copy.start()

    def pair_step(step, carry):
        pair = pairs - 1 - step
        d_response = jnp.concatenate(
            [d_response_ref[block_rows(2 * pair), :], d_response_ref[block_rows(2 * pair + 1), :]],
            axis=1,
        )
        own = analyse(analysis_ref, d_response)
        first_on = (layout_ref[1, 2 * pair] > 0).astype(f32)
        second_on = (layout_ref[1, 2 * pair + 1] > 0).astype(f32)
        later = jnp.concatenate([own[:, width:] * first_on, next_ref[...] * second_on], axis=1)
        next_ref[...] = own[:, :width]
        own_real, own_imag = own[:KM], own[KM:]
        real_x, imag_x = spectra_ref[pair, 0:KM, :], spectra_ref[pair, KM:, :]
        cross_real = own_real * real_x + own_imag * imag_x
        cross_imag = own_imag * real_x - own_real * imag_x
        cross_ref[0:KM, :] += cross_real[:, :width] + cross_real[:, width:]
        cross_ref[KM:, :] += cross_imag[:, :width] + cross_imag[:, width:]
        sign = alternate((KM, 2 * width))
        real = own_real + sign * later[KM:]
        imag = own_imag - sign * later[:KM]
        filter_real = jnp.concatenate([filter_ref[0:KM, :]] * 2, axis=1)
        filter_imag = jnp.concatenate([filter_ref[KM:, :]] * 2, axis=1)
        d_mixed = synthesise(
            synthesis_ref,
            real * filter_real + imag * filter_imag,
            imag * filter_real - real * filter_imag,
        )
        for half in (1, 0):
            block = 2 * pair + half
            d_mixed_block = d_mixed[:, half * width : (half + 1) * width]
            for stream, ahead_ref in ((1, key_ahead), (2, value_ahead)):
                factor = feature_ref[3 - stream, block_rows(block), :].astype(f32)
                d_feature = (d_mixed_block * factor).astype(bf16)
                d_others_ref[stream - 1, block_rows(block), :] = d_feature
                set_ahead(ahead_ref, d_feature, layout_ref[1, block])
                spread_rows = spread(ahead_ref, taps_ref, stream)
                store_units(grad_ref.at[stream - 1], unit_ref, block, spread_rows)
        return carry

    lax.fori_loop(0, pairs, pair_step, 0)
    departures = [
        pltpu.make_async_copy(
            grad_ref.at[:, pl.ds(slot * rows, rows)],
            target.at[1:3] if slot == 1 else target,
            sems.at[slot],
        )
        for slot, target in enumerate(leaving)
    ]
    for copy in departures:
        copy.start()
    sign = alternate((KM, width))
    mixer_grad_ref[...] = synthesise(
        synthesis_ref, sign * cross_ref[KM:, :], -(sign * cross_ref[0:KM, :])
    )
    for copy in departures + [query_copy]:
        copy.wait()


def tap_grad_kernel(
    total_channels,
    unit_ref, layout_ref, staged_ref, d_query_ref, d_others_ref, gated_ref, cotangent_ref,
    sums_ref, taps_grad_ref, gain_grad_ref, extended_ref, tap_sums_ref, gain_sums_ref,
):
    blocks = gated_ref.shape[0] // KM
    width = gated_ref.shape[1]
    tap_sums_ref[...] = jnp.zeros_like(tap_sums_ref)
    gain_sums_ref[...] = jnp.zeros_like(gain_sums_ref)

    def block_step(block, carry):
        scale_row = scale_of(sums_ref, block, layout_ref[2, block], total_channels)
        (scale,) = down_rows([scale_row], width)
        normed = gated_ref[block_rows(block), :].astype(f32) * scale
        cotangent = cotangent_ref[block_rows(block), :].astype(f32)
        gain_sums_ref[...] += fold(cotangent * normed)
        for stream in range(3):
            extended = extended_ref.at[stream]
            fetch_block(staged_ref.at[stream], extended, unit_ref, layout_ref, block)
            if stream == 0:
                d_feature = d_query_ref[block_rows(block), :]
            else:
                d_feature = d_others_ref[stream - 1, block_rows(block), :]
            add_tap_sums(tap_sums_ref.at[stream], d_feature.astype(f32), extended)
        return carry

    lax.fori_loop(0, blocks, block_step, 0)
    gain_grad_ref[...] = jnp.sum(gain_sums_ref[...], axis=0, keepdims=True)
    for stream in range(3):
        for lag in range(KF):
            taps_grad_ref[3 * lag + stream : 3 * lag + stream + 1, :] = jnp.sum(
                tap_sums_ref[stream, 8 * lag : 8 * (lag + 1), :], axis=0, keepdims=True
            )


def scale_out_kernel(total_channels, shards, rows, *refs):
    layout_ref, position_ref, sums_ref = refs[:3]
    pieces = refs[3 : 3 + shards]
    scaled = refs[3 + shards :]

    def block_step(step, carry):
        block = position_ref[0] * (rows // KM) + step
        scale_row = scale_of(sums_ref, block, layout_ref[2, block], total_channels)
        (scale,) = down_rows([scale_row], pieces[0].shape[1])
        for piece, target in zip(pieces, scaled):
            terms = piece[rows : rows + UNIT, :].astype(f32)
            gain = terms[0:1] + terms[1:2] + terms[2:3]
            normed = piece[block_rows(step), :].astype(f32) * scale
            target[block_rows(step), :] = (normed * gain).astype(bf16)
        return carry

    lax.fori_loop(0, rows // KM, block_step, 0)


def lane_place(position, slot, width):
    return pl.ds(pl.multiple_of((position ^ slot) * width, width), width)


def assemble_out_kernel(shards, width, position_ref, *refs):
    pieces, target, sems = refs[:shards], refs[shards], refs[shards + 1]
    copies = []
    for slot, piece in enumerate(pieces):
        lanes = lane_place(position_ref[0], slot, width)
        copies.append(pltpu.make_async_copy(piece, target.at[:, lanes], sems.at[slot]))
    for copy in copies:
        copy.start()
    for copy in copies:
        copy.wait()


def assemble_grad_kernel(shards, width, position_ref, *refs):
    queries, others, target, sems = refs[: shards - 1], refs[shards - 1 : -2], refs[-2], refs[-1]
    copies = []
    for slot in range(shards):
        lanes = lane_place(position_ref[0], slot, width)
        first = 0 if slot == 1 else 1
        copies.append((others[slot], target.at[first:3, :, lanes]))
        if slot != 1:
            copies.append((queries[min(slot, 1) + max(slot - 2, 0)], target.at[0, :, lanes]))
    copies = [
        pltpu.make_async_copy(source, view, sems.at[i]) for i, (source, view) in enumerate(copies)
    ]
    for copy in copies:
        copy.start()
    for copy in copies:
        copy.wait()


NEAR = pltpu.VMEM
FAR = pl.ANY


def run_kernel(kernel, scalars, arrays, outs, scratch, microseconds, name, sems=0):
    in_specs = [pl.BlockSpec(memory_space=pltpu.SMEM)] * len(scalars)
    operands = list(scalars)
    for array, space in arrays:
        operands.append(array)
        in_specs.append(pl.BlockSpec(memory_space=space))
    scratch_shapes = [pltpu.VMEM(s, d) for s, d in scratch]
    if sems:
        scratch_shapes.append(pltpu.SemaphoreType.DMA((sems,)))
    return pl.pallas_call(
        kernel,
        out_shape=[jax.ShapeDtypeStruct(s, d) for s, d, _ in outs],
        in_specs=in_specs,
        out_specs=[pl.BlockSpec(memory_space=space) for _, _, space in outs],
        scratch_shapes=scratch_shapes,
        compiler_params=pltpu.CompilerParams(vmem_limit_bytes=20 * 1024 * 1024),
        cost_estimate=pl.CostEstimate(
            flops=int(microseconds * 1e9), bytes_accessed=0, transcendentals=0
        ),
        name=name,
    )(*operands)


def exchange(array, axis, bits):
    return lax.ppermute(array, axis, [(i, i ^ bits) for i in range(lax.axis_size(axis))])


def butterfly(sums, axis):
    bit = 1
    while bit < lax.axis_size(axis):
        sums = sums + exchange(sums, axis, bit)
        bit *= 2
    return sums


def body(
    streams, record_blocks, tail_rows, unit_dest, mixer_filter, feat_filter, norm_gain, out_grad
):
    rows = streams.shape[1]
    channels = streams.shape[2]
    shards = lax.axis_size("seq")
    position = lax.axis_index("seq")
    total_channels = channels * lax.axis_size("fsdp")
    tokens = rows * shards
    blocks = tokens // KM
    units = tokens // UNIT
    units_dev = rows // UNIT
    narrow = channels // shards
    width = -(-narrow // LANES) * LANES

    def widen(array):
        if width == narrow:
            return array
        return jnp.pad(array, ((0, 0),) * (array.ndim - 1) + ((0, width - narrow),))

    def to_channels(array):
        pieces = []
        for slot in range(shards):
            first = (position ^ slot) * narrow
            part = lax.dynamic_slice_in_dim(array, first, narrow, array.ndim - 1)
            pieces.append(widen(exchange(part, "seq", slot) if slot else part))
        return pieces

    def to_tokens(pieces, slots):
        return [
            exchange(part[..., :narrow], "seq", slot) if slot else part[..., :narrow]
            for slot, part in zip(slots, pieces)
        ]

    every_slot = range(shards)

    position_word = position.astype(jnp.int32).reshape(1)
    layout = record_layout(record_blocks, tail_rows, blocks)
    unit_ids = jnp.arange(units, dtype=jnp.int32)
    loaded_unit = jnp.sum(
        jnp.where(unit_dest[None, :] == unit_ids[:, None], unit_ids[None, :], 0), axis=1
    ).astype(jnp.int32)
    slot = position ^ (loaded_unit // units_dev)
    unit_table = slot * units_dev + loaded_unit % units_dev
    analysis, synthesis_on, synthesis_back = (jnp.asarray(m) for m in transform_matrices())
    taps = widen(feat_filter.reshape(3 * KF, narrow))
    own_gain = norm_gain.reshape(1, narrow)
    gain = widen(own_gain)
    mixer = widen(mixer_filter)

    arrived = to_channels(streams)
    arrived[1], late_grad = lax.optimization_barrier((arrived[1], out_grad))
    cotangent_pieces = to_channels(late_grad)

    whole = (tokens, width)
    spectra_shape = (blocks // 2, 2 * KM, 2 * width)
    extended_shape = (KM + HALO, width)
    extended = (extended_shape, f32)
    scalars = (unit_table, layout)
    forward = run_kernel(
        lambda *refs: forward_kernel(shards, rows, *refs),
        scalars + (position_word,),
        [(part, FAR) for part in arrived]
        + [(a, NEAR) for a in (taps, mixer, gain, analysis, synthesis_on)],
        (
            ((3,) + whole, bf16, NEAR), ((3,) + whole, bf16, NEAR), (whole, f32, NEAR),
            (spectra_shape, f32, NEAR), ((2 * KM, width), f32, NEAR), (whole, bf16, NEAR),
            ((blocks, KM), f32, NEAR),
        ) + (((rows + UNIT, width), bf16, FAR),) * shards,
        (extended,) * 3 + (((2 * KM, width), f32), ((UNIT, width), bf16)),
        9,
        "forward",
        sems=2 * shards,
    )
    staged, features, response, spectra, filter_spectrum, gated, squares = forward[:7]
    gated_back = to_tokens(forward[7:], every_slot)
    cotangent, sums = run_kernel(
        lambda *refs: product_kernel(shards, rows, *refs),
        (position_word,),
        [(a, NEAR) for a in cotangent_pieces] + [(a, NEAR) for a in (gated, squares, gain)],
        ((whole, bf16, NEAR), ((2 * blocks, KM), f32, NEAR)),
        (),
        2,
        "product",
        sems=shards,
    )
    sums = butterfly(sums, "fsdp")
    sums, gated_back = lax.optimization_barrier((sums, gated_back))
    sums = butterfly(sums, "seq")
    norm = run_kernel(
        lambda *refs: norm_kernel(total_channels, shards, rows, *refs),
        scalars,
        [(a, NEAR) for a in (cotangent, response, taps, gain, features, gated, sums)],
        ((whole, bf16, NEAR),) * 2 + (((rows, width), bf16, FAR),) * shards,
        ((whole, bf16), extended),
        3,
        "norm",
        sems=shards,
    )
    d_query, d_response = norm[:2]
    query_back = to_tokens(norm[2:3] + norm[4:], [slot for slot in every_slot if slot != 1])
    back = run_kernel(
        lambda *refs: mix_back_kernel(shards, rows, *refs),
        scalars,
        [
            (a, NEAR)
            for a in (
                taps, analysis, synthesis_back, features, spectra, filter_spectrum, d_response
            )
        ]
        + [(norm[3], FAR)],
        (((KM, width), f32, NEAR), ((2,) + whole, bf16, NEAR))
        + tuple(((3 if slot == 1 else 2, rows, width), bf16, FAR) for slot in every_slot),
        (((2,) + whole, bf16),) + (extended,) * 2 + (((2 * KM, width), f32),) * 2,
        7,
        "mix_back",
        sems=shards + 1,
    )
    mixer_grad, d_others = back[:2]
    others_back = to_tokens(back[2:], every_slot)
    taps_grad, gain_grad = run_kernel(
        lambda *refs: tap_grad_kernel(total_channels, *refs),
        scalars,
        [(a, NEAR) for a in (staged, d_query, d_others, gated, cotangent, sums)],
        (((3 * KF, width), f32, NEAR), ((1, width), f32, NEAR)),
        (((3,) + extended_shape, f32), ((3, 8 * KF, width), f32), ((8, width), f32)),
        4,
        "tap_grad",
    )
    scaled = run_kernel(
        lambda *refs: scale_out_kernel(total_channels, shards, rows, *refs),
        (layout, position_word),
        [(sums, NEAR)] + [(a, NEAR) for a in gated_back],
        (((rows, narrow), bf16, NEAR),) * shards,
        (),
        1,
        "scale_out",
    )
    if width == narrow:
        (out,) = run_kernel(
            lambda *refs: assemble_out_kernel(shards, width, *refs),
            (position_word,),
            [(a, FAR) for a in scaled],
            (((rows, channels), bf16, FAR),),
            (),
            1,
            "assemble_out",
            sems=shards,
        )
        (stream_grad,) = run_kernel(
            lambda *refs: assemble_grad_kernel(shards, width, *refs),
            (position_word,),
            [(a, FAR) for a in query_back] + [(a, FAR) for a in others_back],
            (((3, rows, channels), bf16, FAR),),
            (),
            1,
            "assemble_grad",
            sems=2 * shards,
        )
    else:
        def assemble(pieces):
            stacked = jnp.stack(pieces)
            in_place = jnp.take(stacked, position ^ jnp.arange(shards), axis=0)
            return jnp.moveaxis(in_place, 0, -2).reshape(pieces[0].shape[:-1] + (channels,))

        out = assemble(scaled)
        queries = query_back[:1] + [others_back[1][0]] + query_back[1:]
        others_back[1] = others_back[1][1:]
        stream_grad = jnp.concatenate([assemble(queries)[None], assemble(others_back)])
    feat_grad = taps_grad[:, :narrow].reshape(KF, 3, narrow)
    return (out, stream_grad, mixer_grad[:, :narrow], feat_grad, gain_grad[0, :narrow])


def solution(mesh):
    placed = (
        P(None, "seq", "fsdp"),
        P(),
        P(),
        P(),
        P(None, ("fsdp", "seq")),
        P(None, None, ("fsdp", "seq")),
        P(("fsdp", "seq")),
        P("seq", "fsdp"),
    )
    return jax.shard_map(
        body,
        mesh=mesh,
        in_specs=placed,
        out_specs=(
            P("seq", "fsdp"),
            P(None, "seq", "fsdp"),
            P(None, ("fsdp", "seq")),
            P(None, None, ("fsdp", "seq")),
            P(("fsdp", "seq")),
        ),
        check_vma=False,
    )
```

```python
import jax
import jax.numpy as jnp
import numpy as np
from jax import lax
from jax.experimental import pallas as pl
from jax.experimental.pallas import tpu as pltpu
from jax.sharding import PartitionSpec as P

KM = 128
KF = 7
UNIT = 16
HALO = 8
LANES = 128
PER_BLOCK = KM // UNIT


EPSILON = 1e-06

bf16 = jnp.bfloat16
f32 = jnp.float32


def split_bf16(matrix):
    high = matrix.astype(bf16)
    low = (matrix - high.astype(np.float64)).astype(bf16)
    return high, low


def transform_matrices():
    angle = 2.0 * np.pi * (np.arange(KM) + 0.5)[:, None] / (2 * KM)
    ahead = np.arange(KM)[None, :] * angle
    analysis = np.concatenate([np.cos(ahead), -np.sin(ahead)], axis=0)
    high, low = split_bf16(analysis)
    analysis_pair = np.concatenate([high, low], axis=1)

    def synthesis(first):
        turn = (first + np.arange(KM))[:, None] * angle.T
        matrix = np.concatenate([np.cos(turn), -np.sin(turn)], axis=1) / KM
        high, low = split_bf16(matrix)
        return np.concatenate([high, low], axis=0)

    return analysis_pair, synthesis(KM), synthesis(0)


def record_layout(record_blocks, tail_rows, block_count):
    starts = jnp.cumsum(record_blocks) - record_blocks
    record_ends = starts + record_blocks - 1
    block_ids = jnp.arange(block_count, dtype=jnp.int32)
    starts_here = jnp.any(starts[None, :] == block_ids[:, None], axis=1)
    starts_next = jnp.any(starts[None, :] == block_ids[:, None] + 1, axis=1)
    starts_next = starts_next | (block_ids == block_count - 1)
    closing = record_ends[None, :] == block_ids[:, None]
    filled_rows = jnp.where(
        jnp.any(closing, axis=1), jnp.sum(jnp.where(closing, tail_rows[None, :], 0), axis=1), KM
    )
    carry_on = 1 - starts_here.astype(jnp.int32)
    carry_next = 1 - starts_next.astype(jnp.int32)
    return jnp.stack([carry_on, carry_next, filled_rows.astype(jnp.int32)])


def analyse(analysis_ref, block):
    twice = jnp.concatenate([block, block], axis=0)
    return jnp.dot(analysis_ref[...], twice, preferred_element_type=f32)


def synthesise(synthesis_ref, real, imag):
    spectrum = jnp.concatenate([real, imag], axis=0)
    high = spectrum.astype(bf16)
    low = (spectrum - high.astype(f32)).astype(bf16)
    both = jnp.dot(synthesis_ref[...], high, preferred_element_type=f32)
    rest = jnp.dot(synthesis_ref[0:KM, :], low, preferred_element_type=f32)
    return both[:KM] + (both[KM:] + rest)


def alternate(shape):
    rows = lax.broadcasted_iota(jnp.int32, shape, 0)
    return (1 - 2 * (rows & 1)).astype(f32)


def fetch_block(source_ref, extended_ref, unit_ref, layout_ref, block):
    for unit in range(PER_BLOCK):
        first = pl.multiple_of(unit_ref[block * PER_BLOCK + unit] * UNIT, UNIT)
        extended_ref[HALO + unit * UNIT : HALO + (unit + 1) * UNIT, :] = source_ref[
            pl.ds(first, UNIT), :
        ].astype(f32)
    before = jnp.maximum(block * PER_BLOCK - 1, 0)
    first = pl.multiple_of(unit_ref[before] * UNIT, UNIT)
    rim = source_ref[pl.ds(first, UNIT), :].astype(f32)[UNIT - HALO :]
    extended_ref[0:HALO, :] = jnp.where(layout_ref[0, block] > 0, rim, 0.0)


def store_units(target_ref, unit_ref, block, rows):
    for unit in range(PER_BLOCK):
        first = pl.multiple_of(unit_ref[block * PER_BLOCK + unit] * UNIT, UNIT)
        target_ref[pl.ds(first, UNIT), :] = rows[unit * UNIT : (unit + 1) * UNIT]


def featurize(extended_ref, taps_ref, stream, filled):
    total = None
    for lag in range(KF):
        tap = taps_ref[3 * lag + stream : 3 * lag + stream + 1, :]
        term = tap * extended_ref[HALO - lag : HALO - lag + KM, :]
        total = term if total is None else total + term
    rows = lax.broadcasted_iota(jnp.int32, total.shape, 0)
    return jnp.where(rows < filled, total, 0.0).astype(bf16)


def spread(ahead_ref, taps_ref, stream):
    total = None
    for lag in range(KF):
        tap = taps_ref[3 * lag + stream : 3 * lag + stream + 1, :]
        term = tap * ahead_ref[lag : lag + KM, :]
        total = term if total is None else total + term
    return total.astype(bf16)


def fold(rows):
    return jnp.sum(rows.reshape(-1, 8, rows.shape[1]), axis=0)


def add_tap_sums(sums_ref, d_float, extended_ref):
    for lag in range(KF):
        window = extended_ref[HALO - lag : HALO - lag + KM, :]
        sums_ref[8 * lag : 8 * (lag + 1), :] += fold(d_float * window)


def set_ahead(ahead_ref, layout_ref, block, d_feature):
    ahead_ref[block + 1, 0:KM, :] = d_feature
    going_on = layout_ref[1, jnp.maximum(block - 1, 0)]
    ahead_ref[block, KM:, :] = jnp.where(going_on > 0, d_feature[:HALO], 0.0)


def repeat(count, per_step, work):
    def step(index, carry):
        for offset in range(per_step):
            work(per_step * index + offset, offset)
        return carry

    lax.fori_loop(0, count // per_step, step, 0)


def block_rows(block):
    return pl.ds(pl.multiple_of(block * KM, KM), KM)


def twice(array):
    return jnp.concatenate([array, array], axis=1)


def respond_kernel(shards, rows, *refs):
    unit_ref, layout_ref = refs[:2]
    pieces = refs[2 : 2 + shards]
    taps_ref, mixer_ref, analysis_ref, synthesis_ref = refs[2 + shards : 6 + shards]
    staged_ref, feature_ref, response_ref, filter_ref = refs[6 + shards : 10 + shards]
    extended_ref, mixed_ref, spectra_ref, sems = refs[10 + shards :]
    width = staged_ref.shape[2]
    pairs = staged_ref.shape[1] // (2 * KM)
    arrivals = [
        pltpu.make_async_copy(
            pieces[slot], staged_ref.at[:, pl.ds(slot * rows, rows)], sems.at[slot]
        )
        for slot in range(shards)
    ]
    for copy in arrivals:
        copy.start()
    filter_ref[...] = analyse(analysis_ref, mixer_ref[...].astype(bf16))
    spectra_ref[0, ...] = jnp.zeros(spectra_ref.shape[1:], f32)
    for copy in arrivals:
        copy.wait()

    def feature_pair(pair, offset):
        mixed = []
        for half in range(2):
            block = 2 * pair + half
            filled = layout_ref[2, block]
            features = []
            for stream in range(2):
                extended = extended_ref.at[2 * half + stream]
                fetch_block(staged_ref.at[stream], extended, unit_ref, layout_ref, block)
                feature = featurize(extended, taps_ref, stream + 1, filled)
                feature_ref[stream, block_rows(block), :] = feature
                features.append(feature.astype(f32))
            mixed.append((features[0] * features[1]).astype(bf16))
        mixed_ref[pair, ...] = jnp.concatenate(mixed, axis=1)

    def analyse_pair(pair, offset):
        spectra_ref[pair + 1, ...] = analyse(analysis_ref, mixed_ref[pair, ...])

    def respond_pair(pair, offset):
        own = spectra_ref[pair + 1, ...]
        first_on = (layout_ref[0, 2 * pair] > 0).astype(f32)
        second_on = (layout_ref[0, 2 * pair + 1] > 0).astype(f32)
        earlier = jnp.concatenate(
            [spectra_ref[pair, :, width:] * first_on, own[:, :width] * second_on], axis=1
        )
        sign = alternate((KM, 2 * width))
        real = earlier[:KM] + sign * own[KM:]
        imag = earlier[KM:] - sign * own[:KM]
        filter_real, filter_imag = twice(filter_ref[0:KM, :]), twice(filter_ref[KM:, :])
        response = synthesise(
            synthesis_ref,
            real * filter_real - imag * filter_imag,
            real * filter_imag + imag * filter_real,
        )
        response_ref[block_rows(2 * pair), :] = response[:, :width]
        response_ref[block_rows(2 * pair + 1), :] = response[:, width:]

    repeat(pairs, 1, feature_pair)
    repeat(pairs, 2, analyse_pair)
    repeat(pairs, 2, respond_pair)


def gate_kernel(shards, rows, *refs):
    unit_ref, layout_ref, position_ref = refs[:3]
    pieces = refs[3 : 3 + shards]
    response_ref, taps_ref, gain_ref = refs[3 + shards : 6 + shards]
    staged_ref, feature_ref, gated_ref, squares_ref = refs[6 + shards : 10 + shards]
    leaving = refs[10 + shards : 10 + 2 * shards]
    extended_ref, sems = refs[10 + 2 * shards :]
    width = staged_ref.shape[1]
    blocks = staged_ref.shape[0] // KM
    arrivals = [
        pltpu.make_async_copy(piece, staged_ref.at[pl.ds(slot * rows, rows)], sems.at[slot])
        for slot, piece in enumerate(pieces)
    ]
    for copy in arrivals:
        copy.start()
    terms = [term.astype(f32) for term in bf16_terms(gain_ref[...], 3)]
    rest = jnp.zeros((UNIT - 3, width), f32)
    gain_rows = jnp.concatenate(terms + [rest], axis=0).astype(bf16)
    for shard in range(shards):
        gated_ref[shard, rows:, :] = gain_rows
    for copy in arrivals:
        copy.wait()

    def gate_block(block, offset):
        extended = extended_ref.at[offset]
        fetch_block(staged_ref, extended, unit_ref, layout_ref, block)
        feature = featurize(extended, taps_ref, 0, layout_ref[2, block])
        feature_ref[block_rows(block), :] = feature
        gated = (feature.astype(f32) * response_ref[block_rows(block), :]).astype(bf16)
        set_gated(gated_ref, block, gated)
        gated = gated.astype(f32)
        squares_ref[pl.ds(block, 1), :] = sum_lanes(gated * gated)

    repeat(blocks, 4, gate_block)
    departures = [
        pltpu.make_async_copy(gated_ref.at[position_ref[0] ^ slot], target, sems.at[slot])
        for slot, target in enumerate(leaving)
    ]
    for copy in departures:
        copy.start()
    for copy in departures:
        copy.wait()


def product_kernel(shards, rows, *refs):
    position_ref = refs[0]
    pieces = refs[1 : 1 + shards]
    gated_ref, squares_ref, gain_ref, staged_ref, sums_ref, sems = refs[1 + shards :]
    blocks = squares_ref.shape[0]
    arrivals = []
    for slot in range(shards):
        first = pl.multiple_of((position_ref[0] ^ slot) * rows, rows)
        arrivals.append(
            pltpu.make_async_copy(pieces[slot], staged_ref.at[pl.ds(first, rows)], sems.at[slot])
        )
    for copy in arrivals:
        copy.start()
    sums_ref[0:blocks, :] = squares_ref[...]
    for slot in range(shards):
        shard = position_ref[0] ^ slot
        for step in range(rows // KM):
            here = slice(step * KM, (step + 1) * KM)
            gated = gated_ref[shard, here, :].astype(f32)
            weighted = pieces[slot][here, :].astype(f32) * gain_ref[...]
            block = shard * (rows // KM) + step
            sums_ref[pl.ds(blocks + block, 1), :] = sum_lanes(weighted * gated)
    for copy in arrivals:
        copy.wait()


def gated_place(gated_ref, block):
    per_shard = (gated_ref.shape[1] - UNIT) // KM
    return block // per_shard, block_rows(block % per_shard)


def set_gated(gated_ref, block, gated):
    shard, place = gated_place(gated_ref, block)
    gated_ref[shard, place, :] = gated


def get_gated(gated_ref, block):
    shard, place = gated_place(gated_ref, block)
    return gated_ref[shard, place, :].astype(f32)


def send_slots(source_ref, leaving, rows, sems):
    departures = [
        pltpu.make_async_copy(source_ref.at[pl.ds(slot * rows, rows)], target, sems.at[slot])
        for slot, target in enumerate(leaving)
    ]
    for copy in departures:
        copy.start()
    for copy in departures:
        copy.wait()


def bf16_terms(values, count):
    terms = []
    for _ in range(count):
        terms.append(values.astype(bf16))
        values = values - terms[-1].astype(f32)
    return terms


def sum_lanes(values):
    terms = jnp.concatenate(bf16_terms(values, 2), axis=1)
    ones = jnp.ones((8, terms.shape[1]), bf16)
    return lax.dot_general(
        ones, terms, (((1,), (1,)), ((), ())), preferred_element_type=f32
    )[0:1]


def scale_of(sums_ref, block, filled, total_channels):
    lanes = lax.broadcasted_iota(jnp.int32, (1, KM), 1)
    squares = sums_ref[pl.ds(block, 1), :]
    return jnp.where(lanes < filled, lax.rsqrt(squares / total_channels + EPSILON), 0.0)


def down_rows(row, width):
    return jnp.broadcast_to(row, (width, KM)).T


def norm_kernel(total_channels, shards, rows, *refs):
    (
        unit_ref, layout_ref, cotangent_ref, response_ref, taps_ref, gain_ref, feature_ref,
        gated_ref, sums_ref, d_query_ref, d_response_ref,
    ) = refs[:11]
    leaving = refs[11 : 11 + shards]
    grad_ref, ahead_ref, sems = refs[11 + shards :]
    blocks = cotangent_ref.shape[0] // KM
    width = cotangent_ref.shape[1]
    ahead_ref[blocks, KM:, :] = jnp.zeros((HALO, width), f32)

    def scale_block(block, offset):
        scale_row = scale_of(sums_ref, block, layout_ref[2, block], total_channels)
        products = sums_ref[pl.ds(blocks + block, 1), :]
        inner_row = scale_row * products / total_channels
        scale = down_rows(scale_row, width)
        pull = down_rows(scale_row * scale_row * inner_row, width)
        gated = get_gated(gated_ref, block)
        weighted = cotangent_ref[block_rows(block), :].astype(f32) * gain_ref[...]
        d_gated = (scale * weighted - pull * gated).astype(bf16).astype(f32)
        feature = feature_ref[block_rows(block), :].astype(f32)
        d_response_ref[block_rows(block), :] = (d_gated * feature).astype(bf16)
        d_query = (d_gated * response_ref[block_rows(block), :]).astype(bf16)
        d_query_ref[block_rows(block), :] = d_query
        set_ahead(ahead_ref, layout_ref, block, d_query.astype(f32))

    def spread_block(block, offset):
        spread_rows = spread(ahead_ref.at[block + 1], taps_ref, 0)
        store_units(grad_ref, unit_ref, block, spread_rows)

    repeat(blocks, 2, scale_block)
    repeat(blocks, 2, spread_block)
    send_slots(grad_ref, leaving, rows, sems)


def mix_back_kernel(shards, rows, *refs):
    (
        unit_ref, layout_ref, taps_ref, analysis_ref, synthesis_ref, feature_ref, filter_ref,
        d_response_ref, query_piece_ref, mixer_grad_ref, d_others_ref,
    ) = refs[:11]
    leaving = refs[11 : 11 + shards]
    grad_ref, ahead_ref, spectra_ref, cross_ref, sems = refs[11 + shards :]
    width = feature_ref.shape[2]
    blocks = feature_ref.shape[1] // KM
    pairs = blocks // 2
    query_copy = pltpu.make_async_copy(query_piece_ref, leaving[1].at[0], sems.at[shards])
    query_copy.start()
    cross_ref[...] = jnp.zeros_like(cross_ref)
    spectra_ref[pairs, ...] = jnp.zeros(spectra_ref.shape[1:], f32)
    for stream in range(2):
        ahead_ref[stream, blocks, KM:, :] = jnp.zeros((HALO, width), f32)

    def analyse_pair(pair, offset):
        d_response = jnp.concatenate(
            [d_response_ref[block_rows(2 * pair), :], d_response_ref[block_rows(2 * pair + 1), :]],
            axis=1,
        )
        spectra_ref[pair, ...] = analyse(analysis_ref, d_response)

    def mix_pair(pair, offset):
        own = spectra_ref[pair, ...]
        first_on = (layout_ref[1, 2 * pair] > 0).astype(f32)
        second_on = (layout_ref[1, 2 * pair + 1] > 0).astype(f32)
        later = jnp.concatenate(
            [own[:, width:] * first_on, spectra_ref[pair + 1, :, :width] * second_on], axis=1
        )
        sign = alternate((KM, 2 * width))
        real = own[:KM] + sign * later[KM:]
        imag = own[KM:] - sign * later[:KM]
        mixed = []
        for block in (2 * pair, 2 * pair + 1):
            key_feature = feature_ref[0, block_rows(block), :].astype(f32)
            value_feature = feature_ref[1, block_rows(block), :].astype(f32)
            mixed.append((key_feature * value_feature).astype(bf16))
        source = analyse(analysis_ref, jnp.concatenate(mixed, axis=1))
        cross_real = real * source[:KM] + imag * source[KM:]
        cross_imag = imag * source[:KM] - real * source[KM:]
        cross_ref[0:KM, :] += cross_real[:, :width] + cross_real[:, width:]
        cross_ref[KM:, :] += cross_imag[:, :width] + cross_imag[:, width:]
        filter_real, filter_imag = twice(filter_ref[0:KM, :]), twice(filter_ref[KM:, :])
        d_mixed = synthesise(
            synthesis_ref,
            real * filter_real + imag * filter_imag,
            imag * filter_real - real * filter_imag,
        )
        for half in range(2):
            block = 2 * pair + half
            d_mixed_block = d_mixed[:, half * width : (half + 1) * width]
            for stream in (1, 2):
                factor = feature_ref[2 - stream, block_rows(block), :].astype(f32)
                d_feature = (d_mixed_block * factor).astype(bf16)
                d_others_ref[stream - 1, block_rows(block), :] = d_feature
                set_ahead(ahead_ref.at[stream - 1], layout_ref, block, d_feature.astype(f32))

    def spread_block(block, offset):
        for stream in (1, 2):
            spread_rows = spread(ahead_ref.at[stream - 1, block + 1], taps_ref, stream)
            store_units(grad_ref.at[stream - 1], unit_ref, block, spread_rows)

    repeat(pairs, 2, analyse_pair)
    repeat(pairs, 2, mix_pair)
    repeat(blocks, 1, spread_block)
    departures = [
        pltpu.make_async_copy(
            grad_ref.at[:, pl.ds(slot * rows, rows)],
            target.at[1:3] if slot == 1 else target,
            sems.at[slot],
        )
        for slot, target in enumerate(leaving)
    ]
    for copy in departures:
        copy.start()
    mixer_grad_ref[...] = synthesise(synthesis_ref, cross_ref[0:KM, :], cross_ref[KM:, :])
    for copy in departures + [query_copy]:
        copy.wait()


def tap_grad_kernel(
    total_channels,
    unit_ref, layout_ref, query_ref, others_ref, d_query_ref, d_others_ref, gated_ref,
    cotangent_ref, sums_ref, taps_grad_ref, gain_grad_ref, extended_ref, tap_sums_ref,
    gain_sums_ref,
):
    blocks = cotangent_ref.shape[0] // KM
    width = cotangent_ref.shape[1]
    tap_sums_ref[...] = jnp.zeros_like(tap_sums_ref)
    gain_sums_ref[...] = jnp.zeros_like(gain_sums_ref)

    def block_step(block, carry):
        scale_row = scale_of(sums_ref, block, layout_ref[2, block], total_channels)
        scale = down_rows(scale_row, width)
        normed = get_gated(gated_ref, block) * scale
        cotangent = cotangent_ref[block_rows(block), :].astype(f32)
        gain_sums_ref[...] += fold(cotangent * normed)
        for stream in range(3):
            extended = extended_ref.at[stream]
            if stream == 0:
                source_ref = query_ref
                d_feature = d_query_ref[block_rows(block), :]
            else:
                source_ref = others_ref.at[stream - 1]
                d_feature = d_others_ref[stream - 1, block_rows(block), :]
            fetch_block(source_ref, extended, unit_ref, layout_ref, block)
            add_tap_sums(tap_sums_ref.at[stream], d_feature.astype(f32), extended)
        return carry

    lax.fori_loop(0, blocks, block_step, 0)
    gain_grad_ref[...] = jnp.sum(gain_sums_ref[...], axis=0, keepdims=True)
    for stream in range(3):
        for lag in range(KF):
            taps_grad_ref[3 * lag + stream : 3 * lag + stream + 1, :] = jnp.sum(
                tap_sums_ref[stream, 8 * lag : 8 * (lag + 1), :], axis=0, keepdims=True
            )


def scale_out_kernel(total_channels, shards, rows, *refs):
    layout_ref, position_ref, sums_ref = refs[:3]
    pieces = refs[3 : 3 + shards]
    out_ref, scaled_ref, sems = refs[3 + shards :]
    narrow = pieces[0].shape[1]

    def scale_block(step, offset):
        block = position_ref[0] * (rows // KM) + step
        scale_row = scale_of(sums_ref, block, layout_ref[2, block], total_channels)
        scale = down_rows(scale_row, narrow)
        for slot, piece in enumerate(pieces):
            terms = piece[rows : rows + UNIT, :].astype(f32)
            gain = terms[0:1] + terms[1:2] + terms[2:3]
            normed = piece[block_rows(step), :].astype(f32) * scale
            scaled_ref[slot, block_rows(step), :] = (normed * gain).astype(bf16)

    repeat(rows // KM, 1, scale_block)
    copies = []
    for slot in range(shards):
        if len(out_ref.shape) == 2:
            target = out_ref.at[:, lane_place(position_ref[0], slot, narrow)]
        else:
            target = out_ref.at[position_ref[0] ^ slot]
        copies.append(pltpu.make_async_copy(scaled_ref.at[slot], target, sems.at[slot]))
    for copy in copies:
        copy.start()
    for copy in copies:
        copy.wait()


def lane_place(position, slot, width):
    return pl.ds(pl.multiple_of((position ^ slot) * width, width), width)


def assemble_grad_kernel(shards, width, position_ref, *refs):
    queries, others, target, sems = refs[: shards - 1], refs[shards - 1 : -2], refs[-2], refs[-1]
    copies = []
    for slot in range(shards):
        lanes = lane_place(position_ref[0], slot, width)
        first = 0 if slot == 1 else 1
        copies.append((others[slot], target.at[first:3, :, lanes]))
        if slot != 1:
            copies.append((queries[min(slot, 1) + max(slot - 2, 0)], target.at[0, :, lanes]))
    copies = [
        pltpu.make_async_copy(source, view, sems.at[i]) for i, (source, view) in enumerate(copies)
    ]
    for copy in copies:
        copy.start()
    for copy in copies:
        copy.wait()


NEAR = pltpu.VMEM
FAR = pl.ANY


def run_kernel(kernel, scalars, arrays, outs, scratch, microseconds, name, sems=0):
    in_specs = [pl.BlockSpec(memory_space=pltpu.SMEM)] * len(scalars)
    operands = list(scalars)
    for array, space in arrays:
        operands.append(array)
        in_specs.append(pl.BlockSpec(memory_space=space))
    scratch_shapes = [pltpu.VMEM(s, d) for s, d in scratch]
    memory = 8 * 1024 * 1024 + sum(
        int(np.prod(s)) * jnp.dtype(d).itemsize for s, d in scratch
    )
    if sems:
        scratch_shapes.append(pltpu.SemaphoreType.DMA((sems,)))
    return pl.pallas_call(
        kernel,
        out_shape=[jax.ShapeDtypeStruct(s, d) for s, d, _ in outs],
        in_specs=in_specs,
        out_specs=[pl.BlockSpec(memory_space=space) for _, _, space in outs],
        scratch_shapes=scratch_shapes,
        compiler_params=pltpu.CompilerParams(vmem_limit_bytes=memory),
        cost_estimate=pl.CostEstimate(
            flops=int(microseconds * 1e9), bytes_accessed=0, transcendentals=0
        ),
        name=name,
    )(*operands)


def exchange(array, axis, bits):
    return lax.ppermute(array, axis, [(i, i ^ bits) for i in range(lax.axis_size(axis))])


def butterfly(sums, axis, radix):
    step = 1
    while step < lax.axis_size(axis):
        radix = min(radix, lax.axis_size(axis) // step)
        others = [exchange(sums, axis, step * k) for k in range(1, radix)]
        for other in others:
            sums = sums + other
        step *= radix
    return sums


def body(
    streams, record_blocks, tail_rows, unit_dest, mixer_filter, feat_filter, norm_gain, out_grad
):
    rows = streams.shape[1]
    channels = streams.shape[2]
    shards = lax.axis_size("seq")
    position = lax.axis_index("seq")
    total_channels = channels * lax.axis_size("fsdp")
    tokens = rows * shards
    blocks = tokens // KM
    units = tokens // UNIT
    units_dev = rows // UNIT
    narrow = channels // shards
    width = -(-narrow // LANES) * LANES

    def widen(array):
        if width == narrow:
            return array
        return jnp.pad(array, ((0, 0),) * (array.ndim - 1) + ((0, width - narrow),))

    def lane_parts(array):
        return [
            lax.dynamic_slice_in_dim(array, (position ^ slot) * narrow, narrow, array.ndim - 1)
            for slot in range(shards)
        ]

    def exchange_parts(parts):
        return [
            widen(exchange(part, "seq", slot) if slot else part)
            for slot, part in enumerate(parts)
        ]

    def to_tokens(pieces, slots):
        return [
            exchange(part[..., :narrow], "seq", slot) if slot else part[..., :narrow]
            for slot, part in zip(slots, pieces)
        ]

    every_slot = range(shards)

    position_word = position.astype(jnp.int32).reshape(1)
    layout = record_layout(record_blocks, tail_rows, blocks)
    unit_ids = jnp.arange(units, dtype=jnp.int32)
    loaded_unit = jnp.sum(
        jnp.where(unit_dest[None, :] == unit_ids[:, None], unit_ids[None, :], 0), axis=1
    ).astype(jnp.int32)
    slot = position ^ (loaded_unit // units_dev)
    unit_table = slot * units_dev + loaded_unit % units_dev
    analysis, synthesis_on, synthesis_back = (jnp.asarray(m) for m in transform_matrices())
    taps = widen(feat_filter.reshape(3 * KF, narrow))
    own_gain = norm_gain.reshape(1, narrow)
    gain = widen(own_gain)
    mixer = widen(mixer_filter)

    others = exchange_parts(lane_parts(streams[1:]))
    query_parts = lane_parts(streams[0])
    others[1], query_parts = lax.optimization_barrier((others[1], query_parts))
    queries = exchange_parts(query_parts)
    grad_parts = lane_parts(out_grad)
    queries[1], grad_parts = lax.optimization_barrier((queries[1], grad_parts))
    cotangents = exchange_parts(grad_parts)

    whole = (tokens, width)
    spectra = ((blocks // 2 + 1, 2 * KM, 2 * width), f32)
    extended_shape = (KM + HALO, width)
    scalars = (unit_table, layout)
    staged, features, response, filter_spectrum = run_kernel(
        lambda *refs: respond_kernel(shards, rows, *refs),
        scalars,
        [(part, FAR) for part in others]
        + [(a, NEAR) for a in (taps, mixer, analysis, synthesis_on)],
        (
            ((2,) + whole, bf16, NEAR), ((2,) + whole, bf16, NEAR), (whole, f32, NEAR),
            ((2 * KM, width), f32, NEAR),
        ),
        (((4,) + extended_shape, f32), ((blocks // 2, KM, 2 * width), bf16), spectra),
        6,
        "respond",
        sems=shards,
    )
    gate = run_kernel(
        lambda *refs: gate_kernel(shards, rows, *refs),
        scalars + (position_word,),
        [(part, FAR) for part in queries] + [(a, NEAR) for a in (response, taps, gain)],
        (
            (whole, bf16, NEAR), (whole, bf16, NEAR),
            ((shards, rows + UNIT, width), bf16, NEAR), ((blocks, KM), f32, NEAR),
        ) + (((rows + UNIT, width), bf16, FAR),) * shards,
        (((4,) + extended_shape, f32),),
        0.5,
        "gate",
        sems=shards,
    )
    staged_query, query_feature, gated, squares = gate[:4]
    gated_back = to_tokens(gate[4:], every_slot)
    cotangent, sums = run_kernel(
        lambda *refs: product_kernel(shards, rows, *refs),
        (position_word,),
        [(part, NEAR) for part in cotangents] + [(a, NEAR) for a in (gated, squares, gain)],
        ((whole, bf16, NEAR), ((2 * blocks, KM), f32, NEAR)),
        (),
        2,
        "product",
        sems=shards,
    )
    sums = butterfly(sums, "fsdp", 2)
    sums, gated_back = lax.optimization_barrier((sums, gated_back))
    sums = butterfly(sums, "seq", 4)
    norm = run_kernel(
        lambda *refs: norm_kernel(total_channels, shards, rows, *refs),
        scalars,
        [(a, NEAR) for a in (cotangent, response, taps, gain, query_feature, gated, sums)],
        ((whole, bf16, NEAR),) * 2 + (((rows, width), bf16, FAR),) * shards,
        ((whole, bf16), ((blocks + 1,) + extended_shape, f32)),
        3,
        "norm",
        sems=shards,
    )
    d_query, d_response = norm[:2]
    query_back = to_tokens(norm[2:3] + norm[4:], [slot for slot in every_slot if slot != 1])
    back = run_kernel(
        lambda *refs: mix_back_kernel(shards, rows, *refs),
        scalars,
        [
            (a, NEAR)
            for a in (
                taps, analysis, synthesis_back, features, filter_spectrum, d_response
            )
        ]
        + [(norm[3], FAR)],
        (((KM, width), f32, NEAR), ((2,) + whole, bf16, NEAR))
        + tuple(((3 if slot == 1 else 2, rows, width), bf16, FAR) for slot in every_slot),
        (
            ((2,) + whole, bf16), ((2, blocks + 1) + extended_shape, f32), spectra,
            ((2 * KM, width), f32),
        ),
        7,
        "mix_back",
        sems=shards + 1,
    )
    mixer_grad, d_others = back[:2]
    others_back = to_tokens(back[2:], every_slot)
    d_others, query_back = lax.optimization_barrier((d_others, query_back))
    taps_grad, gain_grad = run_kernel(
        lambda *refs: tap_grad_kernel(total_channels, *refs),
        scalars,
        [
            (a, NEAR)
            for a in (staged_query, staged, d_query, d_others, gated, cotangent, sums)
        ],
        (((3 * KF, width), f32, NEAR), ((1, width), f32, NEAR)),
        (((3,) + extended_shape, f32), ((3, 8 * KF, width), f32), ((8, width), f32)),
        4,
        "tap_grad",
    )
    aligned = width == narrow
    (out,) = run_kernel(
        lambda *refs: scale_out_kernel(total_channels, shards, rows, *refs),
        (layout, position_word),
        [(sums, NEAR)] + [(a, NEAR) for a in gated_back],
        (((rows, channels) if aligned else (shards, rows, narrow), bf16, FAR),),
        (((shards, rows, narrow), bf16),),
        2,
        "scale_out",
        sems=shards,
    )
    if aligned:
        (stream_grad,) = run_kernel(
            lambda *refs: assemble_grad_kernel(shards, width, *refs),
            (position_word,),
            [(a, NEAR) for a in query_back] + [(a, NEAR) for a in others_back],
            (((3, rows, channels), bf16, FAR),),
            (),
            1,
            "assemble_grad",
            sems=2 * shards,
        )
    else:
        def assemble(pieces):
            stacked = jnp.stack(pieces)
            in_place = jnp.take(stacked, position ^ jnp.arange(shards), axis=0)
            return jnp.moveaxis(in_place, 0, -2).reshape(pieces[0].shape[:-1] + (channels,))

        out = out.transpose(1, 0, 2).reshape(rows, channels)
        queries = query_back[:1] + [others_back[1][0]] + query_back[1:]
        others_back[1] = others_back[1][1:]
        stream_grad = jnp.concatenate([assemble(queries)[None], assemble(others_back)])
    feat_grad = taps_grad[:, :narrow].reshape(KF, 3, narrow)
    return (out, stream_grad, mixer_grad[:, :narrow], feat_grad, gain_grad[0, :narrow])


def solution(mesh):
    placed = (
        P(None, "seq", "fsdp"),
        P(),
        P(),
        P(),
        P(None, ("fsdp", "seq")),
        P(None, None, ("fsdp", "seq")),
        P(("fsdp", "seq")),
        P("seq", "fsdp"),
    )
    return jax.shard_map(
        body,
        mesh=mesh,
        in_specs=placed,
        out_specs=(
            P("seq", "fsdp"),
            P(None, "seq", "fsdp"),
            P(None, ("fsdp", "seq")),
            P(None, None, ("fsdp", "seq")),
            P(("fsdp", "seq")),
        ),
        check_vma=False,
    )
```

```python
import jax
import jax.numpy as jnp
import numpy as np
from jax import lax
from jax.experimental import pallas as pl
from jax.experimental.pallas import tpu as pltpu
from jax.sharding import PartitionSpec as P

KM = 128
KF = 7
UNIT = 16
HALO = 8
LANES = 128
PER_BLOCK = KM // UNIT


EPSILON = 1e-06

bf16 = jnp.bfloat16
f32 = jnp.float32


def split_bf16(matrix):
    high = matrix.astype(bf16)
    low = (matrix - high.astype(np.float64)).astype(bf16)
    return high, low


def transform_matrices():
    angle = 2.0 * np.pi * (np.arange(KM) + 0.5)[:, None] / (2 * KM)
    ahead = np.arange(KM)[None, :] * angle
    analysis = np.concatenate([np.cos(ahead), -np.sin(ahead)], axis=0)
    high, low = split_bf16(analysis)
    analysis_pair = np.concatenate([high, low], axis=1)

    def synthesis(first):
        turn = (first + np.arange(KM))[:, None] * angle.T
        matrix = np.concatenate([np.cos(turn), -np.sin(turn)], axis=1) / KM
        high, low = split_bf16(matrix)
        return np.concatenate([high, low], axis=0)

    return analysis_pair, synthesis(KM), synthesis(0)


def record_layout(record_blocks, tail_rows, block_count):
    starts = jnp.cumsum(record_blocks) - record_blocks
    record_ends = starts + record_blocks - 1
    block_ids = jnp.arange(block_count, dtype=jnp.int32)
    starts_here = jnp.any(starts[None, :] == block_ids[:, None], axis=1)
    starts_next = jnp.any(starts[None, :] == block_ids[:, None] + 1, axis=1)
    starts_next = starts_next | (block_ids == block_count - 1)
    closing = record_ends[None, :] == block_ids[:, None]
    filled_rows = jnp.where(
        jnp.any(closing, axis=1), jnp.sum(jnp.where(closing, tail_rows[None, :], 0), axis=1), KM
    )
    carry_on = 1 - starts_here.astype(jnp.int32)
    carry_next = 1 - starts_next.astype(jnp.int32)
    return jnp.stack([carry_on, carry_next, filled_rows.astype(jnp.int32)])


def analyse(analysis_ref, block):
    twice = jnp.concatenate([block, block], axis=0)
    return jnp.dot(analysis_ref[...], twice, preferred_element_type=f32)


def synthesise(synthesis_ref, real, imag):
    spectrum = jnp.concatenate([real, imag], axis=0)
    high = spectrum.astype(bf16)
    low = (spectrum - high.astype(f32)).astype(bf16)
    both = jnp.dot(synthesis_ref[...], high, preferred_element_type=f32)
    rest = jnp.dot(synthesis_ref[0:KM, :], low, preferred_element_type=f32)
    return both[:KM] + (both[KM:] + rest)


def alternate(shape):
    rows = lax.broadcasted_iota(jnp.int32, shape, 0)
    return (1 - 2 * (rows & 1)).astype(f32)


def fetch_block(source_ref, extended_ref, unit_ref, layout_ref, block):
    for unit in range(PER_BLOCK):
        first = pl.multiple_of(unit_ref[block * PER_BLOCK + unit] * UNIT, UNIT)
        extended_ref[HALO + unit * UNIT : HALO + (unit + 1) * UNIT, :] = source_ref[
            pl.ds(first, UNIT), :
        ].astype(f32)
    before = jnp.maximum(block * PER_BLOCK - 1, 0)
    first = pl.multiple_of(unit_ref[before] * UNIT, UNIT)
    rim = source_ref[pl.ds(first, UNIT), :].astype(f32)[UNIT - HALO :]
    extended_ref[0:HALO, :] = jnp.where(layout_ref[0, block] > 0, rim, 0.0)


def store_units(target_ref, unit_ref, block, rows):
    for unit in range(PER_BLOCK):
        first = pl.multiple_of(unit_ref[block * PER_BLOCK + unit] * UNIT, UNIT)
        target_ref[pl.ds(first, UNIT), :] = rows[unit * UNIT : (unit + 1) * UNIT]


def featurize(extended_ref, taps_ref, stream, filled):
    total = None
    for lag in range(KF):
        tap = taps_ref[3 * lag + stream : 3 * lag + stream + 1, :]
        term = tap * extended_ref[HALO - lag : HALO - lag + KM, :]
        total = term if total is None else total + term
    rows = lax.broadcasted_iota(jnp.int32, total.shape, 0)
    return jnp.where(rows < filled, total, 0.0).astype(bf16)


def spread(ahead_ref, taps_ref, stream):
    total = None
    for lag in range(KF):
        tap = taps_ref[3 * lag + stream : 3 * lag + stream + 1, :]
        term = tap * ahead_ref[lag : lag + KM, :]
        total = term if total is None else total + term
    return total.astype(bf16)


def fold(rows):
    return jnp.sum(rows.reshape(-1, 8, rows.shape[1]), axis=0)


def add_tap_sums(sums_ref, d_float, extended_ref):
    for lag in range(KF):
        window = extended_ref[HALO - lag : HALO - lag + KM, :]
        sums_ref[8 * lag : 8 * (lag + 1), :] += fold(d_float * window)


def set_ahead(ahead_ref, layout_ref, block, d_feature):
    ahead_ref[block + 1, 0:KM, :] = d_feature
    going_on = layout_ref[1, jnp.maximum(block - 1, 0)]
    ahead_ref[block, KM:, :] = jnp.where(going_on > 0, d_feature[:HALO], 0.0)


def repeat(count, per_step, work):
    def step(index, carry):
        for offset in range(per_step):
            work(per_step * index + offset, offset)
        return carry

    lax.fori_loop(0, count // per_step, step, 0)


def block_rows(block):
    return pl.ds(pl.multiple_of(block * KM, KM), KM)


def twice(array):
    return jnp.concatenate([array, array], axis=1)


def respond_kernel(shards, rows, *refs):
    unit_ref, layout_ref = refs[:2]
    pieces = refs[2 : 2 + shards]
    taps_ref, mixer_ref, analysis_ref, synthesis_ref = refs[2 + shards : 6 + shards]
    staged_ref, feature_ref, response_ref, filter_ref = refs[6 + shards : 10 + shards]
    extended_ref, mixed_ref, spectra_ref, sems = refs[10 + shards :]
    width = staged_ref.shape[2]
    pairs = staged_ref.shape[1] // (2 * KM)
    arrivals = [
        pltpu.make_async_copy(
            pieces[slot], staged_ref.at[:, pl.ds(slot * rows, rows)], sems.at[slot]
        )
        for slot in range(shards)
    ]
    for copy in arrivals:
        copy.start()
    filter_ref[...] = analyse(analysis_ref, mixer_ref[...].astype(bf16))
    spectra_ref[0, ...] = jnp.zeros(spectra_ref.shape[1:], f32)
    for copy in arrivals:
        copy.wait()

    def feature_pair(pair, offset):
        mixed = []
        for half in range(2):
            block = 2 * pair + half
            filled = layout_ref[2, block]
            features = []
            for stream in range(2):
                extended = extended_ref.at[2 * half + stream]
                fetch_block(staged_ref.at[stream], extended, unit_ref, layout_ref, block)
                feature = featurize(extended, taps_ref, stream + 1, filled)
                feature_ref[stream, block_rows(block), :] = feature
                features.append(feature.astype(f32))
            mixed.append((features[0] * features[1]).astype(bf16))
        mixed_ref[pair, ...] = jnp.concatenate(mixed, axis=1)

    def analyse_pair(pair, offset):
        spectra_ref[pair + 1, ...] = analyse(analysis_ref, mixed_ref[pair, ...])

    def respond_pair(pair, offset):
        own = spectra_ref[pair + 1, ...]
        first_on = (layout_ref[0, 2 * pair] > 0).astype(f32)
        second_on = (layout_ref[0, 2 * pair + 1] > 0).astype(f32)
        earlier = jnp.concatenate(
            [spectra_ref[pair, :, width:] * first_on, own[:, :width] * second_on], axis=1
        )
        sign = alternate((KM, 2 * width))
        real = earlier[:KM] + sign * own[KM:]
        imag = earlier[KM:] - sign * own[:KM]
        filter_real, filter_imag = twice(filter_ref[0:KM, :]), twice(filter_ref[KM:, :])
        response = synthesise(
            synthesis_ref,
            real * filter_real - imag * filter_imag,
            real * filter_imag + imag * filter_real,
        )
        response_ref[block_rows(2 * pair), :] = response[:, :width]
        response_ref[block_rows(2 * pair + 1), :] = response[:, width:]

    repeat(pairs, 1, feature_pair)
    repeat(pairs, 2, analyse_pair)
    repeat(pairs, 2, respond_pair)


def gate_kernel(shards, rows, *refs):
    unit_ref, layout_ref = refs[:2]
    pieces = refs[2 : 2 + shards]
    (
        response_ref, taps_ref, gain_ref, staged_ref, feature_ref, gated_ref, squares_ref,
        extended_ref, sems,
    ) = refs[2 + shards :]
    width = staged_ref.shape[1]
    blocks = staged_ref.shape[0] // KM
    arrivals = [
        pltpu.make_async_copy(piece, staged_ref.at[pl.ds(slot * rows, rows)], sems.at[slot])
        for slot, piece in enumerate(pieces)
    ]
    for copy in arrivals:
        copy.start()
    terms = [term.astype(f32) for term in bf16_terms(gain_ref[...], 3)]
    rest = jnp.zeros((UNIT - 3, width), f32)
    gain_rows = jnp.concatenate(terms + [rest], axis=0).astype(bf16)
    for shard in range(shards):
        gated_ref[shard, rows:, :] = gain_rows
    for copy in arrivals:
        copy.wait()

    def gate_block(block, offset):
        extended = extended_ref.at[offset]
        fetch_block(staged_ref, extended, unit_ref, layout_ref, block)
        feature = featurize(extended, taps_ref, 0, layout_ref[2, block])
        feature_ref[block_rows(block), :] = feature
        gated = (feature.astype(f32) * response_ref[block_rows(block), :]).astype(bf16)
        set_gated(gated_ref, block, gated)
        gated = gated.astype(f32)
        squares_ref[pl.ds(block, 1), :] = sum_lanes(gated * gated)

    repeat(blocks, 4, gate_block)


def pack_kernel(shards, *refs):
    position_ref, gated_ref = refs[:2]
    leaving, sems = refs[2 : 2 + shards], refs[2 + shards]
    departures = [
        pltpu.make_async_copy(gated_ref.at[position_ref[0] ^ slot], target, sems.at[slot])
        for slot, target in enumerate(leaving)
    ]
    for copy in departures:
        copy.start()
    for copy in departures:
        copy.wait()


def product_kernel(shards, rows, *refs):
    position_ref = refs[0]
    pieces = refs[1 : 1 + shards]
    gated_ref, squares_ref, gain_ref, staged_ref, sums_ref, sems = refs[1 + shards :]
    blocks = squares_ref.shape[0]
    arrivals = []
    for slot in range(shards):
        first = pl.multiple_of((position_ref[0] ^ slot) * rows, rows)
        arrivals.append(
            pltpu.make_async_copy(pieces[slot], staged_ref.at[pl.ds(first, rows)], sems.at[slot])
        )
    for copy in arrivals:
        copy.start()
    sums_ref[0:blocks, :] = squares_ref[...]
    for slot in range(shards):
        shard = position_ref[0] ^ slot
        for step in range(rows // KM):
            here = slice(step * KM, (step + 1) * KM)
            gated = gated_ref[shard, here, :].astype(f32)
            weighted = pieces[slot][here, :].astype(f32) * gain_ref[...]
            block = shard * (rows // KM) + step
            sums_ref[pl.ds(blocks + block, 1), :] = sum_lanes(weighted * gated)
    for copy in arrivals:
        copy.wait()


def gated_place(gated_ref, block):
    per_shard = (gated_ref.shape[1] - UNIT) // KM
    return block // per_shard, block_rows(block % per_shard)


def set_gated(gated_ref, block, gated):
    shard, place = gated_place(gated_ref, block)
    gated_ref[shard, place, :] = gated


def get_gated(gated_ref, block):
    shard, place = gated_place(gated_ref, block)
    return gated_ref[shard, place, :].astype(f32)


def send_slots(source_ref, leaving, rows, sems):
    departures = [
        pltpu.make_async_copy(source_ref.at[pl.ds(slot * rows, rows)], target, sems.at[slot])
        for slot, target in enumerate(leaving)
    ]
    for copy in departures:
        copy.start()
    for copy in departures:
        copy.wait()


def bf16_terms(values, count):
    terms = []
    for _ in range(count):
        terms.append(values.astype(bf16))
        values = values - terms[-1].astype(f32)
    return terms


def sum_lanes(values):
    terms = jnp.concatenate(bf16_terms(values, 2), axis=1)
    ones = jnp.ones((8, terms.shape[1]), bf16)
    return lax.dot_general(
        ones, terms, (((1,), (1,)), ((), ())), preferred_element_type=f32
    )[0:1]


def scale_of(sums_ref, block, filled, total_channels):
    lanes = lax.broadcasted_iota(jnp.int32, (1, KM), 1)
    squares = sums_ref[pl.ds(block, 1), :]
    return jnp.where(lanes < filled, lax.rsqrt(squares / total_channels + EPSILON), 0.0)


def down_rows(row, width):
    return jnp.broadcast_to(row, (width, KM)).T


def norm_kernel(total_channels, shards, rows, *refs):
    (
        unit_ref, layout_ref, cotangent_ref, response_ref, taps_ref, gain_ref, feature_ref,
        gated_ref, sums_ref, d_query_ref, d_response_ref,
    ) = refs[:11]
    leaving = refs[11 : 11 + shards]
    grad_ref, ahead_ref, sems = refs[11 + shards :]
    blocks = cotangent_ref.shape[0] // KM
    width = cotangent_ref.shape[1]
    ahead_ref[blocks, KM:, :] = jnp.zeros((HALO, width), f32)

    def scale_block(block, offset):
        scale_row = scale_of(sums_ref, block, layout_ref[2, block], total_channels)
        products = sums_ref[pl.ds(blocks + block, 1), :]
        inner_row = scale_row * products / total_channels
        scale = down_rows(scale_row, width)
        pull = down_rows(scale_row * scale_row * inner_row, width)
        gated = get_gated(gated_ref, block)
        weighted = cotangent_ref[block_rows(block), :].astype(f32) * gain_ref[...]
        d_gated = (scale * weighted - pull * gated).astype(bf16).astype(f32)
        feature = feature_ref[block_rows(block), :].astype(f32)
        d_response_ref[block_rows(block), :] = (d_gated * feature).astype(bf16)
        d_query = (d_gated * response_ref[block_rows(block), :]).astype(bf16)
        d_query_ref[block_rows(block), :] = d_query
        set_ahead(ahead_ref, layout_ref, block, d_query.astype(f32))

    def spread_block(block, offset):
        spread_rows = spread(ahead_ref.at[block + 1], taps_ref, 0)
        store_units(grad_ref, unit_ref, block, spread_rows)

    scale_block(blocks - 1, 0)
    scale_block(blocks - 2, 1)

    def both(index, offset):
        block = blocks - 3 - index
        scale_block(block, offset)
        spread_block(block + 2, offset)

    repeat(blocks - 2, 2, both)
    spread_block(1, 0)
    spread_block(0, 1)
    send_slots(grad_ref, leaving, rows, sems)


def mix_back_kernel(shards, rows, *refs):
    (
        unit_ref, layout_ref, taps_ref, analysis_ref, synthesis_ref, feature_ref, filter_ref,
        d_response_ref, query_piece_ref, mixer_grad_ref, d_others_ref,
    ) = refs[:11]
    leaving = refs[11 : 11 + shards]
    grad_ref, ahead_ref, spectra_ref, cross_ref, sems = refs[11 + shards :]
    width = feature_ref.shape[2]
    blocks = feature_ref.shape[1] // KM
    pairs = blocks // 2
    query_copy = pltpu.make_async_copy(query_piece_ref, leaving[1].at[0], sems.at[shards])
    query_copy.start()
    cross_ref[...] = jnp.zeros_like(cross_ref)
    spectra_ref[pairs, ...] = jnp.zeros(spectra_ref.shape[1:], f32)
    for stream in range(2):
        ahead_ref[stream, blocks, KM:, :] = jnp.zeros((HALO, width), f32)

    def analyse_pair(pair, offset):
        d_response = jnp.concatenate(
            [d_response_ref[block_rows(2 * pair), :], d_response_ref[block_rows(2 * pair + 1), :]],
            axis=1,
        )
        spectra_ref[pair, ...] = analyse(analysis_ref, d_response)

    def mix_pair(pair, offset):
        own = spectra_ref[pair, ...]
        first_on = (layout_ref[1, 2 * pair] > 0).astype(f32)
        second_on = (layout_ref[1, 2 * pair + 1] > 0).astype(f32)
        later = jnp.concatenate(
            [own[:, width:] * first_on, spectra_ref[pair + 1, :, :width] * second_on], axis=1
        )
        sign = alternate((KM, 2 * width))
        real = own[:KM] + sign * later[KM:]
        imag = own[KM:] - sign * later[:KM]
        mixed = []
        for block in (2 * pair, 2 * pair + 1):
            key_feature = feature_ref[0, block_rows(block), :].astype(f32)
            value_feature = feature_ref[1, block_rows(block), :].astype(f32)
            mixed.append((key_feature * value_feature).astype(bf16))
        source = analyse(analysis_ref, jnp.concatenate(mixed, axis=1))
        cross_real = real * source[:KM] + imag * source[KM:]
        cross_imag = imag * source[:KM] - real * source[KM:]
        cross_ref[0:KM, :] += cross_real[:, :width] + cross_real[:, width:]
        cross_ref[KM:, :] += cross_imag[:, :width] + cross_imag[:, width:]
        filter_real, filter_imag = twice(filter_ref[0:KM, :]), twice(filter_ref[KM:, :])
        d_mixed = synthesise(
            synthesis_ref,
            real * filter_real + imag * filter_imag,
            imag * filter_real - real * filter_imag,
        )
        for half in range(2):
            block = 2 * pair + half
            d_mixed_block = d_mixed[:, half * width : (half + 1) * width]
            for stream in (1, 2):
                factor = feature_ref[2 - stream, block_rows(block), :].astype(f32)
                d_feature = (d_mixed_block * factor).astype(bf16)
                d_others_ref[stream - 1, block_rows(block), :] = d_feature
                set_ahead(ahead_ref.at[stream - 1], layout_ref, block, d_feature.astype(f32))

    def spread_block(block, offset):
        for stream in (1, 2):
            spread_rows = spread(ahead_ref.at[stream - 1, block + 1], taps_ref, stream)
            store_units(grad_ref.at[stream - 1], unit_ref, block, spread_rows)

    repeat(pairs, 2, analyse_pair)
    repeat(pairs, 2, mix_pair)
    repeat(blocks, 1, spread_block)
    departures = [
        pltpu.make_async_copy(
            grad_ref.at[:, pl.ds(slot * rows, rows)],
            target.at[1:3] if slot == 1 else target,
            sems.at[slot],
        )
        for slot, target in enumerate(leaving)
    ]
    for copy in departures:
        copy.start()
    mixer_grad_ref[...] = synthesise(synthesis_ref, cross_ref[0:KM, :], cross_ref[KM:, :])
    for copy in departures + [query_copy]:
        copy.wait()


def tap_grad_kernel(
    total_channels,
    unit_ref, layout_ref, query_ref, others_ref, d_query_ref, d_others_ref, gated_ref,
    cotangent_ref, sums_ref, taps_grad_ref, gain_grad_ref, extended_ref, tap_sums_ref,
    gain_sums_ref,
):
    blocks = cotangent_ref.shape[0] // KM
    width = cotangent_ref.shape[1]
    tap_sums_ref[...] = jnp.zeros_like(tap_sums_ref)
    gain_sums_ref[...] = jnp.zeros_like(gain_sums_ref)

    def block_step(block, carry):
        scale_row = scale_of(sums_ref, block, layout_ref[2, block], total_channels)
        scale = down_rows(scale_row, width)
        normed = get_gated(gated_ref, block) * scale
        cotangent = cotangent_ref[block_rows(block), :].astype(f32)
        gain_sums_ref[...] += fold(cotangent * normed)
        for stream in range(3):
            extended = extended_ref.at[stream]
            if stream == 0:
                source_ref = query_ref
                d_feature = d_query_ref[block_rows(block), :]
            else:
                source_ref = others_ref.at[stream - 1]
                d_feature = d_others_ref[stream - 1, block_rows(block), :]
            fetch_block(source_ref, extended, unit_ref, layout_ref, block)
            add_tap_sums(tap_sums_ref.at[stream], d_feature.astype(f32), extended)
        return carry

    lax.fori_loop(0, blocks, block_step, 0)
    gain_grad_ref[...] = jnp.sum(gain_sums_ref[...], axis=0, keepdims=True)
    for stream in range(3):
        for lag in range(KF):
            taps_grad_ref[3 * lag + stream : 3 * lag + stream + 1, :] = jnp.sum(
                tap_sums_ref[stream, 8 * lag : 8 * (lag + 1), :], axis=0, keepdims=True
            )


def scale_out_kernel(total_channels, shards, rows, *refs):
    layout_ref, position_ref, sums_ref = refs[:3]
    pieces = refs[3 : 3 + shards]
    out_ref, scaled_ref, sems = refs[3 + shards :]
    narrow = pieces[0].shape[1]

    def scale_block(step, offset):
        block = position_ref[0] * (rows // KM) + step
        scale_row = scale_of(sums_ref, block, layout_ref[2, block], total_channels)
        scale = down_rows(scale_row, narrow)
        for slot, piece in enumerate(pieces):
            terms = piece[rows : rows + UNIT, :].astype(f32)
            gain = terms[0:1] + terms[1:2] + terms[2:3]
            normed = piece[block_rows(step), :].astype(f32) * scale
            scaled_ref[slot, block_rows(step), :] = (normed * gain).astype(bf16)

    repeat(rows // KM, 1, scale_block)
    copies = []
    for slot in range(shards):
        if len(out_ref.shape) == 2:
            target = out_ref.at[:, lane_place(position_ref[0], slot, narrow)]
        else:
            target = out_ref.at[position_ref[0] ^ slot]
        copies.append(pltpu.make_async_copy(scaled_ref.at[slot], target, sems.at[slot]))
    for copy in copies:
        copy.start()
    for copy in copies:
        copy.wait()


def lane_place(position, slot, width):
    return pl.ds(pl.multiple_of((position ^ slot) * width, width), width)


def assemble_grad_kernel(shards, width, position_ref, *refs):
    queries, others, target, sems = refs[: shards - 1], refs[shards - 1 : -2], refs[-2], refs[-1]
    copies = []
    for slot in range(shards):
        lanes = lane_place(position_ref[0], slot, width)
        first = 0 if slot == 1 else 1
        copies.append((others[slot], target.at[first:3, :, lanes]))
        if slot != 1:
            copies.append((queries[min(slot, 1) + max(slot - 2, 0)], target.at[0, :, lanes]))
    copies = [
        pltpu.make_async_copy(source, view, sems.at[i]) for i, (source, view) in enumerate(copies)
    ]
    for copy in copies:
        copy.start()
    for copy in copies:
        copy.wait()


NEAR = pltpu.VMEM
FAR = pl.ANY


def run_kernel(kernel, scalars, arrays, outs, scratch, microseconds, name, sems=0):
    in_specs = [pl.BlockSpec(memory_space=pltpu.SMEM)] * len(scalars)
    operands = list(scalars)
    for array, space in arrays:
        operands.append(array)
        in_specs.append(pl.BlockSpec(memory_space=space))
    scratch_shapes = [pltpu.VMEM(s, d) for s, d in scratch]
    memory = 8 * 1024 * 1024 + sum(
        int(np.prod(s)) * jnp.dtype(d).itemsize for s, d in scratch
    )
    if sems:
        scratch_shapes.append(pltpu.SemaphoreType.DMA((sems,)))
    return pl.pallas_call(
        kernel,
        out_shape=[jax.ShapeDtypeStruct(s, d) for s, d, _ in outs],
        in_specs=in_specs,
        out_specs=[pl.BlockSpec(memory_space=space) for _, _, space in outs],
        scratch_shapes=scratch_shapes,
        compiler_params=pltpu.CompilerParams(vmem_limit_bytes=memory),
        cost_estimate=pl.CostEstimate(
            flops=int(microseconds * 1e9), bytes_accessed=0, transcendentals=0
        ),
        name=name,
    )(*operands)


def exchange(array, axis, bits):
    return lax.ppermute(array, axis, [(i, i ^ bits) for i in range(lax.axis_size(axis))])


def butterfly(sums, axis, radix):
    step = 1
    while step < lax.axis_size(axis):
        radix = min(radix, lax.axis_size(axis) // step)
        others = [exchange(sums, axis, step * k) for k in range(1, radix)]
        for other in others:
            sums = sums + other
        step *= radix
    return sums


def body(
    streams, record_blocks, tail_rows, unit_dest, mixer_filter, feat_filter, norm_gain, out_grad
):
    rows = streams.shape[1]
    channels = streams.shape[2]
    shards = lax.axis_size("seq")
    position = lax.axis_index("seq")
    total_channels = channels * lax.axis_size("fsdp")
    tokens = rows * shards
    blocks = tokens // KM
    units = tokens // UNIT
    units_dev = rows // UNIT
    narrow = channels // shards
    width = -(-narrow // LANES) * LANES

    def widen(array):
        if width == narrow:
            return array
        return jnp.pad(array, ((0, 0),) * (array.ndim - 1) + ((0, width - narrow),))

    def lane_parts(array):
        return [
            lax.dynamic_slice_in_dim(array, (position ^ slot) * narrow, narrow, array.ndim - 1)
            for slot in range(shards)
        ]

    def exchange_parts(parts):
        return [
            widen(exchange(part, "seq", slot) if slot else part)
            for slot, part in enumerate(parts)
        ]

    def to_tokens(pieces, slots):
        return [
            exchange(part[..., :narrow], "seq", slot) if slot else part[..., :narrow]
            for slot, part in zip(slots, pieces)
        ]

    every_slot = range(shards)

    position_word = position.astype(jnp.int32).reshape(1)
    layout = record_layout(record_blocks, tail_rows, blocks)
    unit_ids = jnp.arange(units, dtype=jnp.int32)
    loaded_unit = jnp.sum(
        jnp.where(unit_dest[None, :] == unit_ids[:, None], unit_ids[None, :], 0), axis=1
    ).astype(jnp.int32)
    slot = position ^ (loaded_unit // units_dev)
    unit_table = slot * units_dev + loaded_unit % units_dev
    analysis, synthesis_on, synthesis_back = (jnp.asarray(m) for m in transform_matrices())
    taps = widen(feat_filter.reshape(3 * KF, narrow))
    own_gain = norm_gain.reshape(1, narrow)
    gain = widen(own_gain)
    mixer = widen(mixer_filter)

    others = exchange_parts(lane_parts(streams[1:]))
    query_parts = lane_parts(streams[0])
    others[1], query_parts = lax.optimization_barrier((others[1], query_parts))
    queries = exchange_parts(query_parts)
    grad_parts = lane_parts(out_grad)
    queries[1], grad_parts = lax.optimization_barrier((queries[1], grad_parts))
    cotangents = exchange_parts(grad_parts)

    whole = (tokens, width)
    spectra = ((blocks // 2 + 1, 2 * KM, 2 * width), f32)
    extended_shape = (KM + HALO, width)
    scalars = (unit_table, layout)
    staged, features, response, filter_spectrum = run_kernel(
        lambda *refs: respond_kernel(shards, rows, *refs),
        scalars,
        [(part, FAR) for part in others]
        + [(a, NEAR) for a in (taps, mixer, analysis, synthesis_on)],
        (
            ((2,) + whole, bf16, NEAR), ((2,) + whole, bf16, NEAR), (whole, f32, NEAR),
            ((2 * KM, width), f32, NEAR),
        ),
        (((4,) + extended_shape, f32), ((blocks // 2, KM, 2 * width), bf16), spectra),
        6,
        "respond",
        sems=shards,
    )
    staged_query, query_feature, gated, squares = run_kernel(
        lambda *refs: gate_kernel(shards, rows, *refs),
        scalars,
        [(part, FAR) for part in queries] + [(a, NEAR) for a in (response, taps, gain)],
        (
            (whole, bf16, NEAR), (whole, bf16, NEAR),
            ((shards, rows + UNIT, width), bf16, NEAR), ((blocks, KM), f32, NEAR),
        ),
        (((4,) + extended_shape, f32),),
        0.5,
        "gate",
        sems=shards,
    )
    cotangent, sums = run_kernel(
        lambda *refs: product_kernel(shards, rows, *refs),
        (position_word,),
        [(part, NEAR) for part in cotangents] + [(a, NEAR) for a in (gated, squares, gain)],
        ((whole, bf16, NEAR), ((2 * blocks, KM), f32, NEAR)),
        (),
        2,
        "product",
        sems=shards,
    )
    sums, ready_gated = lax.optimization_barrier((sums, gated))
    gated_pieces = run_kernel(
        lambda *refs: pack_kernel(shards, *refs),
        (position_word,),
        [(ready_gated, NEAR)],
        (((rows + UNIT, width), bf16, FAR),) * shards,
        (),
        1,
        "pack",
        sems=shards,
    )
    sums = butterfly(sums, "seq", 4)
    gated_far = to_tokens(gated_pieces[2:], every_slot[2:])
    sums = butterfly(sums, "fsdp", 2)
    norm = run_kernel(
        lambda *refs: norm_kernel(total_channels, shards, rows, *refs),
        scalars,
        [(a, NEAR) for a in (cotangent, response, taps, gain, query_feature, gated, sums)],
        ((whole, bf16, NEAR),) * 2 + (((rows, width), bf16, FAR),) * shards,
        ((whole, bf16), ((blocks + 1,) + extended_shape, f32)),
        0.2,
        "norm",
        sems=shards,
    )
    d_query, d_response = norm[:2]
    norm, gated_far, near_piece = lax.optimization_barrier((norm, gated_far, gated_pieces[1]))
    gated_back = to_tokens([gated_pieces[0], near_piece], [0, 1]) + gated_far
    query_back = to_tokens(norm[2:3] + norm[4:], [slot for slot in every_slot if slot != 1])
    back = run_kernel(
        lambda *refs: mix_back_kernel(shards, rows, *refs),
        scalars,
        [
            (a, NEAR)
            for a in (
                taps, analysis, synthesis_back, features, filter_spectrum, d_response
            )
        ]
        + [(norm[3], FAR)],
        (((KM, width), f32, NEAR), ((2,) + whole, bf16, NEAR))
        + tuple(((3 if slot == 1 else 2, rows, width), bf16, FAR) for slot in every_slot),
        (
            ((2,) + whole, bf16), ((2, blocks + 1) + extended_shape, f32), spectra,
            ((2 * KM, width), f32),
        ),
        7,
        "mix_back",
        sems=shards + 1,
    )
    gated_back[1], back = lax.optimization_barrier((gated_back[1], back))
    mixer_grad, d_others = back[:2]
    others_back = to_tokens(back[2:], every_slot)
    d_others, query_back = lax.optimization_barrier((d_others, query_back))
    taps_grad, gain_grad = run_kernel(
        lambda *refs: tap_grad_kernel(total_channels, *refs),
        scalars,
        [
            (a, NEAR)
            for a in (staged_query, staged, d_query, d_others, gated, cotangent, sums)
        ],
        (((3 * KF, width), f32, NEAR), ((1, width), f32, NEAR)),
        (((3,) + extended_shape, f32), ((3, 8 * KF, width), f32), ((8, width), f32)),
        4,
        "tap_grad",
    )
    aligned = width == narrow
    (out,) = run_kernel(
        lambda *refs: scale_out_kernel(total_channels, shards, rows, *refs),
        (layout, position_word),
        [(sums, NEAR)] + [(a, NEAR) for a in gated_back],
        (((rows, channels) if aligned else (shards, rows, narrow), bf16, FAR),),
        (((shards, rows, narrow), bf16),),
        2,
        "scale_out",
        sems=shards,
    )
    if aligned:
        (stream_grad,) = run_kernel(
            lambda *refs: assemble_grad_kernel(shards, width, *refs),
            (position_word,),
            [(a, NEAR) for a in query_back] + [(a, NEAR) for a in others_back],
            (((3, rows, channels), bf16, FAR),),
            (),
            1,
            "assemble_grad",
            sems=2 * shards,
        )
    else:
        def assemble(pieces):
            stacked = jnp.stack(pieces)
            in_place = jnp.take(stacked, position ^ jnp.arange(shards), axis=0)
            return jnp.moveaxis(in_place, 0, -2).reshape(pieces[0].shape[:-1] + (channels,))

        out = out.transpose(1, 0, 2).reshape(rows, channels)
        queries = query_back[:1] + [others_back[1][0]] + query_back[1:]
        others_back[1] = others_back[1][1:]
        stream_grad = jnp.concatenate([assemble(queries)[None], assemble(others_back)])
    feat_grad = taps_grad[:, :narrow].reshape(KF, 3, narrow)
    return (out, stream_grad, mixer_grad[:, :narrow], feat_grad, gain_grad[0, :narrow])


def solution(mesh):
    placed = (
        P(None, "seq", "fsdp"),
        P(),
        P(),
        P(),
        P(None, ("fsdp", "seq")),
        P(None, None, ("fsdp", "seq")),
        P(("fsdp", "seq")),
        P("seq", "fsdp"),
    )
    return jax.shard_map(
        body,
        mesh=mesh,
        in_specs=placed,
        out_specs=(
            P("seq", "fsdp"),
            P(None, "seq", "fsdp"),
            P(None, ("fsdp", "seq")),
            P(None, None, ("fsdp", "seq")),
            P(("fsdp", "seq")),
        ),
        check_vma=False,
    )
```

```python
import jax
import jax.numpy as jnp
import numpy as np
from jax import lax
from jax.experimental import pallas as pl
from jax.experimental.pallas import tpu as pltpu
from jax.sharding import PartitionSpec as P

KM = 128
KF = 7
UNIT = 16
HALO = 8
LANES = 128
PER_BLOCK = KM // UNIT


EPSILON = 1e-06

bf16 = jnp.bfloat16
f32 = jnp.float32


def split_bf16(matrix):
    high = matrix.astype(bf16)
    low = (matrix - high.astype(np.float64)).astype(bf16)
    return high, low


def transform_matrices():
    angle = 2.0 * np.pi * (np.arange(KM) + 0.5)[:, None] / (2 * KM)
    ahead = np.arange(KM)[None, :] * angle
    analysis = np.concatenate([np.cos(ahead), -np.sin(ahead)], axis=0)
    high, low = split_bf16(analysis)
    analysis_pair = np.concatenate([high, low], axis=1)

    def synthesis(first):
        turn = (first + np.arange(KM))[:, None] * angle.T
        matrix = np.concatenate([np.cos(turn), -np.sin(turn)], axis=1) / KM
        high, low = split_bf16(matrix)
        return np.concatenate([high, low], axis=0)

    return analysis_pair, synthesis(KM), synthesis(0)


def record_layout(record_blocks, tail_rows, block_count):
    starts = jnp.cumsum(record_blocks) - record_blocks
    record_ends = starts + record_blocks - 1
    block_ids = jnp.arange(block_count, dtype=jnp.int32)
    starts_here = jnp.any(starts[None, :] == block_ids[:, None], axis=1)
    starts_next = jnp.any(starts[None, :] == block_ids[:, None] + 1, axis=1)
    starts_next = starts_next | (block_ids == block_count - 1)
    closing = record_ends[None, :] == block_ids[:, None]
    filled_rows = jnp.where(
        jnp.any(closing, axis=1), jnp.sum(jnp.where(closing, tail_rows[None, :], 0), axis=1), KM
    )
    carry_on = 1 - starts_here.astype(jnp.int32)
    carry_next = 1 - starts_next.astype(jnp.int32)
    return jnp.stack([carry_on, carry_next, filled_rows.astype(jnp.int32)])


def analyse(analysis_ref, block):
    twice = jnp.concatenate([block, block], axis=0)
    return jnp.dot(analysis_ref[...], twice, preferred_element_type=f32)


def synthesise(synthesis_ref, real, imag):
    spectrum = jnp.concatenate([real, imag], axis=0)
    high = spectrum.astype(bf16)
    low = (spectrum - high.astype(f32)).astype(bf16)
    both = jnp.dot(synthesis_ref[...], high, preferred_element_type=f32)
    rest = jnp.dot(synthesis_ref[0:KM, :], low, preferred_element_type=f32)
    return both[:KM] + (both[KM:] + rest)


def alternate(shape):
    rows = lax.broadcasted_iota(jnp.int32, shape, 0)
    return (1 - 2 * (rows & 1)).astype(f32)


def fetch_block(source_ref, extended_ref, unit_ref, layout_ref, block):
    for unit in range(PER_BLOCK):
        first = pl.multiple_of(unit_ref[block * PER_BLOCK + unit] * UNIT, UNIT)
        extended_ref[HALO + unit * UNIT : HALO + (unit + 1) * UNIT, :] = source_ref[
            pl.ds(first, UNIT), :
        ].astype(f32)
    before = jnp.maximum(block * PER_BLOCK - 1, 0)
    first = pl.multiple_of(unit_ref[before] * UNIT, UNIT)
    rim = source_ref[pl.ds(first, UNIT), :].astype(f32)[UNIT - HALO :]
    extended_ref[0:HALO, :] = jnp.where(layout_ref[0, block] > 0, rim, 0.0)


def store_units(target_ref, unit_ref, block, rows):
    for unit in range(PER_BLOCK):
        first = pl.multiple_of(unit_ref[block * PER_BLOCK + unit] * UNIT, UNIT)
        target_ref[pl.ds(first, UNIT), :] = rows[unit * UNIT : (unit + 1) * UNIT]


def featurize(extended_ref, taps_ref, stream, filled):
    total = None
    for lag in range(KF):
        tap = taps_ref[3 * lag + stream : 3 * lag + stream + 1, :]
        term = tap * extended_ref[HALO - lag : HALO - lag + KM, :]
        total = term if total is None else total + term
    rows = lax.broadcasted_iota(jnp.int32, total.shape, 0)
    return jnp.where(rows < filled, total, 0.0).astype(bf16)


def spread(ahead_ref, taps_ref, stream):
    total = None
    for lag in range(KF):
        tap = taps_ref[3 * lag + stream : 3 * lag + stream + 1, :]
        term = tap * ahead_ref[lag : lag + KM, :]
        total = term if total is None else total + term
    return total.astype(bf16)


def fold(rows):
    return jnp.sum(rows.reshape(-1, 8, rows.shape[1]), axis=0)


def add_tap_sums(sums_ref, d_float, extended_ref):
    for lag in range(KF):
        window = extended_ref[HALO - lag : HALO - lag + KM, :]
        sums_ref[8 * lag : 8 * (lag + 1), :] += fold(d_float * window)


def set_ahead(ahead_ref, layout_ref, block, d_feature):
    ahead_ref[block + 1, 0:KM, :] = d_feature
    going_on = layout_ref[1, jnp.maximum(block - 1, 0)]
    ahead_ref[block, KM:, :] = jnp.where(going_on > 0, d_feature[:HALO], 0.0)


def repeat(count, per_step, work):
    def step(index, carry):
        for offset in range(per_step):
            work(per_step * index + offset, offset)
        return carry

    lax.fori_loop(0, count // per_step, step, 0)


def block_rows(block):
    return pl.ds(pl.multiple_of(block * KM, KM), KM)


def twice(array):
    return jnp.concatenate([array, array], axis=1)


def respond_kernel(shards, rows, *refs):
    unit_ref, layout_ref = refs[:2]
    pieces = refs[2 : 2 + shards]
    taps_ref, mixer_ref, analysis_ref, synthesis_ref = refs[2 + shards : 6 + shards]
    staged_ref, feature_ref, response_ref, filter_ref = refs[6 + shards : 10 + shards]
    extended_ref, mixed_ref, spectra_ref, sems = refs[10 + shards :]
    width = staged_ref.shape[2]
    pairs = staged_ref.shape[1] // (2 * KM)
    arrivals = [
        pltpu.make_async_copy(
            pieces[slot], staged_ref.at[:, pl.ds(slot * rows, rows)], sems.at[slot]
        )
        for slot in range(shards)
    ]
    for copy in arrivals:
        copy.start()
    filter_ref[...] = analyse(analysis_ref, mixer_ref[...].astype(bf16))
    spectra_ref[0, ...] = jnp.zeros(spectra_ref.shape[1:], f32)
    for copy in arrivals:
        copy.wait()

    def feature_pair(pair, offset):
        mixed = []
        for half in range(2):
            block = 2 * pair + half
            filled = layout_ref[2, block]
            features = []
            for stream in range(2):
                extended = extended_ref.at[2 * half + stream]
                fetch_block(staged_ref.at[stream], extended, unit_ref, layout_ref, block)
                feature = featurize(extended, taps_ref, stream + 1, filled)
                feature_ref[stream, block_rows(block), :] = feature
                features.append(feature.astype(f32))
            mixed.append((features[0] * features[1]).astype(bf16))
        mixed_ref[pair, ...] = jnp.concatenate(mixed, axis=1)

    def analyse_pair(pair, offset):
        spectra_ref[pair + 1, ...] = analyse(analysis_ref, mixed_ref[pair, ...])

    def respond_pair(pair, offset):
        own = spectra_ref[pair + 1, ...]
        first_on = (layout_ref[0, 2 * pair] > 0).astype(f32)
        second_on = (layout_ref[0, 2 * pair + 1] > 0).astype(f32)
        earlier = jnp.concatenate(
            [spectra_ref[pair, :, width:] * first_on, own[:, :width] * second_on], axis=1
        )
        sign = alternate((KM, 2 * width))
        real = earlier[:KM] + sign * own[KM:]
        imag = earlier[KM:] - sign * own[:KM]
        filter_real, filter_imag = twice(filter_ref[0:KM, :]), twice(filter_ref[KM:, :])
        response = synthesise(
            synthesis_ref,
            real * filter_real - imag * filter_imag,
            real * filter_imag + imag * filter_real,
        )
        response_ref[block_rows(2 * pair), :] = response[:, :width]
        response_ref[block_rows(2 * pair + 1), :] = response[:, width:]

    repeat(pairs, 1, feature_pair)
    repeat(pairs, 2, analyse_pair)
    repeat(pairs, 2, respond_pair)


def gate_kernel(shards, rows, *refs):
    unit_ref, layout_ref = refs[:2]
    pieces = refs[2 : 2 + shards]
    (
        response_ref, taps_ref, gain_ref, staged_ref, feature_ref, gated_ref, squares_ref,
        extended_ref, sems,
    ) = refs[2 + shards :]
    width = staged_ref.shape[1]
    blocks = staged_ref.shape[0] // KM
    arrivals = [
        pltpu.make_async_copy(piece, staged_ref.at[pl.ds(slot * rows, rows)], sems.at[slot])
        for slot, piece in enumerate(pieces)
    ]
    for copy in arrivals:
        copy.start()
    terms = [term.astype(f32) for term in bf16_terms(gain_ref[...], 3)]
    rest = jnp.zeros((UNIT - 3, width), f32)
    gain_rows = jnp.concatenate(terms + [rest], axis=0).astype(bf16)
    for shard in range(shards):
        gated_ref[shard, rows:, :] = gain_rows
    for copy in arrivals:
        copy.wait()

    def gate_block(block, offset):
        extended = extended_ref.at[offset]
        fetch_block(staged_ref, extended, unit_ref, layout_ref, block)
        feature = featurize(extended, taps_ref, 0, layout_ref[2, block])
        feature_ref[block_rows(block), :] = feature
        gated = (feature.astype(f32) * response_ref[block_rows(block), :]).astype(bf16)
        set_gated(gated_ref, block, gated)
        gated = gated.astype(f32)
        squares_ref[pl.ds(block, 1), :] = sum_lanes(gated * gated)

    repeat(blocks, 4, gate_block)


def pack_kernel(shards, *refs):
    position_ref, gated_ref = refs[:2]
    leaving, sems = refs[2 : 2 + shards], refs[2 + shards]
    departures = [
        pltpu.make_async_copy(gated_ref.at[position_ref[0] ^ slot], target, sems.at[slot])
        for slot, target in enumerate(leaving)
    ]
    for copy in departures:
        copy.start()
    for copy in departures:
        copy.wait()


def product_kernel(shards, rows, *refs):
    position_ref = refs[0]
    pieces = refs[1 : 1 + shards]
    gated_ref, squares_ref, gain_ref, staged_ref, sums_ref, sems = refs[1 + shards :]
    blocks = squares_ref.shape[0]
    arrivals = []
    for slot in range(shards):
        first = pl.multiple_of((position_ref[0] ^ slot) * rows, rows)
        arrivals.append(
            pltpu.make_async_copy(pieces[slot], staged_ref.at[pl.ds(first, rows)], sems.at[slot])
        )
    for copy in arrivals:
        copy.start()
    sums_ref[0:blocks, :] = squares_ref[...]
    for slot in range(shards):
        shard = position_ref[0] ^ slot
        for step in range(rows // KM):
            here = slice(step * KM, (step + 1) * KM)
            gated = gated_ref[shard, here, :].astype(f32)
            weighted = pieces[slot][here, :].astype(f32) * gain_ref[...]
            block = shard * (rows // KM) + step
            sums_ref[pl.ds(blocks + block, 1), :] = sum_lanes(weighted * gated)
    for copy in arrivals:
        copy.wait()


def gated_place(gated_ref, block):
    per_shard = (gated_ref.shape[1] - UNIT) // KM
    return block // per_shard, block_rows(block % per_shard)


def set_gated(gated_ref, block, gated):
    shard, place = gated_place(gated_ref, block)
    gated_ref[shard, place, :] = gated


def get_gated(gated_ref, block):
    shard, place = gated_place(gated_ref, block)
    return gated_ref[shard, place, :].astype(f32)


def send_slots(source_ref, leaving, rows, sems):
    departures = [
        pltpu.make_async_copy(source_ref.at[pl.ds(slot * rows, rows)], target, sems.at[slot])
        for slot, target in enumerate(leaving)
    ]
    for copy in departures:
        copy.start()
    for copy in departures:
        copy.wait()


def bf16_terms(values, count):
    terms = []
    for _ in range(count):
        terms.append(values.astype(bf16))
        values = values - terms[-1].astype(f32)
    return terms


def sum_lanes(values):
    terms = jnp.concatenate(bf16_terms(values, 2), axis=1)
    ones = jnp.ones((8, terms.shape[1]), bf16)
    return lax.dot_general(
        ones, terms, (((1,), (1,)), ((), ())), preferred_element_type=f32
    )[0:1]


def scale_of(sums_ref, block, filled, total_channels):
    lanes = lax.broadcasted_iota(jnp.int32, (1, KM), 1)
    squares = sums_ref[pl.ds(block, 1), :]
    return jnp.where(lanes < filled, lax.rsqrt(squares / total_channels + EPSILON), 0.0)


def down_rows(row, width):
    return jnp.broadcast_to(row, (width, KM)).T


def norm_kernel(total_channels, shards, rows, *refs):
    (
        unit_ref, layout_ref, cotangent_ref, response_ref, taps_ref, gain_ref, feature_ref,
        gated_ref, sums_ref, d_query_ref, d_response_ref,
    ) = refs[:11]
    leaving = refs[11 : 11 + shards]
    grad_ref, ahead_ref, sems = refs[11 + shards :]
    blocks = cotangent_ref.shape[0] // KM
    width = cotangent_ref.shape[1]
    ahead_ref[blocks, KM:, :] = jnp.zeros((HALO, width), f32)

    def scale_block(block, offset):
        scale_row = scale_of(sums_ref, block, layout_ref[2, block], total_channels)
        products = sums_ref[pl.ds(blocks + block, 1), :]
        inner_row = scale_row * products / total_channels
        scale = down_rows(scale_row, width)
        pull = down_rows(scale_row * scale_row * inner_row, width)
        gated = get_gated(gated_ref, block)
        weighted = cotangent_ref[block_rows(block), :].astype(f32) * gain_ref[...]
        d_gated = (scale * weighted - pull * gated).astype(bf16).astype(f32)
        feature = feature_ref[block_rows(block), :].astype(f32)
        d_response_ref[block_rows(block), :] = (d_gated * feature).astype(bf16)
        d_query = (d_gated * response_ref[block_rows(block), :]).astype(bf16)
        d_query_ref[block_rows(block), :] = d_query
        set_ahead(ahead_ref, layout_ref, block, d_query.astype(f32))

    def spread_block(block, offset):
        spread_rows = spread(ahead_ref.at[block + 1], taps_ref, 0)
        store_units(grad_ref, unit_ref, block, spread_rows)

    scale_block(blocks - 1, 0)
    scale_block(blocks - 2, 1)

    def both(index, offset):
        block = blocks - 3 - index
        scale_block(block, offset)
        spread_block(block + 2, offset)

    repeat(blocks - 2, 2, both)
    spread_block(1, 0)
    spread_block(0, 1)
    send_slots(grad_ref, leaving, rows, sems)


def mix_back_kernel(shards, rows, *refs):
    (
        unit_ref, layout_ref, taps_ref, analysis_ref, synthesis_ref, feature_ref, filter_ref,
        d_response_ref, query_piece_ref, mixer_grad_ref, d_others_ref,
    ) = refs[:11]
    leaving = refs[11 : 11 + shards]
    grad_ref, ahead_ref, spectra_ref, cross_ref, sems = refs[11 + shards :]
    width = feature_ref.shape[2]
    blocks = feature_ref.shape[1] // KM
    pairs = blocks // 2
    query_copy = pltpu.make_async_copy(query_piece_ref, leaving[1].at[0], sems.at[shards])
    query_copy.start()
    cross_ref[...] = jnp.zeros_like(cross_ref)
    spectra_ref[pairs, ...] = jnp.zeros(spectra_ref.shape[1:], f32)
    for stream in range(2):
        ahead_ref[stream, blocks, KM:, :] = jnp.zeros((HALO, width), f32)

    def analyse_pair(pair, offset):
        d_response = jnp.concatenate(
            [d_response_ref[block_rows(2 * pair), :], d_response_ref[block_rows(2 * pair + 1), :]],
            axis=1,
        )
        spectra_ref[pair, ...] = analyse(analysis_ref, d_response)

    def mix_pair(pair, offset):
        own = spectra_ref[pair, ...]
        first_on = (layout_ref[1, 2 * pair] > 0).astype(f32)
        second_on = (layout_ref[1, 2 * pair + 1] > 0).astype(f32)
        later = jnp.concatenate(
            [own[:, width:] * first_on, spectra_ref[pair + 1, :, :width] * second_on], axis=1
        )
        sign = alternate((KM, 2 * width))
        real = own[:KM] + sign * later[KM:]
        imag = own[KM:] - sign * later[:KM]
        mixed = []
        for block in (2 * pair, 2 * pair + 1):
            key_feature = feature_ref[0, block_rows(block), :].astype(f32)
            value_feature = feature_ref[1, block_rows(block), :].astype(f32)
            mixed.append((key_feature * value_feature).astype(bf16))
        source = analyse(analysis_ref, jnp.concatenate(mixed, axis=1))
        cross_real = real * source[:KM] + imag * source[KM:]
        cross_imag = imag * source[:KM] - real * source[KM:]
        cross_ref[0:KM, :] += cross_real[:, :width] + cross_real[:, width:]
        cross_ref[KM:, :] += cross_imag[:, :width] + cross_imag[:, width:]
        filter_real, filter_imag = twice(filter_ref[0:KM, :]), twice(filter_ref[KM:, :])
        d_mixed = synthesise(
            synthesis_ref,
            real * filter_real + imag * filter_imag,
            imag * filter_real - real * filter_imag,
        )
        for half in range(2):
            block = 2 * pair + half
            d_mixed_block = d_mixed[:, half * width : (half + 1) * width]
            for stream in (1, 2):
                factor = feature_ref[2 - stream, block_rows(block), :].astype(f32)
                d_feature = (d_mixed_block * factor).astype(bf16)
                d_others_ref[stream - 1, block_rows(block), :] = d_feature
                set_ahead(ahead_ref.at[stream - 1], layout_ref, block, d_feature.astype(f32))

    def spread_block(block, offset):
        for stream in (1, 2):
            spread_rows = spread(ahead_ref.at[stream - 1, block + 1], taps_ref, stream)
            store_units(grad_ref.at[stream - 1], unit_ref, block, spread_rows)

    repeat(pairs, 2, analyse_pair)
    repeat(pairs, 2, mix_pair)
    repeat(blocks, 1, spread_block)
    departures = [
        pltpu.make_async_copy(
            grad_ref.at[:, pl.ds(slot * rows, rows)],
            target.at[1:3] if slot == 1 else target,
            sems.at[slot],
        )
        for slot, target in enumerate(leaving)
    ]
    for copy in departures:
        copy.start()
    mixer_grad_ref[...] = synthesise(synthesis_ref, cross_ref[0:KM, :], cross_ref[KM:, :])
    for copy in departures + [query_copy]:
        copy.wait()


def tap_grad_kernel(
    total_channels,
    unit_ref, layout_ref, query_ref, others_ref, d_query_ref, d_others_ref, gated_ref,
    cotangent_ref, sums_ref, taps_grad_ref, gain_grad_ref, extended_ref, tap_sums_ref,
    gain_sums_ref,
):
    blocks = cotangent_ref.shape[0] // KM
    width = cotangent_ref.shape[1]
    tap_sums_ref[...] = jnp.zeros_like(tap_sums_ref)
    gain_sums_ref[...] = jnp.zeros_like(gain_sums_ref)

    def block_step(block, carry):
        scale_row = scale_of(sums_ref, block, layout_ref[2, block], total_channels)
        scale = down_rows(scale_row, width)
        normed = get_gated(gated_ref, block) * scale
        cotangent = cotangent_ref[block_rows(block), :].astype(f32)
        gain_sums_ref[...] += fold(cotangent * normed)
        for stream in range(3):
            extended = extended_ref.at[stream]
            if stream == 0:
                source_ref = query_ref
                d_feature = d_query_ref[block_rows(block), :]
            else:
                source_ref = others_ref.at[stream - 1]
                d_feature = d_others_ref[stream - 1, block_rows(block), :]
            fetch_block(source_ref, extended, unit_ref, layout_ref, block)
            add_tap_sums(tap_sums_ref.at[stream], d_feature.astype(f32), extended)
        return carry

    lax.fori_loop(0, blocks, block_step, 0)
    gain_grad_ref[...] = jnp.sum(gain_sums_ref[...], axis=0, keepdims=True)
    for stream in range(3):
        for lag in range(KF):
            taps_grad_ref[3 * lag + stream : 3 * lag + stream + 1, :] = jnp.sum(
                tap_sums_ref[stream, 8 * lag : 8 * (lag + 1), :], axis=0, keepdims=True
            )


def scale_out_kernel(total_channels, shards, rows, *refs):
    layout_ref, position_ref, sums_ref = refs[:3]
    pieces = refs[3 : 3 + shards]
    out_ref, scaled_ref, sems = refs[3 + shards :]
    narrow = pieces[0].shape[1]

    def scale_block(step, offset):
        block = position_ref[0] * (rows // KM) + step
        scale_row = scale_of(sums_ref, block, layout_ref[2, block], total_channels)
        scale = down_rows(scale_row, narrow)
        for slot, piece in enumerate(pieces):
            terms = piece[rows : rows + UNIT, :].astype(f32)
            gain = terms[0:1] + terms[1:2] + terms[2:3]
            normed = piece[block_rows(step), :].astype(f32) * scale
            scaled_ref[slot, block_rows(step), :] = (normed * gain).astype(bf16)

    repeat(rows // KM, 1, scale_block)
    copies = []
    for slot in range(shards):
        if len(out_ref.shape) == 2:
            target = out_ref.at[:, lane_place(position_ref[0], slot, narrow)]
        else:
            target = out_ref.at[position_ref[0] ^ slot]
        copies.append(pltpu.make_async_copy(scaled_ref.at[slot], target, sems.at[slot]))
    for copy in copies:
        copy.start()
    for copy in copies:
        copy.wait()


def lane_place(position, slot, width):
    return pl.ds(pl.multiple_of((position ^ slot) * width, width), width)


def assemble_grad_kernel(shards, width, position_ref, *refs):
    queries, others, target, sems = refs[: shards - 1], refs[shards - 1 : -2], refs[-2], refs[-1]
    copies = []
    for slot in range(shards):
        lanes = lane_place(position_ref[0], slot, width)
        first = 0 if slot == 1 else 1
        copies.append((others[slot], target.at[first:3, :, lanes]))
        if slot != 1:
            copies.append((queries[min(slot, 1) + max(slot - 2, 0)], target.at[0, :, lanes]))
    copies = [
        pltpu.make_async_copy(source, view, sems.at[i]) for i, (source, view) in enumerate(copies)
    ]
    for copy in copies:
        copy.start()
    for copy in copies:
        copy.wait()


NEAR = pltpu.VMEM
FAR = pl.ANY


def run_kernel(kernel, scalars, arrays, outs, scratch, microseconds, name, sems=0):
    in_specs = [pl.BlockSpec(memory_space=pltpu.SMEM)] * len(scalars)
    operands = list(scalars)
    for array, space in arrays:
        operands.append(array)
        in_specs.append(pl.BlockSpec(memory_space=space))
    scratch_shapes = [pltpu.VMEM(s, d) for s, d in scratch]
    memory = 8 * 1024 * 1024 + sum(
        int(np.prod(s)) * jnp.dtype(d).itemsize for s, d in scratch
    )
    if sems:
        scratch_shapes.append(pltpu.SemaphoreType.DMA((sems,)))
    return pl.pallas_call(
        kernel,
        out_shape=[jax.ShapeDtypeStruct(s, d) for s, d, _ in outs],
        in_specs=in_specs,
        out_specs=[pl.BlockSpec(memory_space=space) for _, _, space in outs],
        scratch_shapes=scratch_shapes,
        compiler_params=pltpu.CompilerParams(vmem_limit_bytes=memory),
        cost_estimate=pl.CostEstimate(
            flops=int(microseconds * 1e9), bytes_accessed=0, transcendentals=0
        ),
        name=name,
    )(*operands)


def exchange(array, axis, bits):
    return lax.ppermute(array, axis, [(i, i ^ bits) for i in range(lax.axis_size(axis))])


def butterfly(sums, axis, radix):
    step = 1
    while step < lax.axis_size(axis):
        radix = min(radix, lax.axis_size(axis) // step)
        others = [exchange(sums, axis, step * k) for k in range(1, radix)]
        for other in others:
            sums = sums + other
        step *= radix
    return sums


def body(
    streams, record_blocks, tail_rows, unit_dest, mixer_filter, feat_filter, norm_gain, out_grad
):
    rows = streams.shape[1]
    channels = streams.shape[2]
    shards = lax.axis_size("seq")
    position = lax.axis_index("seq")
    total_channels = channels * lax.axis_size("fsdp")
    tokens = rows * shards
    blocks = tokens // KM
    units = tokens // UNIT
    units_dev = rows // UNIT
    narrow = channels // shards
    width = -(-narrow // LANES) * LANES

    def widen(array):
        if width == narrow:
            return array
        return jnp.pad(array, ((0, 0),) * (array.ndim - 1) + ((0, width - narrow),))

    def lane_parts(array):
        return [
            lax.dynamic_slice_in_dim(array, (position ^ slot) * narrow, narrow, array.ndim - 1)
            for slot in range(shards)
        ]

    def exchange_parts(parts):
        return [
            widen(exchange(part, "seq", slot) if slot else part)
            for slot, part in enumerate(parts)
        ]

    def to_tokens(pieces, slots):
        return [
            exchange(part[..., :narrow], "seq", slot) if slot else part[..., :narrow]
            for slot, part in zip(slots, pieces)
        ]

    every_slot = range(shards)

    position_word = position.astype(jnp.int32).reshape(1)
    layout = record_layout(record_blocks, tail_rows, blocks)
    unit_ids = jnp.arange(units, dtype=jnp.int32)
    loaded_unit = jnp.sum(
        jnp.where(unit_dest[None, :] == unit_ids[:, None], unit_ids[None, :], 0), axis=1
    ).astype(jnp.int32)
    slot = position ^ (loaded_unit // units_dev)
    unit_table = slot * units_dev + loaded_unit % units_dev
    analysis, synthesis_on, synthesis_back = (jnp.asarray(m) for m in transform_matrices())
    taps = widen(feat_filter.reshape(3 * KF, narrow))
    own_gain = norm_gain.reshape(1, narrow)
    gain = widen(own_gain)
    mixer = widen(mixer_filter)

    others = exchange_parts(lane_parts(streams[1:]))
    query_parts = lane_parts(streams[0])
    others[1], query_parts = lax.optimization_barrier((others[1], query_parts))
    queries = exchange_parts(query_parts)
    grad_parts = lane_parts(out_grad)
    queries[1], grad_parts = lax.optimization_barrier((queries[1], grad_parts))
    cotangents = exchange_parts(grad_parts)

    whole = (tokens, width)
    spectra = ((blocks // 2 + 1, 2 * KM, 2 * width), f32)
    extended_shape = (KM + HALO, width)
    scalars = (unit_table, layout)
    staged, features, response, filter_spectrum = run_kernel(
        lambda *refs: respond_kernel(shards, rows, *refs),
        scalars,
        [(part, FAR) for part in others]
        + [(a, NEAR) for a in (taps, mixer, analysis, synthesis_on)],
        (
            ((2,) + whole, bf16, NEAR), ((2,) + whole, bf16, NEAR), (whole, f32, NEAR),
            ((2 * KM, width), f32, NEAR),
        ),
        (((4,) + extended_shape, f32), ((blocks // 2, KM, 2 * width), bf16), spectra),
        6,
        "respond",
        sems=shards,
    )
    staged_query, query_feature, gated, squares = run_kernel(
        lambda *refs: gate_kernel(shards, rows, *refs),
        scalars,
        [(part, FAR) for part in queries] + [(a, NEAR) for a in (response, taps, gain)],
        (
            (whole, bf16, NEAR), (whole, bf16, NEAR),
            ((shards, rows + UNIT, width), bf16, NEAR), ((blocks, KM), f32, NEAR),
        ),
        (((4,) + extended_shape, f32),),
        0.5,
        "gate",
        sems=shards,
    )
    cotangent, sums = run_kernel(
        lambda *refs: product_kernel(shards, rows, *refs),
        (position_word,),
        [(part, NEAR) for part in cotangents] + [(a, NEAR) for a in (gated, squares, gain)],
        ((whole, bf16, NEAR), ((2 * blocks, KM), f32, NEAR)),
        (),
        2,
        "product",
        sems=shards,
    )
    sums, ready_gated = lax.optimization_barrier((sums, gated))
    gated_pieces = run_kernel(
        lambda *refs: pack_kernel(shards, *refs),
        (position_word,),
        [(ready_gated, NEAR)],
        (((rows + UNIT, width), bf16, FAR),) * shards,
        (),
        1,
        "pack",
        sems=shards,
    )
    sums = butterfly(sums, "seq", 4)
    gated_far = to_tokens(gated_pieces[2:], every_slot[2:])
    sums = butterfly(sums, "fsdp", 2)
    norm = run_kernel(
        lambda *refs: norm_kernel(total_channels, shards, rows, *refs),
        scalars,
        [(a, NEAR) for a in (cotangent, response, taps, gain, query_feature, gated, sums)],
        ((whole, bf16, NEAR),) * 2 + (((rows, width), bf16, FAR),) * shards,
        ((whole, bf16), ((blocks + 1,) + extended_shape, f32)),
        0.2,
        "norm",
        sems=shards,
    )
    d_query, d_response = norm[:2]
    norm, gated_far, near_piece = lax.optimization_barrier((norm, gated_far, gated_pieces[1]))
    gated_back = to_tokens([gated_pieces[0], near_piece], [0, 1]) + gated_far
    query_back = to_tokens(norm[2:3] + norm[4:], [slot for slot in every_slot if slot != 1])
    back = run_kernel(
        lambda *refs: mix_back_kernel(shards, rows, *refs),
        scalars,
        [
            (a, NEAR)
            for a in (
                taps, analysis, synthesis_back, features, filter_spectrum, d_response
            )
        ]
        + [(norm[3], FAR)],
        (((KM, width), f32, NEAR), ((2,) + whole, bf16, NEAR))
        + tuple(((3 if slot == 1 else 2, rows, width), bf16, FAR) for slot in every_slot),
        (
            ((2,) + whole, bf16), ((2, blocks + 1) + extended_shape, f32), spectra,
            ((2 * KM, width), f32),
        ),
        7,
        "mix_back",
        sems=shards + 1,
    )
    mixer_grad, d_others, *back_pieces = back
    gated_back[1], back_pieces[1] = lax.optimization_barrier((gated_back[1], back_pieces[1]))
    others_back = to_tokens(back_pieces, every_slot)
    taps_grad, gain_grad = run_kernel(
        lambda *refs: tap_grad_kernel(total_channels, *refs),
        scalars,
        [
            (a, NEAR)
            for a in (staged_query, staged, d_query, d_others, gated, cotangent, sums)
        ],
        (((3 * KF, width), f32, NEAR), ((1, width), f32, NEAR)),
        (((3,) + extended_shape, f32), ((3, 8 * KF, width), f32), ((8, width), f32)),
        4,
        "tap_grad",
    )
    aligned = width == narrow
    (out,) = run_kernel(
        lambda *refs: scale_out_kernel(total_channels, shards, rows, *refs),
        (layout, position_word),
        [(sums, NEAR)] + [(a, NEAR) for a in gated_back],
        (((rows, channels) if aligned else (shards, rows, narrow), bf16, FAR),),
        (((shards, rows, narrow), bf16),),
        2,
        "scale_out",
        sems=shards,
    )
    if aligned:
        (stream_grad,) = run_kernel(
            lambda *refs: assemble_grad_kernel(shards, width, *refs),
            (position_word,),
            [(a, NEAR) for a in query_back] + [(a, NEAR) for a in others_back],
            (((3, rows, channels), bf16, FAR),),
            (),
            1,
            "assemble_grad",
            sems=2 * shards,
        )
    else:
        def assemble(pieces):
            stacked = jnp.stack(pieces)
            in_place = jnp.take(stacked, position ^ jnp.arange(shards), axis=0)
            return jnp.moveaxis(in_place, 0, -2).reshape(pieces[0].shape[:-1] + (channels,))

        out = out.transpose(1, 0, 2).reshape(rows, channels)
        queries = query_back[:1] + [others_back[1][0]] + query_back[1:]
        others_back[1] = others_back[1][1:]
        stream_grad = jnp.concatenate([assemble(queries)[None], assemble(others_back)])
    feat_grad = taps_grad[:, :narrow].reshape(KF, 3, narrow)
    return (out, stream_grad, mixer_grad[:, :narrow], feat_grad, gain_grad[0, :narrow])


def solution(mesh):
    placed = (
        P(None, "seq", "fsdp"),
        P(),
        P(),
        P(),
        P(None, ("fsdp", "seq")),
        P(None, None, ("fsdp", "seq")),
        P(("fsdp", "seq")),
        P("seq", "fsdp"),
    )
    return jax.shard_map(
        body,
        mesh=mesh,
        in_specs=placed,
        out_specs=(
            P("seq", "fsdp"),
            P(None, "seq", "fsdp"),
            P(None, ("fsdp", "seq")),
            P(None, None, ("fsdp", "seq")),
            P(("fsdp", "seq")),
        ),
        check_vma=False,
    )
```

```python
import jax
import jax.numpy as jnp
import numpy as np
from jax import lax
from jax.experimental import pallas as pl
from jax.experimental.pallas import tpu as pltpu
from jax.sharding import PartitionSpec as P

KM = 128
KF = 7
UNIT = 16
HALO = 8
LANES = 128
PER_BLOCK = KM // UNIT


EPSILON = 1e-06

bf16 = jnp.bfloat16
f32 = jnp.float32


def split_bf16(matrix):
    high = matrix.astype(bf16)
    low = (matrix - high.astype(np.float64)).astype(bf16)
    return high, low


def transform_matrices():
    angle = 2.0 * np.pi * (np.arange(KM) + 0.5)[:, None] / (2 * KM)
    ahead = np.arange(KM)[None, :] * angle
    analysis = np.concatenate([np.cos(ahead), -np.sin(ahead)], axis=0)
    high, low = split_bf16(analysis)
    analysis_pair = np.concatenate([high, low], axis=1)

    def synthesis(first):
        turn = (first + np.arange(KM))[:, None] * angle.T
        matrix = np.concatenate([np.cos(turn), -np.sin(turn)], axis=1) / KM
        high, low = split_bf16(matrix)
        return np.concatenate([high, low], axis=0)

    return analysis_pair, synthesis(KM), synthesis(0)


def record_layout(record_blocks, tail_rows, block_count):
    starts = jnp.cumsum(record_blocks) - record_blocks
    record_ends = starts + record_blocks - 1
    block_ids = jnp.arange(block_count, dtype=jnp.int32)
    starts_here = jnp.any(starts[None, :] == block_ids[:, None], axis=1)
    starts_next = jnp.any(starts[None, :] == block_ids[:, None] + 1, axis=1)
    starts_next = starts_next | (block_ids == block_count - 1)
    closing = record_ends[None, :] == block_ids[:, None]
    filled_rows = jnp.where(
        jnp.any(closing, axis=1), jnp.sum(jnp.where(closing, tail_rows[None, :], 0), axis=1), KM
    )
    carry_on = 1 - starts_here.astype(jnp.int32)
    carry_next = 1 - starts_next.astype(jnp.int32)
    return jnp.stack([carry_on, carry_next, filled_rows.astype(jnp.int32)])


def analyse(analysis_ref, block):
    twice = jnp.concatenate([block, block], axis=0)
    return jnp.dot(analysis_ref[...], twice, preferred_element_type=f32)


def synthesise(synthesis_ref, real, imag):
    spectrum = jnp.concatenate([real, imag], axis=0)
    high = spectrum.astype(bf16)
    low = (spectrum - high.astype(f32)).astype(bf16)
    both = jnp.dot(synthesis_ref[...], high, preferred_element_type=f32)
    rest = jnp.dot(synthesis_ref[0:KM, :], low, preferred_element_type=f32)
    return both[:KM] + (both[KM:] + rest)


def alternate(shape):
    rows = lax.broadcasted_iota(jnp.int32, shape, 0)
    return (1 - 2 * (rows & 1)).astype(f32)


def fetch_block(source_ref, extended_ref, unit_ref, layout_ref, block):
    for unit in range(PER_BLOCK):
        first = pl.multiple_of(unit_ref[block * PER_BLOCK + unit] * UNIT, UNIT)
        extended_ref[HALO + unit * UNIT : HALO + (unit + 1) * UNIT, :] = source_ref[
            pl.ds(first, UNIT), :
        ].astype(f32)
    before = jnp.maximum(block * PER_BLOCK - 1, 0)
    first = pl.multiple_of(unit_ref[before] * UNIT, UNIT)
    rim = source_ref[pl.ds(first, UNIT), :].astype(f32)[UNIT - HALO :]
    extended_ref[0:HALO, :] = jnp.where(layout_ref[0, block] > 0, rim, 0.0)


def store_units(target_ref, unit_ref, block, rows):
    for unit in range(PER_BLOCK):
        first = pl.multiple_of(unit_ref[block * PER_BLOCK + unit] * UNIT, UNIT)
        target_ref[pl.ds(first, UNIT), :] = rows[unit * UNIT : (unit + 1) * UNIT]


def featurize(extended_ref, taps_ref, stream, filled):
    total = None
    for lag in range(KF):
        tap = taps_ref[3 * lag + stream : 3 * lag + stream + 1, :]
        term = tap * extended_ref[HALO - lag : HALO - lag + KM, :]
        total = term if total is None else total + term
    rows = lax.broadcasted_iota(jnp.int32, total.shape, 0)
    return jnp.where(rows < filled, total, 0.0).astype(bf16)


def spread(ahead_ref, taps_ref, stream):
    total = None
    for lag in range(KF):
        tap = taps_ref[3 * lag + stream : 3 * lag + stream + 1, :]
        term = tap * ahead_ref[lag : lag + KM, :]
        total = term if total is None else total + term
    return total.astype(bf16)


def fold(rows):
    return jnp.sum(rows.reshape(-1, 8, rows.shape[1]), axis=0)


def add_tap_sums(sums_ref, d_float, extended_ref):
    for lag in range(KF):
        window = extended_ref[HALO - lag : HALO - lag + KM, :]
        sums_ref[8 * lag : 8 * (lag + 1), :] += fold(d_float * window)


def set_ahead(ahead_ref, layout_ref, block, d_feature):
    ahead_ref[block + 1, 0:KM, :] = d_feature
    going_on = layout_ref[1, jnp.maximum(block - 1, 0)]
    ahead_ref[block, KM:, :] = jnp.where(going_on > 0, d_feature[:HALO], 0.0)


def repeat(count, per_step, work):
    def step(index, carry):
        for offset in range(per_step):
            work(per_step * index + offset, offset)
        return carry

    lax.fori_loop(0, count // per_step, step, 0)


def block_rows(block):
    return pl.ds(pl.multiple_of(block * KM, KM), KM)


def twice(array):
    return jnp.concatenate([array, array], axis=1)


def respond_kernel(shards, rows, *refs):
    unit_ref, layout_ref = refs[:2]
    pieces = refs[2 : 2 + shards]
    taps_ref, mixer_ref, analysis_ref, synthesis_ref = refs[2 + shards : 6 + shards]
    staged_ref, feature_ref, response_ref, filter_ref = refs[6 + shards : 10 + shards]
    extended_ref, mixed_ref, spectra_ref, sems = refs[10 + shards :]
    width = staged_ref.shape[2]
    pairs = staged_ref.shape[1] // (2 * KM)
    arrivals = [
        pltpu.make_async_copy(
            pieces[slot], staged_ref.at[:, pl.ds(slot * rows, rows)], sems.at[slot]
        )
        for slot in range(shards)
    ]
    for copy in arrivals:
        copy.start()
    filter_ref[...] = analyse(analysis_ref, mixer_ref[...].astype(bf16))
    spectra_ref[0, ...] = jnp.zeros(spectra_ref.shape[1:], f32)
    for copy in arrivals:
        copy.wait()

    def feature_pair(pair, offset):
        mixed = []
        for half in range(2):
            block = 2 * pair + half
            filled = layout_ref[2, block]
            features = []
            for stream in range(2):
                extended = extended_ref.at[2 * half + stream]
                fetch_block(staged_ref.at[stream], extended, unit_ref, layout_ref, block)
                feature = featurize(extended, taps_ref, stream + 1, filled)
                feature_ref[stream, block_rows(block), :] = feature
                features.append(feature.astype(f32))
            mixed.append((features[0] * features[1]).astype(bf16))
        mixed_ref[pair, ...] = jnp.concatenate(mixed, axis=1)

    def analyse_pair(pair, offset):
        spectra_ref[pair + 1, ...] = analyse(analysis_ref, mixed_ref[pair, ...])

    def respond_pair(pair, offset):
        own = spectra_ref[pair + 1, ...]
        first_on = (layout_ref[0, 2 * pair] > 0).astype(f32)
        second_on = (layout_ref[0, 2 * pair + 1] > 0).astype(f32)
        earlier = jnp.concatenate(
            [spectra_ref[pair, :, width:] * first_on, own[:, :width] * second_on], axis=1
        )
        sign = alternate((KM, 2 * width))
        real = earlier[:KM] + sign * own[KM:]
        imag = earlier[KM:] - sign * own[:KM]
        filter_real, filter_imag = twice(filter_ref[0:KM, :]), twice(filter_ref[KM:, :])
        response = synthesise(
            synthesis_ref,
            real * filter_real - imag * filter_imag,
            real * filter_imag + imag * filter_real,
        )
        response_ref[block_rows(2 * pair), :] = response[:, :width]
        response_ref[block_rows(2 * pair + 1), :] = response[:, width:]

    repeat(pairs, 1, feature_pair)
    repeat(pairs, 2, analyse_pair)
    repeat(pairs, 2, respond_pair)


def gate_kernel(shards, rows, *refs):
    unit_ref, layout_ref = refs[:2]
    pieces = refs[2 : 2 + shards]
    (
        response_ref, taps_ref, gain_ref, staged_ref, feature_ref, gated_ref, squares_ref,
        extended_ref, sems,
    ) = refs[2 + shards :]
    width = staged_ref.shape[1]
    blocks = staged_ref.shape[0] // KM
    arrivals = [
        pltpu.make_async_copy(piece, staged_ref.at[pl.ds(slot * rows, rows)], sems.at[slot])
        for slot, piece in enumerate(pieces)
    ]
    for copy in arrivals:
        copy.start()
    terms = [term.astype(f32) for term in bf16_terms(gain_ref[...], 3)]
    rest = jnp.zeros((UNIT - 3, width), f32)
    gain_rows = jnp.concatenate(terms + [rest], axis=0).astype(bf16)
    for shard in range(shards):
        gated_ref[shard, rows:, :] = gain_rows
    for copy in arrivals:
        copy.wait()

    def gate_block(block, offset):
        extended = extended_ref.at[offset]
        fetch_block(staged_ref, extended, unit_ref, layout_ref, block)
        feature = featurize(extended, taps_ref, 0, layout_ref[2, block])
        feature_ref[block_rows(block), :] = feature
        gated = (feature.astype(f32) * response_ref[block_rows(block), :]).astype(bf16)
        set_gated(gated_ref, block, gated)
        gated = gated.astype(f32)
        squares_ref[pl.ds(block, 1), :] = sum_lanes(gated * gated)

    repeat(blocks, 4, gate_block)


def pack_kernel(shards, *refs):
    position_ref, gated_ref = refs[:2]
    leaving, sems = refs[2 : 2 + shards], refs[2 + shards]
    departures = [
        pltpu.make_async_copy(gated_ref.at[position_ref[0] ^ slot], target, sems.at[slot])
        for slot, target in enumerate(leaving)
    ]
    for copy in departures:
        copy.start()
    for copy in departures:
        copy.wait()


def product_kernel(shards, rows, *refs):
    position_ref = refs[0]
    pieces = refs[1 : 1 + shards]
    gated_ref, squares_ref, gain_ref, staged_ref, sums_ref, sems = refs[1 + shards :]
    blocks = squares_ref.shape[0]
    arrivals = []
    for slot in range(shards):
        first = pl.multiple_of((position_ref[0] ^ slot) * rows, rows)
        arrivals.append(
            pltpu.make_async_copy(pieces[slot], staged_ref.at[pl.ds(first, rows)], sems.at[slot])
        )
    for copy in arrivals:
        copy.start()
    sums_ref[0:blocks, :] = squares_ref[...]
    for slot in range(shards):
        shard = position_ref[0] ^ slot
        for step in range(rows // KM):
            here = slice(step * KM, (step + 1) * KM)
            gated = gated_ref[shard, here, :].astype(f32)
            weighted = pieces[slot][here, :].astype(f32) * gain_ref[...]
            block = shard * (rows // KM) + step
            sums_ref[pl.ds(blocks + block, 1), :] = sum_lanes(weighted * gated)
    for copy in arrivals:
        copy.wait()


def gated_place(gated_ref, block):
    per_shard = (gated_ref.shape[1] - UNIT) // KM
    return block // per_shard, block_rows(block % per_shard)


def set_gated(gated_ref, block, gated):
    shard, place = gated_place(gated_ref, block)
    gated_ref[shard, place, :] = gated


def get_gated(gated_ref, block):
    shard, place = gated_place(gated_ref, block)
    return gated_ref[shard, place, :].astype(f32)


def send_slots(source_ref, leaving, rows, sems):
    departures = [
        pltpu.make_async_copy(source_ref.at[pl.ds(slot * rows, rows)], target, sems.at[slot])
        for slot, target in enumerate(leaving)
    ]
    for copy in departures:
        copy.start()
    for copy in departures:
        copy.wait()


def bf16_terms(values, count):
    terms = []
    for _ in range(count):
        terms.append(values.astype(bf16))
        values = values - terms[-1].astype(f32)
    return terms


def sum_lanes(values):
    terms = jnp.concatenate(bf16_terms(values, 2), axis=1)
    ones = jnp.ones((8, terms.shape[1]), bf16)
    return lax.dot_general(
        ones, terms, (((1,), (1,)), ((), ())), preferred_element_type=f32
    )[0:1]


def scale_of(sums_ref, block, filled, total_channels):
    lanes = lax.broadcasted_iota(jnp.int32, (1, KM), 1)
    squares = sums_ref[pl.ds(block, 1), :]
    return jnp.where(lanes < filled, lax.rsqrt(squares / total_channels + EPSILON), 0.0)


def down_rows(row, width):
    return jnp.broadcast_to(row, (width, KM)).T


def norm_kernel(total_channels, shards, rows, *refs):
    (
        unit_ref, layout_ref, cotangent_ref, response_ref, taps_ref, gain_ref, feature_ref,
        gated_ref, sums_ref, d_query_ref, d_response_ref,
    ) = refs[:11]
    leaving = refs[11 : 11 + shards]
    grad_ref, ahead_ref, sems = refs[11 + shards :]
    blocks = cotangent_ref.shape[0] // KM
    width = cotangent_ref.shape[1]
    ahead_ref[blocks, KM:, :] = jnp.zeros((HALO, width), f32)

    def scale_block(block, offset):
        scale_row = scale_of(sums_ref, block, layout_ref[2, block], total_channels)
        products = sums_ref[pl.ds(blocks + block, 1), :]
        inner_row = scale_row * products / total_channels
        scale = down_rows(scale_row, width)
        pull = down_rows(scale_row * scale_row * inner_row, width)
        gated = get_gated(gated_ref, block)
        weighted = cotangent_ref[block_rows(block), :].astype(f32) * gain_ref[...]
        d_gated = (scale * weighted - pull * gated).astype(bf16).astype(f32)
        feature = feature_ref[block_rows(block), :].astype(f32)
        d_response_ref[block_rows(block), :] = (d_gated * feature).astype(bf16)
        d_query = (d_gated * response_ref[block_rows(block), :]).astype(bf16)
        d_query_ref[block_rows(block), :] = d_query
        set_ahead(ahead_ref, layout_ref, block, d_query.astype(f32))

    def spread_block(block, offset):
        spread_rows = spread(ahead_ref.at[block + 1], taps_ref, 0)
        store_units(grad_ref, unit_ref, block, spread_rows)

    scale_block(blocks - 1, 0)
    scale_block(blocks - 2, 1)

    def both(index, offset):
        block = blocks - 3 - index
        scale_block(block, offset)
        spread_block(block + 2, offset)

    repeat(blocks - 2, 2, both)
    spread_block(1, 0)
    spread_block(0, 1)
    send_slots(grad_ref, leaving, rows, sems)


def mix_back_kernel(shards, rows, *refs):
    (
        unit_ref, layout_ref, taps_ref, analysis_ref, synthesis_ref, feature_ref, filter_ref,
        d_response_ref, query_piece_ref, mixer_grad_ref, d_others_ref,
    ) = refs[:11]
    leaving = refs[11 : 11 + shards]
    grad_ref, ahead_ref, spectra_ref, cross_ref, sems = refs[11 + shards :]
    width = feature_ref.shape[2]
    blocks = feature_ref.shape[1] // KM
    pairs = blocks // 2
    query_copy = pltpu.make_async_copy(query_piece_ref, leaving[1].at[0], sems.at[shards])
    query_copy.start()
    cross_ref[...] = jnp.zeros_like(cross_ref)
    spectra_ref[pairs, ...] = jnp.zeros(spectra_ref.shape[1:], f32)
    for stream in range(2):
        ahead_ref[stream, blocks, KM:, :] = jnp.zeros((HALO, width), f32)

    def analyse_pair(pair, offset):
        d_response = jnp.concatenate(
            [d_response_ref[block_rows(2 * pair), :], d_response_ref[block_rows(2 * pair + 1), :]],
            axis=1,
        )
        spectra_ref[pair, ...] = analyse(analysis_ref, d_response)

    def mix_pair(pair, offset):
        own = spectra_ref[pair, ...]
        first_on = (layout_ref[1, 2 * pair] > 0).astype(f32)
        second_on = (layout_ref[1, 2 * pair + 1] > 0).astype(f32)
        later = jnp.concatenate(
            [own[:, width:] * first_on, spectra_ref[pair + 1, :, :width] * second_on], axis=1
        )
        sign = alternate((KM, 2 * width))
        real = own[:KM] + sign * later[KM:]
        imag = own[KM:] - sign * later[:KM]
        mixed = []
        for block in (2 * pair, 2 * pair + 1):
            key_feature = feature_ref[0, block_rows(block), :].astype(f32)
            value_feature = feature_ref[1, block_rows(block), :].astype(f32)
            mixed.append((key_feature * value_feature).astype(bf16))
        source = analyse(analysis_ref, jnp.concatenate(mixed, axis=1))
        cross_real = real * source[:KM] + imag * source[KM:]
        cross_imag = imag * source[:KM] - real * source[KM:]
        cross_ref[0:KM, :] += cross_real[:, :width] + cross_real[:, width:]
        cross_ref[KM:, :] += cross_imag[:, :width] + cross_imag[:, width:]
        filter_real, filter_imag = twice(filter_ref[0:KM, :]), twice(filter_ref[KM:, :])
        d_mixed = synthesise(
            synthesis_ref,
            real * filter_real + imag * filter_imag,
            imag * filter_real - real * filter_imag,
        )
        for half in range(2):
            block = 2 * pair + half
            d_mixed_block = d_mixed[:, half * width : (half + 1) * width]
            for stream in (1, 2):
                factor = feature_ref[2 - stream, block_rows(block), :].astype(f32)
                d_feature = (d_mixed_block * factor).astype(bf16)
                d_others_ref[stream - 1, block_rows(block), :] = d_feature
                set_ahead(ahead_ref.at[stream - 1], layout_ref, block, d_feature.astype(f32))

    def spread_block(block, offset):
        for stream in (1, 2):
            spread_rows = spread(ahead_ref.at[stream - 1, block + 1], taps_ref, stream)
            store_units(grad_ref.at[stream - 1], unit_ref, block, spread_rows)

    repeat(pairs, 2, analyse_pair)
    repeat(pairs, 2, mix_pair)
    repeat(blocks, 1, spread_block)
    departures = [
        pltpu.make_async_copy(
            grad_ref.at[:, pl.ds(slot * rows, rows)],
            target.at[1:3] if slot == 1 else target,
            sems.at[slot],
        )
        for slot, target in enumerate(leaving)
    ]
    for copy in departures:
        copy.start()
    mixer_grad_ref[...] = synthesise(synthesis_ref, cross_ref[0:KM, :], cross_ref[KM:, :])
    for copy in departures + [query_copy]:
        copy.wait()


def tap_grad_kernel(
    total_channels,
    unit_ref, layout_ref, query_ref, others_ref, d_query_ref, d_others_ref, gated_ref,
    cotangent_ref, sums_ref, taps_grad_ref, gain_grad_ref, extended_ref, tap_sums_ref,
    gain_sums_ref,
):
    blocks = cotangent_ref.shape[0] // KM
    width = cotangent_ref.shape[1]
    tap_sums_ref[...] = jnp.zeros_like(tap_sums_ref)
    gain_sums_ref[...] = jnp.zeros_like(gain_sums_ref)

    def block_step(block, carry):
        scale_row = scale_of(sums_ref, block, layout_ref[2, block], total_channels)
        scale = down_rows(scale_row, width)
        normed = get_gated(gated_ref, block) * scale
        cotangent = cotangent_ref[block_rows(block), :].astype(f32)
        gain_sums_ref[...] += fold(cotangent * normed)
        for stream in range(3):
            extended = extended_ref.at[stream]
            if stream == 0:
                source_ref = query_ref
                d_feature = d_query_ref[block_rows(block), :]
            else:
                source_ref = others_ref.at[stream - 1]
                d_feature = d_others_ref[stream - 1, block_rows(block), :]
            fetch_block(source_ref, extended, unit_ref, layout_ref, block)
            add_tap_sums(tap_sums_ref.at[stream], d_feature.astype(f32), extended)
        return carry

    lax.fori_loop(0, blocks, block_step, 0)
    gain_grad_ref[...] = jnp.sum(gain_sums_ref[...], axis=0, keepdims=True)
    for stream in range(3):
        for lag in range(KF):
            taps_grad_ref[3 * lag + stream : 3 * lag + stream + 1, :] = jnp.sum(
                tap_sums_ref[stream, 8 * lag : 8 * (lag + 1), :], axis=0, keepdims=True
            )


def scale_out_kernel(total_channels, shards, rows, *refs):
    layout_ref, position_ref, sums_ref = refs[:3]
    pieces = refs[3 : 3 + shards]
    out_ref, scaled_ref, sems = refs[3 + shards :]
    narrow = pieces[0].shape[1]

    def scale_block(step, offset):
        block = position_ref[0] * (rows // KM) + step
        scale_row = scale_of(sums_ref, block, layout_ref[2, block], total_channels)
        scale = down_rows(scale_row, narrow)
        for slot, piece in enumerate(pieces):
            terms = piece[rows : rows + UNIT, :].astype(f32)
            gain = terms[0:1] + terms[1:2] + terms[2:3]
            normed = piece[block_rows(step), :].astype(f32) * scale
            scaled_ref[slot, block_rows(step), :] = (normed * gain).astype(bf16)

    repeat(rows // KM, 1, scale_block)
    copies = []
    for slot in range(shards):
        if len(out_ref.shape) == 2:
            target = out_ref.at[:, lane_place(position_ref[0], slot, narrow)]
        else:
            target = out_ref.at[position_ref[0] ^ slot]
        copies.append(pltpu.make_async_copy(scaled_ref.at[slot], target, sems.at[slot]))
    for copy in copies:
        copy.start()
    for copy in copies:
        copy.wait()


def lane_place(position, slot, width):
    return pl.ds(pl.multiple_of((position ^ slot) * width, width), width)


def assemble_grad_kernel(shards, width, position_ref, *refs):
    queries, others, target, sems = refs[: shards - 1], refs[shards - 1 : -2], refs[-2], refs[-1]
    copies = []
    for slot in range(shards):
        lanes = lane_place(position_ref[0], slot, width)
        first = 0 if slot == 1 else 1
        copies.append((others[slot], target.at[first:3, :, lanes]))
        if slot != 1:
            copies.append((queries[min(slot, 1) + max(slot - 2, 0)], target.at[0, :, lanes]))
    copies = [
        pltpu.make_async_copy(source, view, sems.at[i]) for i, (source, view) in enumerate(copies)
    ]
    for copy in copies:
        copy.start()
    for copy in copies:
        copy.wait()


NEAR = pltpu.VMEM
FAR = pl.ANY


def run_kernel(kernel, scalars, arrays, outs, scratch, microseconds, name, sems=0):
    in_specs = [pl.BlockSpec(memory_space=pltpu.SMEM)] * len(scalars)
    operands = list(scalars)
    for array, space in arrays:
        operands.append(array)
        in_specs.append(pl.BlockSpec(memory_space=space))
    scratch_shapes = [pltpu.VMEM(s, d) for s, d in scratch]
    memory = 8 * 1024 * 1024 + sum(
        int(np.prod(s)) * jnp.dtype(d).itemsize for s, d in scratch
    )
    if sems:
        scratch_shapes.append(pltpu.SemaphoreType.DMA((sems,)))
    return pl.pallas_call(
        kernel,
        out_shape=[jax.ShapeDtypeStruct(s, d) for s, d, _ in outs],
        in_specs=in_specs,
        out_specs=[pl.BlockSpec(memory_space=space) for _, _, space in outs],
        scratch_shapes=scratch_shapes,
        compiler_params=pltpu.CompilerParams(vmem_limit_bytes=memory),
        cost_estimate=pl.CostEstimate(
            flops=int(microseconds * 1e9), bytes_accessed=0, transcendentals=0
        ),
        name=name,
    )(*operands)


def exchange(array, axis, bits):
    return lax.ppermute(array, axis, [(i, i ^ bits) for i in range(lax.axis_size(axis))])


def butterfly(sums, axis, radix):
    step = 1
    while step < lax.axis_size(axis):
        radix = min(radix, lax.axis_size(axis) // step)
        others = [exchange(sums, axis, step * k) for k in range(1, radix)]
        for other in others:
            sums = sums + other
        step *= radix
    return sums


def body(
    streams, record_blocks, tail_rows, unit_dest, mixer_filter, feat_filter, norm_gain, out_grad
):
    rows = streams.shape[1]
    channels = streams.shape[2]
    shards = lax.axis_size("seq")
    position = lax.axis_index("seq")
    total_channels = channels * lax.axis_size("fsdp")
    tokens = rows * shards
    blocks = tokens // KM
    units = tokens // UNIT
    units_dev = rows // UNIT
    narrow = channels // shards
    width = -(-narrow // LANES) * LANES

    def widen(array):
        if width == narrow:
            return array
        return jnp.pad(array, ((0, 0),) * (array.ndim - 1) + ((0, width - narrow),))

    def lane_parts(array, start=(), counts=()):
        starts = start + (0,) * (array.ndim - 1 - len(start))
        sizes = counts + array.shape[len(counts) : -1] + (narrow,)
        return [
            lax.dynamic_slice(array, starts + ((position ^ slot) * narrow,), sizes)
            for slot in range(shards)
        ]

    def exchange_parts(parts):
        return [
            widen(exchange(part, "seq", slot) if slot else part)
            for slot, part in enumerate(parts)
        ]

    def to_tokens(pieces, slots):
        return [
            exchange(part[..., :narrow], "seq", slot) if slot else part[..., :narrow]
            for slot, part in zip(slots, pieces)
        ]

    every_slot = range(shards)

    position_word = position.astype(jnp.int32).reshape(1)
    layout = record_layout(record_blocks, tail_rows, blocks)
    unit_ids = jnp.arange(units, dtype=jnp.int32)
    loaded_unit = jnp.sum(
        jnp.where(unit_dest[None, :] == unit_ids[:, None], unit_ids[None, :], 0), axis=1
    ).astype(jnp.int32)
    slot = position ^ (loaded_unit // units_dev)
    unit_table = slot * units_dev + loaded_unit % units_dev
    analysis, synthesis_on, synthesis_back = (jnp.asarray(m) for m in transform_matrices())
    taps = widen(feat_filter.reshape(3 * KF, narrow))
    own_gain = norm_gain.reshape(1, narrow)
    gain = widen(own_gain)
    mixer = widen(mixer_filter)

    others = exchange_parts(lane_parts(streams, (1,), (2,)))
    query_parts = [part[0] for part in lane_parts(streams, (0,), (1,))]
    others[1], query_parts = lax.optimization_barrier((others[1], query_parts))
    queries = exchange_parts(query_parts)
    grad_parts = lane_parts(out_grad)
    queries[1], grad_parts = lax.optimization_barrier((queries[1], grad_parts))
    cotangents = exchange_parts(grad_parts)

    whole = (tokens, width)
    spectra = ((blocks // 2 + 1, 2 * KM, 2 * width), f32)
    extended_shape = (KM + HALO, width)
    scalars = (unit_table, layout)
    staged, features, response, filter_spectrum = run_kernel(
        lambda *refs: respond_kernel(shards, rows, *refs),
        scalars,
        [(part, FAR) for part in others]
        + [(a, NEAR) for a in (taps, mixer, analysis, synthesis_on)],
        (
            ((2,) + whole, bf16, NEAR), ((2,) + whole, bf16, NEAR), (whole, f32, NEAR),
            ((2 * KM, width), f32, NEAR),
        ),
        (((4,) + extended_shape, f32), ((blocks // 2, KM, 2 * width), bf16), spectra),
        6,
        "respond",
        sems=shards,
    )
    staged_query, query_feature, gated, squares = run_kernel(
        lambda *refs: gate_kernel(shards, rows, *refs),
        scalars,
        [(part, FAR) for part in queries] + [(a, NEAR) for a in (response, taps, gain)],
        (
            (whole, bf16, NEAR), (whole, bf16, NEAR),
            ((shards, rows + UNIT, width), bf16, NEAR), ((blocks, KM), f32, NEAR),
        ),
        (((4,) + extended_shape, f32),),
        0.5,
        "gate",
        sems=shards,
    )
    cotangent, sums = run_kernel(
        lambda *refs: product_kernel(shards, rows, *refs),
        (position_word,),
        [(part, NEAR) for part in cotangents] + [(a, NEAR) for a in (gated, squares, gain)],
        ((whole, bf16, NEAR), ((2 * blocks, KM), f32, NEAR)),
        (),
        2,
        "product",
        sems=shards,
    )
    sums, ready_gated = lax.optimization_barrier((sums, gated))
    gated_pieces = run_kernel(
        lambda *refs: pack_kernel(shards, *refs),
        (position_word,),
        [(ready_gated, NEAR)],
        (((rows + UNIT, width), bf16, FAR),) * shards,
        (),
        1,
        "pack",
        sems=shards,
    )
    sums = butterfly(sums, "seq", 4)
    gated_far = to_tokens(gated_pieces[2:], every_slot[2:])
    sums = butterfly(sums, "fsdp", 2)
    norm = run_kernel(
        lambda *refs: norm_kernel(total_channels, shards, rows, *refs),
        scalars,
        [(a, NEAR) for a in (cotangent, response, taps, gain, query_feature, gated, sums)],
        ((whole, bf16, NEAR),) * 2 + (((rows, width), bf16, FAR),) * shards,
        ((whole, bf16), ((blocks + 1,) + extended_shape, f32)),
        0.2,
        "norm",
        sems=shards,
    )
    norm = list(norm)
    first_piece = norm[4]
    norm, gated_far, near_piece = lax.optimization_barrier((norm, gated_far, gated_pieces[1]))
    norm[4] = first_piece
    d_query, d_response = norm[:2]
    gated_back = to_tokens([gated_pieces[0], near_piece], [0, 1]) + gated_far
    query_back = to_tokens(norm[2:3] + norm[4:], [slot for slot in every_slot if slot != 1])
    back = run_kernel(
        lambda *refs: mix_back_kernel(shards, rows, *refs),
        scalars,
        [
            (a, NEAR)
            for a in (
                taps, analysis, synthesis_back, features, filter_spectrum, d_response
            )
        ]
        + [(norm[3], FAR)],
        (((KM, width), f32, NEAR), ((2,) + whole, bf16, NEAR))
        + tuple(((3 if slot == 1 else 2, rows, width), bf16, FAR) for slot in every_slot),
        (
            ((2,) + whole, bf16), ((2, blocks + 1) + extended_shape, f32), spectra,
            ((2 * KM, width), f32),
        ),
        7,
        "mix_back",
        sems=shards + 1,
    )
    mixer_grad, d_others, *back_pieces = back
    gated_back[1], back_pieces[1] = lax.optimization_barrier((gated_back[1], back_pieces[1]))
    others_back = to_tokens(back_pieces, every_slot)
    taps_grad, gain_grad = run_kernel(
        lambda *refs: tap_grad_kernel(total_channels, *refs),
        scalars,
        [
            (a, NEAR)
            for a in (staged_query, staged, d_query, d_others, gated, cotangent, sums)
        ],
        (((3 * KF, width), f32, NEAR), ((1, width), f32, NEAR)),
        (((3,) + extended_shape, f32), ((3, 8 * KF, width), f32), ((8, width), f32)),
        4,
        "tap_grad",
    )
    aligned = width == narrow
    (out,) = run_kernel(
        lambda *refs: scale_out_kernel(total_channels, shards, rows, *refs),
        (layout, position_word),
        [(sums, NEAR)] + [(a, NEAR) for a in gated_back],
        (((rows, channels) if aligned else (shards, rows, narrow), bf16, FAR),),
        (((shards, rows, narrow), bf16),),
        2,
        "scale_out",
        sems=shards,
    )
    if aligned:
        (stream_grad,) = run_kernel(
            lambda *refs: assemble_grad_kernel(shards, width, *refs),
            (position_word,),
            [(a, NEAR) for a in query_back] + [(a, NEAR) for a in others_back],
            (((3, rows, channels), bf16, FAR),),
            (),
            1,
            "assemble_grad",
            sems=2 * shards,
        )
    else:
        def assemble(pieces):
            stacked = jnp.stack(pieces)
            in_place = jnp.take(stacked, position ^ jnp.arange(shards), axis=0)
            return jnp.moveaxis(in_place, 0, -2).reshape(pieces[0].shape[:-1] + (channels,))

        out = out.transpose(1, 0, 2).reshape(rows, channels)
        queries = query_back[:1] + [others_back[1][0]] + query_back[1:]
        others_back[1] = others_back[1][1:]
        stream_grad = jnp.concatenate([assemble(queries)[None], assemble(others_back)])
    feat_grad = taps_grad[:, :narrow].reshape(KF, 3, narrow)
    return (out, stream_grad, mixer_grad[:, :narrow], feat_grad, gain_grad[0, :narrow])


def solution(mesh):
    placed = (
        P(None, "seq", "fsdp"),
        P(),
        P(),
        P(),
        P(None, ("fsdp", "seq")),
        P(None, None, ("fsdp", "seq")),
        P(("fsdp", "seq")),
        P("seq", "fsdp"),
    )
    return jax.shard_map(
        body,
        mesh=mesh,
        in_specs=placed,
        out_specs=(
            P("seq", "fsdp"),
            P(None, "seq", "fsdp"),
            P(None, ("fsdp", "seq")),
            P(None, None, ("fsdp", "seq")),
            P(("fsdp", "seq")),
        ),
        check_vma=False,
    )
```

```python
import jax
import jax.numpy as jnp
import numpy as np
from jax import lax
from jax.experimental import pallas as pl
from jax.experimental.pallas import tpu as pltpu
from jax.sharding import PartitionSpec as P

KM = 128
KF = 7
UNIT = 16
HALO = 8
LANES = 128
PER_BLOCK = KM // UNIT


EPSILON = 1e-06

bf16 = jnp.bfloat16
f32 = jnp.float32


def split_bf16(matrix):
    high = matrix.astype(bf16)
    low = (matrix - high.astype(np.float64)).astype(bf16)
    return high, low


def transform_matrices():
    angle = 2.0 * np.pi * (np.arange(KM) + 0.5)[:, None] / (2 * KM)
    ahead = np.arange(KM)[None, :] * angle
    analysis = np.concatenate([np.cos(ahead), -np.sin(ahead)], axis=0)
    high, low = split_bf16(analysis)
    analysis_pair = np.concatenate([high, low], axis=1)

    def synthesis(first):
        turn = (first + np.arange(KM))[:, None] * angle.T
        matrix = np.concatenate([np.cos(turn), -np.sin(turn)], axis=1) / KM
        high, low = split_bf16(matrix)
        return np.concatenate([high, low], axis=0)

    return analysis_pair, synthesis(KM), synthesis(0)


def record_layout(record_blocks, tail_rows, block_count):
    starts = jnp.cumsum(record_blocks) - record_blocks
    record_ends = starts + record_blocks - 1
    block_ids = jnp.arange(block_count, dtype=jnp.int32)
    starts_here = jnp.any(starts[None, :] == block_ids[:, None], axis=1)
    starts_next = jnp.any(starts[None, :] == block_ids[:, None] + 1, axis=1)
    starts_next = starts_next | (block_ids == block_count - 1)
    closing = record_ends[None, :] == block_ids[:, None]
    filled_rows = jnp.where(
        jnp.any(closing, axis=1), jnp.sum(jnp.where(closing, tail_rows[None, :], 0), axis=1), KM
    )
    carry_on = 1 - starts_here.astype(jnp.int32)
    carry_next = 1 - starts_next.astype(jnp.int32)
    return jnp.stack([carry_on, carry_next, filled_rows.astype(jnp.int32)])


def analyse(analysis_ref, block):
    twice = jnp.concatenate([block, block], axis=0)
    return jnp.dot(analysis_ref[...], twice, preferred_element_type=f32)


def synthesise(synthesis_ref, real, imag):
    spectrum = jnp.concatenate([real, imag], axis=0)
    high = spectrum.astype(bf16)
    low = (spectrum - high.astype(f32)).astype(bf16)
    both = jnp.dot(synthesis_ref[...], high, preferred_element_type=f32)
    rest = jnp.dot(synthesis_ref[0:KM, :], low, preferred_element_type=f32)
    return both[:KM] + (both[KM:] + rest)


def alternate(shape):
    rows = lax.broadcasted_iota(jnp.int32, shape, 0)
    return (1 - 2 * (rows & 1)).astype(f32)


def fetch_block(source_ref, extended_ref, unit_ref, layout_ref, block):
    for unit in range(PER_BLOCK):
        first = pl.multiple_of(unit_ref[block * PER_BLOCK + unit] * UNIT, UNIT)
        extended_ref[HALO + unit * UNIT : HALO + (unit + 1) * UNIT, :] = source_ref[
            pl.ds(first, UNIT), :
        ].astype(f32)
    before = jnp.maximum(block * PER_BLOCK - 1, 0)
    first = pl.multiple_of(unit_ref[before] * UNIT, UNIT)
    rim = source_ref[pl.ds(first, UNIT), :].astype(f32)[UNIT - HALO :]
    extended_ref[0:HALO, :] = jnp.where(layout_ref[0, block] > 0, rim, 0.0)


def store_units(target_ref, unit_ref, block, rows):
    for unit in range(PER_BLOCK):
        first = pl.multiple_of(unit_ref[block * PER_BLOCK + unit] * UNIT, UNIT)
        target_ref[pl.ds(first, UNIT), :] = rows[unit * UNIT : (unit + 1) * UNIT]


def featurize(extended_ref, taps_ref, stream, filled):
    total = None
    for lag in range(KF):
        tap = taps_ref[3 * lag + stream : 3 * lag + stream + 1, :]
        term = tap * extended_ref[HALO - lag : HALO - lag + KM, :]
        total = term if total is None else total + term
    rows = lax.broadcasted_iota(jnp.int32, total.shape, 0)
    return jnp.where(rows < filled, total, 0.0).astype(bf16)


def spread(ahead_ref, taps_ref, stream):
    total = None
    for lag in range(KF):
        tap = taps_ref[3 * lag + stream : 3 * lag + stream + 1, :]
        term = tap * ahead_ref[lag : lag + KM, :]
        total = term if total is None else total + term
    return total.astype(bf16)


def fold(rows):
    return jnp.sum(rows.reshape(-1, 8, rows.shape[1]), axis=0)


def add_tap_sums(sums_ref, d_float, extended_ref):
    for lag in range(KF):
        window = extended_ref[HALO - lag : HALO - lag + KM, :]
        sums_ref[8 * lag : 8 * (lag + 1), :] += fold(d_float * window)


def set_ahead(ahead_ref, layout_ref, block, d_feature):
    ahead_ref[block + 1, 0:KM, :] = d_feature
    going_on = layout_ref[1, jnp.maximum(block - 1, 0)]
    ahead_ref[block, KM:, :] = jnp.where(going_on > 0, d_feature[:HALO], 0.0)


def repeat(count, per_step, work):
    def step(index, carry):
        for offset in range(per_step):
            work(per_step * index + offset, offset)
        return carry

    lax.fori_loop(0, count // per_step, step, 0)


def block_rows(block):
    return pl.ds(pl.multiple_of(block * KM, KM), KM)


def twice(array):
    return jnp.concatenate([array, array], axis=1)


def respond_kernel(shards, rows, *refs):
    unit_ref, layout_ref = refs[:2]
    pieces = refs[2 : 2 + shards]
    taps_ref, mixer_ref, analysis_ref, synthesis_ref = refs[2 + shards : 6 + shards]
    staged_ref, feature_ref, response_ref, filter_ref = refs[6 + shards : 10 + shards]
    extended_ref, mixed_ref, spectra_ref, sems = refs[10 + shards :]
    width = staged_ref.shape[2]
    pairs = staged_ref.shape[1] // (2 * KM)
    arrivals = [
        pltpu.make_async_copy(
            pieces[slot], staged_ref.at[:, pl.ds(slot * rows, rows)], sems.at[slot]
        )
        for slot in range(shards)
    ]
    for copy in arrivals:
        copy.start()
    filter_ref[...] = analyse(analysis_ref, mixer_ref[...].astype(bf16))
    spectra_ref[0, ...] = jnp.zeros(spectra_ref.shape[1:], f32)
    for copy in arrivals:
        copy.wait()

    def feature_pair(pair, offset):
        mixed = []
        for half in range(2):
            block = 2 * pair + half
            filled = layout_ref[2, block]
            features = []
            for stream in range(2):
                extended = extended_ref.at[2 * half + stream]
                fetch_block(staged_ref.at[stream], extended, unit_ref, layout_ref, block)
                feature = featurize(extended, taps_ref, stream + 1, filled)
                feature_ref[stream, block_rows(block), :] = feature
                features.append(feature.astype(f32))
            mixed.append((features[0] * features[1]).astype(bf16))
        mixed_ref[pair, ...] = jnp.concatenate(mixed, axis=1)

    def analyse_pair(pair, offset):
        spectra_ref[pair + 1, ...] = analyse(analysis_ref, mixed_ref[pair, ...])

    def respond_pair(pair, offset):
        own = spectra_ref[pair + 1, ...]
        first_on = (layout_ref[0, 2 * pair] > 0).astype(f32)
        second_on = (layout_ref[0, 2 * pair + 1] > 0).astype(f32)
        earlier = jnp.concatenate(
            [spectra_ref[pair, :, width:] * first_on, own[:, :width] * second_on], axis=1
        )
        sign = alternate((KM, 2 * width))
        real = earlier[:KM] + sign * own[KM:]
        imag = earlier[KM:] - sign * own[:KM]
        filter_real, filter_imag = twice(filter_ref[0:KM, :]), twice(filter_ref[KM:, :])
        response = synthesise(
            synthesis_ref,
            real * filter_real - imag * filter_imag,
            real * filter_imag + imag * filter_real,
        )
        response_ref[block_rows(2 * pair), :] = response[:, :width]
        response_ref[block_rows(2 * pair + 1), :] = response[:, width:]

    repeat(pairs, 1, feature_pair)
    repeat(pairs, 2, analyse_pair)
    repeat(pairs, 2, respond_pair)


def gate_kernel(shards, rows, *refs):
    unit_ref, layout_ref = refs[:2]
    pieces = refs[2 : 2 + shards]
    (
        response_ref, taps_ref, gain_ref, staged_ref, feature_ref, gated_ref, squares_ref,
        extended_ref, sems,
    ) = refs[2 + shards :]
    width = staged_ref.shape[1]
    blocks = staged_ref.shape[0] // KM
    arrivals = [
        pltpu.make_async_copy(piece, staged_ref.at[pl.ds(slot * rows, rows)], sems.at[slot])
        for slot, piece in enumerate(pieces)
    ]
    for copy in arrivals:
        copy.start()
    terms = [term.astype(f32) for term in bf16_terms(gain_ref[...], 3)]
    rest = jnp.zeros((UNIT - 3, width), f32)
    gain_rows = jnp.concatenate(terms + [rest], axis=0).astype(bf16)
    for shard in range(shards):
        gated_ref[shard, rows:, :] = gain_rows
    for copy in arrivals:
        copy.wait()

    def gate_block(block, offset):
        extended = extended_ref.at[offset]
        fetch_block(staged_ref, extended, unit_ref, layout_ref, block)
        feature = featurize(extended, taps_ref, 0, layout_ref[2, block])
        feature_ref[block_rows(block), :] = feature
        gated = (feature.astype(f32) * response_ref[block_rows(block), :]).astype(bf16)
        set_gated(gated_ref, block, gated)
        gated = gated.astype(f32)
        squares_ref[pl.ds(block, 1), :] = sum_lanes(gated * gated)

    repeat(blocks, 4, gate_block)


def pack_kernel(shards, *refs):
    position_ref, gated_ref = refs[:2]
    leaving, sems = refs[2 : 2 + shards], refs[2 + shards]
    departures = [
        pltpu.make_async_copy(gated_ref.at[position_ref[0] ^ slot], target, sems.at[slot])
        for slot, target in enumerate(leaving)
    ]
    for copy in departures:
        copy.start()
    for copy in departures:
        copy.wait()


def product_kernel(shards, rows, *refs):
    position_ref = refs[0]
    pieces = refs[1 : 1 + shards]
    gated_ref, squares_ref, gain_ref, staged_ref, sums_ref, sems = refs[1 + shards :]
    blocks = squares_ref.shape[0]
    arrivals = []
    for slot in range(shards):
        first = pl.multiple_of((position_ref[0] ^ slot) * rows, rows)
        arrivals.append(
            pltpu.make_async_copy(pieces[slot], staged_ref.at[pl.ds(first, rows)], sems.at[slot])
        )
    for copy in arrivals:
        copy.start()
    sums_ref[0:blocks, :] = squares_ref[...]
    for slot in range(shards):
        shard = position_ref[0] ^ slot
        for step in range(rows // KM):
            here = slice(step * KM, (step + 1) * KM)
            gated = gated_ref[shard, here, :].astype(f32)
            weighted = pieces[slot][here, :].astype(f32) * gain_ref[...]
            block = shard * (rows // KM) + step
            sums_ref[pl.ds(blocks + block, 1), :] = sum_lanes(weighted * gated)
    for copy in arrivals:
        copy.wait()


def gated_place(gated_ref, block):
    per_shard = (gated_ref.shape[1] - UNIT) // KM
    return block // per_shard, block_rows(block % per_shard)


def set_gated(gated_ref, block, gated):
    shard, place = gated_place(gated_ref, block)
    gated_ref[shard, place, :] = gated


def get_gated(gated_ref, block):
    shard, place = gated_place(gated_ref, block)
    return gated_ref[shard, place, :].astype(f32)


def send_slots(source_ref, leaving, rows, sems):
    departures = [
        pltpu.make_async_copy(source_ref.at[pl.ds(slot * rows, rows)], target, sems.at[slot])
        for slot, target in enumerate(leaving)
    ]
    for copy in departures:
        copy.start()
    for copy in departures:
        copy.wait()


def bf16_terms(values, count):
    terms = []
    for _ in range(count):
        terms.append(values.astype(bf16))
        values = values - terms[-1].astype(f32)
    return terms


def sum_lanes(values):
    terms = jnp.concatenate(bf16_terms(values, 2), axis=1)
    ones = jnp.ones((8, terms.shape[1]), bf16)
    return lax.dot_general(
        ones, terms, (((1,), (1,)), ((), ())), preferred_element_type=f32
    )[0:1]


def scale_of(sums_ref, block, filled, total_channels):
    lanes = lax.broadcasted_iota(jnp.int32, (1, KM), 1)
    squares = sums_ref[pl.ds(block, 1), :]
    return jnp.where(lanes < filled, lax.rsqrt(squares / total_channels + EPSILON), 0.0)


def down_rows(row, width):
    return jnp.broadcast_to(row, (width, KM)).T


def norm_kernel(total_channels, shards, rows, *refs):
    (
        unit_ref, layout_ref, cotangent_ref, response_ref, taps_ref, gain_ref, feature_ref,
        gated_ref, sums_ref, d_query_ref, d_response_ref,
    ) = refs[:11]
    leaving = refs[11 : 11 + shards]
    grad_ref, ahead_ref, sems = refs[11 + shards :]
    blocks = cotangent_ref.shape[0] // KM
    width = cotangent_ref.shape[1]
    ahead_ref[blocks, KM:, :] = jnp.zeros((HALO, width), f32)

    def scale_block(block, offset):
        scale_row = scale_of(sums_ref, block, layout_ref[2, block], total_channels)
        products = sums_ref[pl.ds(blocks + block, 1), :]
        inner_row = scale_row * products / total_channels
        scale = down_rows(scale_row, width)
        pull = down_rows(scale_row * scale_row * inner_row, width)
        gated = get_gated(gated_ref, block)
        weighted = cotangent_ref[block_rows(block), :].astype(f32) * gain_ref[...]
        d_gated = (scale * weighted - pull * gated).astype(bf16).astype(f32)
        feature = feature_ref[block_rows(block), :].astype(f32)
        d_response_ref[block_rows(block), :] = (d_gated * feature).astype(bf16)
        d_query = (d_gated * response_ref[block_rows(block), :]).astype(bf16)
        d_query_ref[block_rows(block), :] = d_query
        set_ahead(ahead_ref, layout_ref, block, d_query.astype(f32))

    def spread_block(block, offset):
        spread_rows = spread(ahead_ref.at[block + 1], taps_ref, 0)
        store_units(grad_ref, unit_ref, block, spread_rows)

    for offset in range(4):
        scale_block(blocks - 1 - offset, offset)

    def both(index, offset):
        block = blocks - 5 - index
        scale_block(block, offset)
        spread_block(block + 4, offset)

    repeat(blocks - 4, 4, both)
    for offset in range(4):
        spread_block(3 - offset, offset)
    send_slots(grad_ref, leaving, rows, sems)


def mix_back_kernel(shards, rows, *refs):
    (
        unit_ref, layout_ref, taps_ref, analysis_ref, synthesis_ref, feature_ref, filter_ref,
        d_response_ref, query_piece_ref, mixer_grad_ref, d_others_ref,
    ) = refs[:11]
    leaving = refs[11 : 11 + shards]
    grad_ref, ahead_ref, spectra_ref, cross_ref, sems = refs[11 + shards :]
    width = feature_ref.shape[2]
    blocks = feature_ref.shape[1] // KM
    pairs = blocks // 2
    query_copy = pltpu.make_async_copy(query_piece_ref, leaving[1].at[0], sems.at[shards])
    query_copy.start()
    cross_ref[...] = jnp.zeros_like(cross_ref)
    spectra_ref[pairs, ...] = jnp.zeros(spectra_ref.shape[1:], f32)
    for stream in range(2):
        ahead_ref[stream, blocks, KM:, :] = jnp.zeros((HALO, width), f32)

    def analyse_pair(pair, offset):
        d_response = jnp.concatenate(
            [d_response_ref[block_rows(2 * pair), :], d_response_ref[block_rows(2 * pair + 1), :]],
            axis=1,
        )
        spectra_ref[pair, ...] = analyse(analysis_ref, d_response)

    def mix_pair(pair, offset):
        own = spectra_ref[pair, ...]
        first_on = (layout_ref[1, 2 * pair] > 0).astype(f32)
        second_on = (layout_ref[1, 2 * pair + 1] > 0).astype(f32)
        later = jnp.concatenate(
            [own[:, width:] * first_on, spectra_ref[pair + 1, :, :width] * second_on], axis=1
        )
        sign = alternate((KM, 2 * width))
        real = own[:KM] + sign * later[KM:]
        imag = own[KM:] - sign * later[:KM]
        mixed = []
        for block in (2 * pair, 2 * pair + 1):
            key_feature = feature_ref[0, block_rows(block), :].astype(f32)
            value_feature = feature_ref[1, block_rows(block), :].astype(f32)
            mixed.append((key_feature * value_feature).astype(bf16))
        source = analyse(analysis_ref, jnp.concatenate(mixed, axis=1))
        cross_real = real * source[:KM] + imag * source[KM:]
        cross_imag = imag * source[:KM] - real * source[KM:]
        cross_ref[0:KM, :] += cross_real[:, :width] + cross_real[:, width:]
        cross_ref[KM:, :] += cross_imag[:, :width] + cross_imag[:, width:]
        filter_real, filter_imag = twice(filter_ref[0:KM, :]), twice(filter_ref[KM:, :])
        d_mixed = synthesise(
            synthesis_ref,
            real * filter_real + imag * filter_imag,
            imag * filter_real - real * filter_imag,
        )
        for half in range(2):
            block = 2 * pair + half
            d_mixed_block = d_mixed[:, half * width : (half + 1) * width]
            for stream in (1, 2):
                factor = feature_ref[2 - stream, block_rows(block), :].astype(f32)
                d_feature = (d_mixed_block * factor).astype(bf16)
                d_others_ref[stream - 1, block_rows(block), :] = d_feature
                set_ahead(ahead_ref.at[stream - 1], layout_ref, block, d_feature.astype(f32))

    def spread_block(block, offset):
        for stream in (1, 2):
            spread_rows = spread(ahead_ref.at[stream - 1, block + 1], taps_ref, stream)
            store_units(grad_ref.at[stream - 1], unit_ref, block, spread_rows)

    repeat(pairs, 2, analyse_pair)
    repeat(pairs, 2, mix_pair)
    repeat(blocks, 1, spread_block)
    departures = [
        pltpu.make_async_copy(
            grad_ref.at[:, pl.ds(slot * rows, rows)],
            target.at[1:3] if slot == 1 else target,
            sems.at[slot],
        )
        for slot, target in enumerate(leaving)
    ]
    for copy in departures:
        copy.start()
    mixer_grad_ref[...] = synthesise(synthesis_ref, cross_ref[0:KM, :], cross_ref[KM:, :])
    for copy in departures + [query_copy]:
        copy.wait()


def tap_grad_kernel(
    total_channels,
    unit_ref, layout_ref, query_ref, others_ref, d_query_ref, d_others_ref, gated_ref,
    cotangent_ref, sums_ref, taps_grad_ref, gain_grad_ref, extended_ref, tap_sums_ref,
    gain_sums_ref,
):
    blocks = cotangent_ref.shape[0] // KM
    width = cotangent_ref.shape[1]
    tap_sums_ref[...] = jnp.zeros_like(tap_sums_ref)
    gain_sums_ref[...] = jnp.zeros_like(gain_sums_ref)

    def block_step(block, carry):
        scale_row = scale_of(sums_ref, block, layout_ref[2, block], total_channels)
        scale = down_rows(scale_row, width)
        normed = get_gated(gated_ref, block) * scale
        cotangent = cotangent_ref[block_rows(block), :].astype(f32)
        gain_sums_ref[...] += fold(cotangent * normed)
        for stream in range(3):
            extended = extended_ref.at[stream]
            if stream == 0:
                source_ref = query_ref
                d_feature = d_query_ref[block_rows(block), :]
            else:
                source_ref = others_ref.at[stream - 1]
                d_feature = d_others_ref[stream - 1, block_rows(block), :]
            fetch_block(source_ref, extended, unit_ref, layout_ref, block)
            add_tap_sums(tap_sums_ref.at[stream], d_feature.astype(f32), extended)
        return carry

    lax.fori_loop(0, blocks, block_step, 0)
    gain_grad_ref[...] = jnp.sum(gain_sums_ref[...], axis=0, keepdims=True)
    for stream in range(3):
        for lag in range(KF):
            taps_grad_ref[3 * lag + stream : 3 * lag + stream + 1, :] = jnp.sum(
                tap_sums_ref[stream, 8 * lag : 8 * (lag + 1), :], axis=0, keepdims=True
            )


def scale_out_kernel(total_channels, shards, rows, *refs):
    layout_ref, position_ref, sums_ref = refs[:3]
    pieces = refs[3 : 3 + shards]
    out_ref, scaled_ref, sems = refs[3 + shards :]
    narrow = pieces[0].shape[1]

    def scale_block(step, offset):
        block = position_ref[0] * (rows // KM) + step
        scale_row = scale_of(sums_ref, block, layout_ref[2, block], total_channels)
        scale = down_rows(scale_row, narrow)
        for slot, piece in enumerate(pieces):
            terms = piece[rows : rows + UNIT, :].astype(f32)
            gain = terms[0:1] + terms[1:2] + terms[2:3]
            normed = piece[block_rows(step), :].astype(f32) * scale
            scaled_ref[slot, block_rows(step), :] = (normed * gain).astype(bf16)

    repeat(rows // KM, 1, scale_block)
    copies = []
    for slot in range(shards):
        if len(out_ref.shape) == 2:
            target = out_ref.at[:, lane_place(position_ref[0], slot, narrow)]
        else:
            target = out_ref.at[position_ref[0] ^ slot]
        copies.append(pltpu.make_async_copy(scaled_ref.at[slot], target, sems.at[slot]))
    for copy in copies:
        copy.start()
    for copy in copies:
        copy.wait()


def lane_place(position, slot, width):
    return pl.ds(pl.multiple_of((position ^ slot) * width, width), width)


def assemble_grad_kernel(shards, width, position_ref, *refs):
    queries, others, target, sems = refs[: shards - 1], refs[shards - 1 : -2], refs[-2], refs[-1]
    copies = []
    for slot in range(shards):
        lanes = lane_place(position_ref[0], slot, width)
        first = 0 if slot == 1 else 1
        copies.append((others[slot], target.at[first:3, :, lanes]))
        if slot != 1:
            copies.append((queries[min(slot, 1) + max(slot - 2, 0)], target.at[0, :, lanes]))
    copies = [
        pltpu.make_async_copy(source, view, sems.at[i]) for i, (source, view) in enumerate(copies)
    ]
    for copy in copies:
        copy.start()
    for copy in copies:
        copy.wait()


NEAR = pltpu.VMEM
FAR = pl.ANY


def run_kernel(kernel, scalars, arrays, outs, scratch, microseconds, name, sems=0):
    in_specs = [pl.BlockSpec(memory_space=pltpu.SMEM)] * len(scalars)
    operands = list(scalars)
    for array, space in arrays:
        operands.append(array)
        in_specs.append(pl.BlockSpec(memory_space=space))
    scratch_shapes = [pltpu.VMEM(s, d) for s, d in scratch]
    memory = 8 * 1024 * 1024 + sum(
        int(np.prod(s)) * jnp.dtype(d).itemsize for s, d in scratch
    )
    if sems:
        scratch_shapes.append(pltpu.SemaphoreType.DMA((sems,)))
    return pl.pallas_call(
        kernel,
        out_shape=[jax.ShapeDtypeStruct(s, d) for s, d, _ in outs],
        in_specs=in_specs,
        out_specs=[pl.BlockSpec(memory_space=space) for _, _, space in outs],
        scratch_shapes=scratch_shapes,
        compiler_params=pltpu.CompilerParams(vmem_limit_bytes=memory),
        cost_estimate=pl.CostEstimate(
            flops=int(microseconds * 1e9), bytes_accessed=0, transcendentals=0
        ),
        name=name,
    )(*operands)


def exchange(array, axis, bits):
    return lax.ppermute(array, axis, [(i, i ^ bits) for i in range(lax.axis_size(axis))])


def butterfly(sums, axis, radices):
    length, step, radix = lax.axis_size(axis), 1, radices[0]
    while step < length:
        others = [exchange(sums, axis, step * k) for k in range(1, radix)]
        for other in others:
            sums = sums + other
        step *= radix
        radix = min(radices[1], max(length // step, 1))
    return sums


def body(
    streams, record_blocks, tail_rows, unit_dest, mixer_filter, feat_filter, norm_gain, out_grad
):
    rows = streams.shape[1]
    channels = streams.shape[2]
    shards = lax.axis_size("seq")
    position = lax.axis_index("seq")
    total_channels = channels * lax.axis_size("fsdp")
    tokens = rows * shards
    blocks = tokens // KM
    units = tokens // UNIT
    units_dev = rows // UNIT
    narrow = channels // shards
    width = -(-narrow // LANES) * LANES

    def widen(array):
        if width == narrow:
            return array
        return jnp.pad(array, ((0, 0),) * (array.ndim - 1) + ((0, width - narrow),))

    def lane_parts(array, start=(), counts=()):
        starts = start + (0,) * (array.ndim - 1 - len(start))
        sizes = counts + array.shape[len(counts) : -1] + (narrow,)
        return [
            lax.dynamic_slice(array, starts + ((position ^ slot) * narrow,), sizes)
            for slot in range(shards)
        ]

    def exchange_parts(parts):
        return [
            widen(exchange(part, "seq", slot) if slot else part)
            for slot, part in enumerate(parts)
        ]

    def to_tokens(pieces, slots):
        return [
            exchange(part[..., :narrow], "seq", slot) if slot else part[..., :narrow]
            for slot, part in zip(slots, pieces)
        ]

    every_slot = range(shards)

    position_word = position.astype(jnp.int32).reshape(1)
    layout = record_layout(record_blocks, tail_rows, blocks)
    unit_ids = jnp.arange(units, dtype=jnp.int32)
    loaded_unit = jnp.sum(
        jnp.where(unit_dest[None, :] == unit_ids[:, None], unit_ids[None, :], 0), axis=1
    ).astype(jnp.int32)
    slot = position ^ (loaded_unit // units_dev)
    unit_table = slot * units_dev + loaded_unit % units_dev
    analysis, synthesis_on, synthesis_back = (jnp.asarray(m) for m in transform_matrices())
    taps = widen(feat_filter.reshape(3 * KF, narrow))
    own_gain = norm_gain.reshape(1, narrow)
    gain = widen(own_gain)
    mixer = widen(mixer_filter)

    others = exchange_parts(lane_parts(streams, (1,), (2,)))
    query_parts = [part[0] for part in lane_parts(streams, (0,), (1,))]
    others[1], query_parts = lax.optimization_barrier((others[1], query_parts))
    queries = exchange_parts(query_parts)
    grad_parts = lane_parts(out_grad)
    queries[1], grad_parts = lax.optimization_barrier((queries[1], grad_parts))
    cotangents = exchange_parts(grad_parts)

    whole = (tokens, width)
    spectra = ((blocks // 2 + 1, 2 * KM, 2 * width), f32)
    extended_shape = (KM + HALO, width)
    scalars = (unit_table, layout)
    staged, features, response, filter_spectrum = run_kernel(
        lambda *refs: respond_kernel(shards, rows, *refs),
        scalars,
        [(part, FAR) for part in others]
        + [(a, NEAR) for a in (taps, mixer, analysis, synthesis_on)],
        (
            ((2,) + whole, bf16, NEAR), ((2,) + whole, bf16, NEAR), (whole, f32, NEAR),
            ((2 * KM, width), f32, NEAR),
        ),
        (((4,) + extended_shape, f32), ((blocks // 2, KM, 2 * width), bf16), spectra),
        6,
        "respond",
        sems=shards,
    )
    staged_query, query_feature, gated, squares = run_kernel(
        lambda *refs: gate_kernel(shards, rows, *refs),
        scalars,
        [(part, FAR) for part in queries] + [(a, NEAR) for a in (response, taps, gain)],
        (
            (whole, bf16, NEAR), (whole, bf16, NEAR),
            ((shards, rows + UNIT, width), bf16, NEAR), ((blocks, KM), f32, NEAR),
        ),
        (((4,) + extended_shape, f32),),
        0.5,
        "gate",
        sems=shards,
    )
    cotangent, sums = run_kernel(
        lambda *refs: product_kernel(shards, rows, *refs),
        (position_word,),
        [(part, NEAR) for part in cotangents] + [(a, NEAR) for a in (gated, squares, gain)],
        ((whole, bf16, NEAR), ((2 * blocks, KM), f32, NEAR)),
        (),
        2,
        "product",
        sems=shards,
    )
    sums, ready_gated = lax.optimization_barrier((sums, gated))
    gated_pieces = run_kernel(
        lambda *refs: pack_kernel(shards, *refs),
        (position_word,),
        [(ready_gated, NEAR)],
        (((rows + UNIT, width), bf16, FAR),) * shards,
        (),
        1,
        "pack",
        sems=shards,
    )
    sums = butterfly(sums, "seq", (4, 4))
    gated_far = to_tokens(gated_pieces[2:], every_slot[2:])
    sums = butterfly(sums, "fsdp", (2, 2))
    norm = run_kernel(
        lambda *refs: norm_kernel(total_channels, shards, rows, *refs),
        scalars,
        [(a, NEAR) for a in (cotangent, response, taps, gain, query_feature, gated, sums)],
        ((whole, bf16, NEAR),) * 2 + (((rows, width), bf16, FAR),) * shards,
        ((whole, bf16), ((blocks + 1,) + extended_shape, f32)),
        0.2,
        "norm",
        sems=shards,
    )
    norm = list(norm)
    first_piece = norm[4]
    norm, gated_far, near_piece = lax.optimization_barrier((norm, gated_far, gated_pieces[1]))
    norm[4] = first_piece
    d_query, d_response = norm[:2]
    gated_back = to_tokens([gated_pieces[0], near_piece], [0, 1]) + gated_far
    query_back = to_tokens(norm[2:3] + norm[4:], [slot for slot in every_slot if slot != 1])
    back = run_kernel(
        lambda *refs: mix_back_kernel(shards, rows, *refs),
        scalars,
        [
            (a, NEAR)
            for a in (
                taps, analysis, synthesis_back, features, filter_spectrum, d_response
            )
        ]
        + [(norm[3], FAR)],
        (((KM, width), f32, NEAR), ((2,) + whole, bf16, NEAR))
        + tuple(((3 if slot == 1 else 2, rows, width), bf16, FAR) for slot in every_slot),
        (
            ((2,) + whole, bf16), ((2, blocks + 1) + extended_shape, f32), spectra,
            ((2 * KM, width), f32),
        ),
        7,
        "mix_back",
        sems=shards + 1,
    )
    mixer_grad, d_others, *back_pieces = back
    gated_back[1], back_pieces[1] = lax.optimization_barrier((gated_back[1], back_pieces[1]))
    others_back = to_tokens(back_pieces, every_slot)
    taps_grad, gain_grad = run_kernel(
        lambda *refs: tap_grad_kernel(total_channels, *refs),
        scalars,
        [
            (a, NEAR)
            for a in (staged_query, staged, d_query, d_others, gated, cotangent, sums)
        ],
        (((3 * KF, width), f32, NEAR), ((1, width), f32, NEAR)),
        (((3,) + extended_shape, f32), ((3, 8 * KF, width), f32), ((8, width), f32)),
        4,
        "tap_grad",
    )
    aligned = width == narrow
    (out,) = run_kernel(
        lambda *refs: scale_out_kernel(total_channels, shards, rows, *refs),
        (layout, position_word),
        [(sums, NEAR)] + [(a, NEAR) for a in gated_back],
        (((rows, channels) if aligned else (shards, rows, narrow), bf16, FAR),),
        (((shards, rows, narrow), bf16),),
        2,
        "scale_out",
        sems=shards,
    )
    if aligned:
        (stream_grad,) = run_kernel(
            lambda *refs: assemble_grad_kernel(shards, width, *refs),
            (position_word,),
            [(a, NEAR) for a in query_back] + [(a, NEAR) for a in others_back],
            (((3, rows, channels), bf16, FAR),),
            (),
            1,
            "assemble_grad",
            sems=2 * shards,
        )
    else:
        def assemble(pieces):
            stacked = jnp.stack(pieces)
            in_place = jnp.take(stacked, position ^ jnp.arange(shards), axis=0)
            return jnp.moveaxis(in_place, 0, -2).reshape(pieces[0].shape[:-1] + (channels,))

        out = out.transpose(1, 0, 2).reshape(rows, channels)
        queries = query_back[:1] + [others_back[1][0]] + query_back[1:]
        others_back[1] = others_back[1][1:]
        stream_grad = jnp.concatenate([assemble(queries)[None], assemble(others_back)])
    feat_grad = taps_grad[:, :narrow].reshape(KF, 3, narrow)
    return (out, stream_grad, mixer_grad[:, :narrow], feat_grad, gain_grad[0, :narrow])


def solution(mesh):
    placed = (
        P(None, "seq", "fsdp"),
        P(),
        P(),
        P(),
        P(None, ("fsdp", "seq")),
        P(None, None, ("fsdp", "seq")),
        P(("fsdp", "seq")),
        P("seq", "fsdp"),
    )
    return jax.shard_map(
        body,
        mesh=mesh,
        in_specs=placed,
        out_specs=(
            P("seq", "fsdp"),
            P(None, "seq", "fsdp"),
            P(None, ("fsdp", "seq")),
            P(None, None, ("fsdp", "seq")),
            P(("fsdp", "seq")),
        ),
        check_vma=False,
    )
```
